32 devices in a mesh: dp: 16 (over z, y, x), tensor: 2 (over core).
Axes of the slice: x: 2, y: 2, z: 4, core: 2. Of those that a mesh axis runs over, the one named last changes fastest.
Arguments:
- hidden_in: bfloat16 [8192, 2560], P('dp'), may hold values from -6 to 6
- adapter_ids: int32 [16, 3], P('dp'), may hold values from 0 to 7, all different within a row
- attn_gain: bfloat16 [2560], replicated, may hold values from 0.5 to 1.5
- mlp_gain: bfloat16 [2560], replicated, may hold values from 0.5 to 1.5
- w_query: bfloat16 [2560, 2560], P('dp', 'tensor'), may hold values from -0.125 to 0.125
- w_key: bfloat16 [2560, 640], P('dp', 'tensor'), may hold values from -0.125 to 0.125
- w_value: bfloat16 [2560, 640], P('dp', 'tensor'), may hold values from -0.125 to 0.125
- w_output: bfloat16 [2560, 2560], P('tensor', 'dp'), may hold values from -0.5 to 0.5
- w_gate: bfloat16 [2560, 7168], P('dp', 'tensor'), may hold values from -0.125 to 0.125
- w_up: bfloat16 [2560, 7168], P('dp', 'tensor'), may hold values from -0.125 to 0.125
- w_down: bfloat16 [7168, 2560], P('tensor', 'dp'), may hold values from -0.125 to 0.125
- in_query: bfloat16 [2560, 128], replicated, may hold values from -0.125 to 0.125
- second_query: bfloat16 [128, 2560], P(None, 'tensor'), may hold values from -0.25 to 0.25
- in_key: bfloat16 [2560, 128], replicated, may hold values from -0.125 to 0.125
- second_key: bfloat16 [128, 640], P(None, 'tensor'), may hold values from -0.25 to 0.25
- in_value: bfloat16 [2560, 128], replicated, may hold values from -0.125 to 0.125
- second_value: bfloat16 [128, 640], P(None, 'tensor'), may hold values from -0.25 to 0.25
- in_output: bfloat16 [2560, 128], P('tensor'), may hold values from -0.5 to 0.5
- second_output: bfloat16 [128, 2560], replicated, may hold values from -0.25 to 0.25
- in_gate: bfloat16 [2560, 128], replicated, may hold values from -0.125 to 0.125
- second_gate: bfloat16 [128, 7168], P(None, 'tensor'), may hold values from -0.25 to 0.25
- in_up: bfloat16 [2560, 128], replicated, may hold values from -0.125 to 0.125
- second_up: bfloat16 [128, 7168], P(None, 'tensor'), may hold values from -0.25 to 0.25
- in_down: bfloat16 [7168, 128], P('tensor'), may hold values from -0.125 to 0.125
- second_down: bfloat16 [128, 2560], replicated, may hold values from -0.25 to 0.25
- cotangent: bfloat16 [8192, 2560], P('dp'), may hold values from -6 to 6
Outputs:
- layer_output: bfloat16 [8192, 2560], P('dp')
- grad_in: bfloat16 [8192, 2560], P('dp')
- delta_in_query: float32 [2560, 128], replicated
- gradient_second_query: float32 [128, 2560], replicated
- delta_in_key: float32 [2560, 128], replicated
- gradient_second_key: float32 [128, 640], replicated
- delta_in_value: float32 [2560, 128], replicated
- gradient_second_value: float32 [128, 640], replicated
- delta_in_output: float32 [2560, 128], replicated
- gradient_second_output: float32 [128, 2560], replicated
- delta_in_gate: float32 [2560, 128], replicated
- gradient_second_gate: float32 [128, 7168], replicated
- delta_in_up: float32 [2560, 128], replicated
- gradient_second_up: float32 [128, 7168], replicated
- delta_in_down: float32 [7168, 128], replicated
- gradient_second_down: float32 [128, 2560], replicated
The draws below stay inside these ranges and needn't reach their ends.
Inputs may be any that keep to these rules, and one draw needn't show every extreme that they name: `adapter_ids`: the 3 sequences of a group use different adapters, and every adapter is used by some sequence.
All inputs are finite; a program needn't handle non-finite values.
Results may differ from the reference program's by a relative error of at most 0.018.
Values may be sent and summed in bfloat16 or wider, within the bound.
No kernel may reach another device: no remote copies, remote signals or barrier semaphores. Data moves between devices by JAX's collectives and lax.ppermute only.
A program may use at most 256 MiB of HBM per device.

```python
import math
import jax
import jax.numpy as jnp
from jax import lax

D = 2560
HEADS = 32
KV_HEADS = 8
HEAD_DIM = 80
FF = 7168
RANK = 16
ADAPTERS = 8
PROMPT = 256
CONT_LEN = 128
SEQS = 3
ROWS = 512
GROUPS = 16
TOKENS = 8192


def shard_levels(key, shape, shards, smallest, largest):
    def one(axis_at, shards_of):
        draws = jax.random.uniform(jax.random.fold_in(jax.random.fold_in(key, 6), axis_at), (shards_of,), jnp.float32, smallest / len(shards), largest / len(shards))
        return jnp.repeat(jnp.exp(draws), shape[axis_at] // shards_of).reshape((-1,) + (1,) * (len(shape) - axis_at - 1))

    loudness = one(*shards[0])
    for cut in shards[1:]:
        loudness = loudness * one(*cut)
    return loudness


def different_ones(own_key, rows, amount, top, lift):
    order = jax.random.permutation(jax.random.fold_in(own_key, 1), amount)
    boost = order
    for power in range(3):
        boost = boost * boost // amount
    boost = boost * lift // amount
    tickets = jax.random.randint(jax.random.fold_in(own_key, 2), (rows, amount), 0, 4096) + boost
    sure = jax.random.permutation(jax.random.fold_in(own_key, 3), rows)[jnp.arange(amount) % rows]
    tickets = jnp.where(jnp.arange(rows)[:, None] == sure[None, :], 1 << 14, tickets)
    score = tickets * amount + jnp.arange(amount)
    return lax.top_k(score.astype(jnp.int32), top)[1].astype(jnp.int32)


def noise(key, extent, width, limit, cuts=(), held_as=jnp.bfloat16):
    gain = shard_levels(key, extent, cuts, -0.22, 0.18) if cuts else 1.0
    entries = jax.random.normal(key, extent, jnp.float32) * width * gain
    return jnp.minimum(jnp.maximum(entries, -limit), limit).astype(held_as)


def setup_inputs(seed: int = 0) -> dict:
    keys = jax.random.split(jax.random.key(seed), 27)
    return {
        "hidden_in": noise(keys[0], (TOKENS, D), 1.0, 6.0, ((0, 16),)),
        "adapter_ids": different_ones(keys[1], GROUPS, ADAPTERS, SEQS, 3072),
        "attn_gain": jnp.clip(1.0 + 0.1 * jax.random.normal(keys[2], (D,), jnp.float32), 0.5, 1.5).astype(jnp.bfloat16),
        "mlp_gain": jnp.clip(1.0 + 0.1 * jax.random.normal(keys[3], (D,), jnp.float32), 0.5, 1.5).astype(jnp.bfloat16),
        "w_query": noise(keys[4], (D, HEADS * HEAD_DIM), D ** -0.5, 0.125, ((0, 16), (1, 2))),
        "w_key": noise(keys[5], (D, KV_HEADS * HEAD_DIM), D ** -0.5, 0.125, ((0, 16), (1, 2))),
        "w_value": noise(keys[6], (D, KV_HEADS * HEAD_DIM), D ** -0.5, 0.125, ((0, 16), (1, 2))),
        "w_output": noise(keys[7], (HEADS * HEAD_DIM, D), (HEADS * HEAD_DIM // 16) ** -0.5, 0.5, ((0, 2), (1, 16))),
        "w_gate": noise(keys[8], (D, FF), D ** -0.5, 0.125, ((0, 16), (1, 2))),
        "w_up": noise(keys[9], (D, FF), D ** -0.5, 0.125, ((0, 16), (1, 2))),
        "w_down": noise(keys[10], (FF, D), (FF // 4) ** -0.5, 0.125, ((0, 2), (1, 16))),
        "in_query": noise(keys[11], (D, ADAPTERS * RANK), D ** -0.5, 0.125),
        "second_query": noise(keys[12], (ADAPTERS * RANK, HEADS * HEAD_DIM), 0.04, 0.25, ((1, 2),)),
        "in_key": noise(keys[13], (D, ADAPTERS * RANK), D ** -0.5, 0.125),
        "second_key": noise(keys[14], (ADAPTERS * RANK, KV_HEADS * HEAD_DIM), 0.04, 0.25, ((1, 2),)),
        "in_value": noise(keys[15], (D, ADAPTERS * RANK), D ** -0.5, 0.125),
        "second_value": noise(keys[16], (ADAPTERS * RANK, KV_HEADS * HEAD_DIM), 0.04, 0.25, ((1, 2),)),
        "in_output": noise(keys[17], (HEADS * HEAD_DIM, ADAPTERS * RANK), (HEADS * HEAD_DIM // 16) ** -0.5, 0.5, ((0, 2),)),
        "second_output": noise(keys[18], (ADAPTERS * RANK, D), 0.04, 0.25),
        "in_gate": noise(keys[19], (D, ADAPTERS * RANK), D ** -0.5, 0.125),
        "second_gate": noise(keys[20], (ADAPTERS * RANK, FF), 0.04, 0.25, ((1, 2),)),
        "in_up": noise(keys[21], (D, ADAPTERS * RANK), D ** -0.5, 0.125),
        "second_up": noise(keys[22], (ADAPTERS * RANK, FF), 0.04, 0.25, ((1, 2),)),
        "in_down": noise(keys[23], (FF, ADAPTERS * RANK), (FF // 4) ** -0.5, 0.125, ((0, 2),)),
        "second_down": noise(keys[24], (ADAPTERS * RANK, D), 0.04, 0.25),
        "cotangent": noise(keys[25], (TOKENS, D), 1.0, 6.0, ((0, 16),)),
    }


adapter_scale = 2.0
norm_eps = 1e-05
rope_base = 1000000.0
highest = lax.Precision.HIGHEST

@jax.custom_vjp
def reduced_projection(v):
    return lax.optimization_barrier(v.astype(jnp.bfloat16)).astype(jnp.float32)

@jax.custom_vjp
def reduced_backward(v):
    return v

def low_keep(v):
    return (reduced_projection(v), None)

def low_pass(kept, grad):
    return (grad,)

def back_keep(v):
    return (v, None)

def back_low(kept, grad):
    return (reduced_projection(grad),)
reduced_projection.defvjp(low_keep, low_pass)
reduced_backward.defvjp(back_keep, back_low)

def rms_norm(values, gain_vec):
    return values * lax.rsqrt(lax.optimization_barrier(jnp.mean(values * values, axis=-1, keepdims=True)) + norm_eps) * gain_vec

def rotate(values, cos_table, sin_table):
    half_dim = values.shape[-1] // 2
    first_half = values[..., :half_dim]
    second_half = values[..., half_dim:]
    return jnp.concatenate([first_half * cos_table - second_half * sin_table, second_half * cos_table + first_half * sin_table], axis=-1)

def matrix_product(left, right):
    return jnp.dot(left, right, precision=highest)

def add_up(first, second):
    return first + second

def reference(hidden_in, adapter_ids, attn_gain, mlp_gain, w_query, w_key, w_value, w_output, w_gate, w_up, w_down, in_query, second_query, in_key, second_key, in_value, second_value, in_output, second_output, in_gate, second_gate, in_up, second_up, in_down, second_down, cotangent):
    gain_attn = attn_gain.astype(jnp.float32)
    gain_mlp = mlp_gain.astype(jnp.float32)
    frozen_query = w_query.astype(jnp.float32)
    frozen_key = w_key.astype(jnp.float32)
    frozen_value = w_value.astype(jnp.float32)
    frozen_output = w_output.astype(jnp.float32)
    frozen_gate = w_gate.astype(jnp.float32)
    frozen_up = w_up.astype(jnp.float32)
    frozen_down = w_down.astype(jnp.float32)
    adapters = (in_query.astype(jnp.float32), second_query.astype(jnp.float32), in_key.astype(jnp.float32), second_key.astype(jnp.float32), in_value.astype(jnp.float32), second_value.astype(jnp.float32), in_output.astype(jnp.float32), second_output.astype(jnp.float32), in_gate.astype(jnp.float32), second_gate.astype(jnp.float32), in_up.astype(jnp.float32), second_up.astype(jnp.float32), in_down.astype(jnp.float32), second_down.astype(jnp.float32))
    row_index = jnp.arange(ROWS, dtype=jnp.int32)
    is_later = row_index >= PROMPT
    seq_of = jnp.where(is_later, 1 + (row_index - PROMPT) // CONT_LEN, 0).astype(jnp.int32)
    position = jnp.where(is_later, PROMPT + (row_index - PROMPT) % CONT_LEN, row_index)
    visible = (row_index[None, :] <= row_index[:, None]) & ((row_index[None, :] < PROMPT) | (seq_of[None, :] == seq_of[:, None]))
    inv_freq = rope_base ** (-2.0 * jnp.arange(HEAD_DIM // 2, dtype=jnp.float32) / HEAD_DIM)
    angles = position.astype(jnp.float32)[:, None] * inv_freq[None, :]
    cos_table = jnp.cos(angles)[:, None, :]
    sin_table = jnp.sin(angles)[:, None, :]
    col_adapter = jnp.arange(ADAPTERS * RANK, dtype=jnp.int32) // RANK
    inv_sqrt = 1.0 / math.sqrt(HEAD_DIM)
    group_size = HEADS // KV_HEADS

    def one_group(totals, pieces):
        hidden_g, ids_g, cot_g = pieces
        row_adapter = ids_g[seq_of]
        select_adapter = (col_adapter[None, :] == row_adapter[:, None]).astype(jnp.float32)

        def forward(hidden_state, adapter_apply):
            normalized_attention_input = reduced_projection(rms_norm(hidden_state, gain_attn))
            reduced_query = reduced_projection(reduced_backward(matrix_product(normalized_attention_input, adapter_apply[0]) * select_adapter))
            reduced_key = reduced_projection(reduced_backward(matrix_product(normalized_attention_input, adapter_apply[2]) * select_adapter))
            reduced_value = reduced_projection(reduced_backward(matrix_product(normalized_attention_input, adapter_apply[4]) * select_adapter))
            query_rows = reduced_backward(matrix_product(normalized_attention_input, frozen_query) + adapter_scale * matrix_product(reduced_query, adapter_apply[1]))
            key_unrotated = reduced_backward(matrix_product(normalized_attention_input, frozen_key) + adapter_scale * matrix_product(reduced_key, adapter_apply[3]))
            value_reduced_rows = reduced_projection(reduced_backward(matrix_product(normalized_attention_input, frozen_value) + adapter_scale * matrix_product(reduced_value, adapter_apply[5])))
            query_rot = reduced_projection(rotate(query_rows.reshape(ROWS, HEADS, HEAD_DIM), cos_table, sin_table)).reshape(ROWS, KV_HEADS, group_size, HEAD_DIM)
            key_rot = reduced_projection(rotate(key_unrotated.reshape(ROWS, KV_HEADS, HEAD_DIM), cos_table, sin_table))
            scores = reduced_backward(jnp.einsum('rkgd,skd->kgrs', query_rot, key_rot, precision=highest) * inv_sqrt)
            scores = jnp.where(visible, scores, -1e+30)
            top_score = lax.optimization_barrier(jnp.max(scores, axis=-1, keepdims=True))
            expo_vals = jnp.exp(scores - top_score)
            attn_prob = reduced_projection(expo_vals / lax.optimization_barrier(jnp.sum(expo_vals, axis=-1, keepdims=True)))
            mixed = jnp.einsum('kgrs,skd->rkgd', attn_prob, value_reduced_rows.reshape(ROWS, KV_HEADS, HEAD_DIM), precision=highest)
            attended_values = reduced_projection(reduced_backward(mixed.reshape(ROWS, HEADS * HEAD_DIM)))
            reduced_output = reduced_projection(reduced_backward(matrix_product(attended_values, adapter_apply[6]) * select_adapter))
            middle_activation = hidden_state + reduced_backward(matrix_product(attended_values, frozen_output) + adapter_scale * matrix_product(reduced_output, adapter_apply[7]))
            normalized_feedforward_input = reduced_projection(rms_norm(middle_activation, gain_mlp))
            reduced_gate = reduced_projection(reduced_backward(matrix_product(normalized_feedforward_input, adapter_apply[8]) * select_adapter))
            reduced_up = reduced_projection(reduced_backward(matrix_product(normalized_feedforward_input, adapter_apply[10]) * select_adapter))
            gate_activation = reduced_backward(matrix_product(normalized_feedforward_input, frozen_gate) + adapter_scale * matrix_product(reduced_gate, adapter_apply[9]))
            up_projected = reduced_backward(matrix_product(normalized_feedforward_input, frozen_up) + adapter_scale * matrix_product(reduced_up, adapter_apply[11]))
            active_rows = reduced_projection(jax.nn.silu(gate_activation) * up_projected)
            reduced_down = reduced_projection(reduced_backward(matrix_product(active_rows, adapter_apply[12]) * select_adapter))
            return middle_activation + reduced_backward(matrix_product(active_rows, frozen_down) + adapter_scale * matrix_product(reduced_down, adapter_apply[13]))
        layer_value, pullback = jax.vjp(forward, hidden_g.astype(jnp.float32), adapters)
        grad_hidden, grad_adapt = pullback(cot_g.astype(jnp.float32))
        totals = jax.tree.map(add_up, totals, grad_adapt)
        return (totals, (layer_value.astype(jnp.bfloat16), grad_hidden.astype(jnp.bfloat16)))
    initial = tuple((jnp.zeros_like(adapter) for adapter in adapters))
    totals, (outs_all, grads_all) = lax.scan(one_group, initial, (hidden_in.reshape(GROUPS, ROWS, D), adapter_ids, cotangent.reshape(GROUPS, ROWS, D)))
    return (outs_all.reshape(TOKENS, D), grads_all.reshape(TOKENS, D), totals[0], totals[1], totals[2], totals[3], totals[4], totals[5], totals[6], totals[7], totals[8], totals[9], totals[10], totals[11], totals[12], totals[13])
```

```python
import math

import jax
import jax.numpy as jnp
from jax import lax
from jax.experimental import pallas as pl
from jax.experimental.pallas import tpu as pltpu
from jax.sharding import PartitionSpec as P

HEAD_DIM = 80
RANK = 16
PROMPT = 256
CONT_LEN = 128
WIDTH = 256

adapter_scale = 2.0
norm_eps = 1e-05
rope_base = 1000000.0

BF = jnp.bfloat16
F32 = jnp.float32

LAG = 2
STEP_FLOPS = 20_000_000_000
NORMED_AFTER = 4
EXCHANGES = ((0, 1), (2, 3), (4, 5, 6))
EXCHANGE_PRIORITY = (-40, -39, 8)
ATTN_PRIORITY = (-20, -10)
YZ_CHUNKS = ()
LAST_WIDE = 30


def matrix_product(left, right):
    return jnp.dot(left, right, preferred_element_type=F32)


def product_with_transpose(left, right):
    return lax.dot_general(left, right, (((1,), (1,)), ((), ())), preferred_element_type=F32)


def transpose_then_product(left, right):
    return lax.dot_general(left, right, (((0,), (0,)), ((), ())), preferred_element_type=F32)


def rms_norm(values, gain_vec):
    return (
        values * lax.rsqrt(jnp.mean(values * values, axis=-1, keepdims=True) + norm_eps) * gain_vec
    )


def rms_back(values, gain_vec, grad):
    scale = lax.rsqrt(jnp.mean(values * values, axis=-1, keepdims=True) + norm_eps)
    e = gain_vec * grad
    return scale * e - values * (scale * scale * scale) * jnp.mean(values * e, axis=-1, keepdims=True)


def ring_and_swaps(n):
    perms = {
        "y": [(i, i ^ 2) for i in range(n)],
        "x": [(i, i ^ 1) for i in range(n)],
        "xy": [(i, i ^ 3) for i in range(n)],
    }
    for r in range(1, n // 4):
        perms[f"z{r}"] = [(i, (i + 4 * r) % n) for i in range(n)]
    perms["z"] = perms["z1"]
    return perms


def plan_transfers(ring_size, chunks):
    plan = {}
    first, second = ATTN_PRIORITY
    plan["A0.y"] = ("y", "A0.o", first, 1)
    for r in range(ring_size):
        if r:
            plan[f"A0.b{r}"] = ("z", f"A0.b{r - 1}", first + 0.01 * r, 2)
            plan[f"A1.p{r}"] = ("z", f"A1.p{r - 1}", second + 0.01 * r, 1)
        plan[f"A1.q{r}"] = ("y", f"A1.p{r}", second + 0.01 * r, 1)
        plan[f"A0.x{r}"] = ("x", f"A0.b{r}", first + 0.01 * r, 2)
        plan[f"A1.x{r}"] = ("x", f"A1.b{r}", second + 0.01 * r, 2)
    for i, group in enumerate(exchanges_of(chunks)):
        plan[f"E{i}.e"] = ("x", f"E{i}.o", EXCHANGE_PRIORITY[min(i, 2)], (len(group) + 1) // 2)
    for j in range(chunks):
        tag = f"M{j}"
        for r in range(ring_size):
            source = (f"{tag}.p{r}" if r else tag)
            if r:
                before = f"{tag}.p{r - 1}" if r > 1 else tag
                plan[f"{tag}.p{r}"] = ("z", before, j + 0.01 * r, 1)
            plan[f"{tag}.q{r}"] = ("y", source, j + 0.01 * r, 1)
    plan["C.x"] = ("x", "C.o", LAST_WIDE, 3)
    plan["N.x"] = ("x", "N.o", -50, 3)
    return plan


def exchanges_of(chunks):
    return EXCHANGES[:2] + (tuple(range(4, chunks)),)


def schedule(plan, chunks):
    makes = {"A0.y": ["A0.b0"]}
    for i, group in enumerate(exchanges_of(chunks)):
        makes[f"E{i}.e"] = [f"M{j}" for j in group]
    ready, busy, arrivals = {}, {}, {}
    for _, source, _, _ in plan.values():
        if source.endswith(".o") and source != "N.o":
            ready[source] = 0
    ready["A1.p0"] = 0
    steps, waiting, now = [], dict(plan), 0
    while waiting:
        step = []
        if "N.o" not in ready and not any(name.startswith("A1") for name in waiting):
            ready["N.o"] = max(s for s, names in arrivals.items() if "A1.x" in str(names))
            ready["N.o"] += NORMED_AFTER
        for link in "xyz":
            able = [
                (entry[2], name)
                for name, entry in waiting.items()
                if entry[0] == link
                and busy.get(link, 0) <= now
                and ready.get(entry[1], 1 << 30) <= now
            ]
            if able:
                name = min(able)[1]
                length = waiting.pop(name)[3]
                step.append(name)
                busy[link] = now + length
                ready[name] = now + (LAG if length == 1 else length)
                arrivals.setdefault(ready[name], []).append(name)
                for made in makes.get(name, []):
                    ready[made] = ready[name]
                if name.startswith("A1") and name[3] in "pq":
                    pair = (f"A1.p{name[4:]}", f"A1.q{name[4:]}")
                    if pair[0] in ready and pair[1] in ready:
                        ready[f"A1.b{name[4:]}"] = max(ready[p] for p in pair)
        steps.append(step)
        now += 1
    return steps, arrivals


def tie(values, others, flops=STEP_FLOPS):
    def kernel(*refs):
        pass

    spec = pl.BlockSpec(memory_space=pltpu.HBM)
    n = len(values)
    return pl.pallas_call(
        kernel,
        out_shape=[jax.ShapeDtypeStruct(v.shape, v.dtype) for v in values],
        in_specs=[spec] * (n + len(others)),
        out_specs=[spec] * n,
        input_output_aliases={i: i for i in range(n)},
        cost_estimate=pl.CostEstimate(flops=flops, transcendentals=0, bytes_accessed=0),
    )(*values, *others)


def bring(blocks, place_ref, target, sems):
    total = sum(block.shape[0] for block in blocks)
    rows = total // place_ref.shape[0]
    copies = []
    for block in blocks:
        for start in range(0, block.shape[0], rows):
            i = len(copies)
            to = pl.multiple_of(place_ref[i] * rows, math.gcd(rows, 16))
            copies.append(
                pltpu.make_async_copy(
                    block.at[pl.ds(start, rows)], target.at[pl.ds(to, rows)], sems.at[i]
                )
            )
    return copies


HBM = pl.BlockSpec(memory_space=pl.ANY)
VMEM = pl.BlockSpec(memory_space=pltpu.VMEM)
SMEM = pl.BlockSpec(memory_space=pltpu.SMEM)


def nt(left, right):
    return lax.dot_general(left, right, (((1,), (1,)), ((), ())), preferred_element_type=F32)


def turn(upright, cos_ref, sin_ref, sign, row):
    half = HEAD_DIM // 2
    first, second = upright[row : row + half], upright[row + half : row + 2 * half]
    cos, sin = cos_ref[...], sin_ref[...] * sign
    return jnp.concatenate([first * cos - second * sin, second * cos + first * sin], axis=0)


def queries_and_keys(places, blocks, normed, low_query, low_key, second_query, second_key, cos, sin):
    count = len(blocks)
    tokens, width = normed.shape
    cols = blocks[0].shape[1]
    q_cols, k_cols = second_query.shape[1], second_key.shape[1]

    def kernel(place_ref, x_ref, lq_ref, lk_ref, sq_ref, sk_ref, cos_ref, sin_ref, *refs):
        parts, (q_out, k_out, w_out, w_s, sems, sem_out) = refs[:count], refs[count:]
        copies = bring(parts, place_ref, w_s, sems)
        for copy in copies:
            copy.start()
        for copy in copies:
            copy.wait()
        keep = pltpu.make_async_copy(w_s, w_out, sem_out)
        keep.start()
        x = x_ref[...]
        step = 4 * HEAD_DIM
        for start, low, second, out, shift in [
            (at, lq_ref, sq_ref, q_out, 0) for at in range(0, q_cols, step)
        ] + [(q_cols + at, lk_ref, sk_ref, k_out, q_cols) for at in range(0, k_cols, step)]:
            own = start - shift
            part = jnp.dot(x, w_s[:, start : start + step], preferred_element_type=F32)
            part += jnp.dot(low[...], second[:, own : own + step], preferred_element_type=F32)
            upright = part.T
            for row in range(0, step, HEAD_DIM):
                out[own + row : own + row + HEAD_DIM, :] = turn(
                    upright, cos_ref, sin_ref, 1.0, row
                ).astype(BF)
        keep.wait()

    return pl.pallas_call(
        kernel,
        out_shape=[
            jax.ShapeDtypeStruct((q_cols, tokens), BF),
            jax.ShapeDtypeStruct((k_cols, tokens), BF),
            jax.ShapeDtypeStruct((width, cols), BF),
        ],
        in_specs=[SMEM] + [VMEM] * 7 + [HBM] * count,
        out_specs=[VMEM, VMEM, HBM],
        scratch_shapes=[
            pltpu.VMEM((width, cols), BF),
            pltpu.SemaphoreType.DMA((places.shape[0],)),
            pltpu.SemaphoreType.DMA,
        ],
        compiler_params=pltpu.CompilerParams(vmem_limit_bytes=48 * 2**20),
        cost_estimate=pl.CostEstimate(
            flops=2 * tokens * width * cols, transcendentals=0, bytes_accessed=4 * width * cols
        ),
    )(places, normed, low_query, low_key, second_query, second_key, cos, sin, *blocks)


def seen(rows, columns, row_start, column_start):
    key = lax.broadcasted_iota(jnp.int32, (rows, columns), 0)
    query = lax.broadcasted_iota(jnp.int32, (rows, columns), 1)
    causal = key <= query
    if row_start >= PROMPT:
        causal = causal & (key // CONT_LEN == query // CONT_LEN)
    return causal


def attention(places, blocks, normed, low_value, second_value, query, key, in_output):
    count = len(blocks)
    tokens, width = normed.shape
    cols = blocks[0].shape[1]
    q_cols, k_cols = query.shape[0], key.shape[0]
    kv_heads = k_cols // HEAD_DIM
    group = q_cols // k_cols
    scale = 1.0 / math.sqrt(HEAD_DIM)

    def kernel(place_ref, x_ref, lv_ref, sv_ref, q_ref, k_ref, io_ref, *refs):
        parts = refs[:count]
        v_out, att_out, lse_out, branch_out, low_out, w_out, w_s, att_s, sems, sem_out = refs[count:]
        copies = bring(parts, place_ref, w_s, sems)
        for copy in copies:
            copy.start()
        for copy in copies:
            copy.wait()
        keep = pltpu.make_async_copy(w_s, w_out, sem_out)
        keep.start()
        value = jnp.dot(x_ref[...], w_s[:, q_cols:cols], preferred_element_type=F32)
        value += jnp.dot(lv_ref[...], sv_ref[...], preferred_element_type=F32)
        v_out[...] = value.T.astype(BF)
        seen_first = seen(PROMPT, PROMPT, 0, 0)
        seen_second = seen(tokens - PROMPT, tokens - PROMPT, PROMPT, PROMPT)

        def one_head(g, _):
            k_rows = pl.ds(pl.multiple_of(g * HEAD_DIM, 16), HEAD_DIM)
            keys = k_ref[k_rows, :].T
            values = v_out[k_rows, :]
            for h in range(group):
                rows = pl.ds(pl.multiple_of((g * group + h) * HEAD_DIM, 16), HEAD_DIM)
                head = q_ref[rows, :]
                early = jnp.dot(keys[:PROMPT], head[:, :PROMPT], preferred_element_type=F32)
                late = jnp.dot(keys, head[:, PROMPT:], preferred_element_type=F32)
                early = jnp.where(seen_first, early * scale, -1e30)
                late_prompt = late[:PROMPT] * scale
                late_own = jnp.where(seen_second, late[PROMPT:] * scale, -1e30)
                top = jnp.max(early, axis=0, keepdims=True)
                expo = jnp.exp(early - top)
                total = jnp.sum(expo, axis=0, keepdims=True)
                prob = (expo * (1.0 / total)).astype(BF)
                lse_out[g, h : h + 1, :PROMPT] = top + jnp.log(total)
                att_s[rows, :PROMPT] = jnp.dot(
                    values[:, :PROMPT], prob, preferred_element_type=F32
                ).astype(BF)
                top = jnp.maximum(
                    jnp.max(late_prompt, axis=0, keepdims=True),
                    jnp.max(late_own, axis=0, keepdims=True),
                )
                expo_p, expo_o = jnp.exp(late_prompt - top), jnp.exp(late_own - top)
                total = jnp.sum(expo_p, axis=0, keepdims=True) + jnp.sum(
                    expo_o, axis=0, keepdims=True
                )
                inverse = 1.0 / total
                prob = jnp.concatenate(
                    [(expo_p * inverse).astype(BF), (expo_o * inverse).astype(BF)], axis=0
                )
                lse_out[g, h : h + 1, PROMPT:] = top + jnp.log(total)
                att_s[rows, PROMPT:] = jnp.dot(
                    values, prob, preferred_element_type=F32
                ).astype(BF)
            return 0

        lax.fori_loop(0, kv_heads, one_head, 0)
        att_out[...] = att_s[...].T
        attended = att_out[...]
        low_out[...] = jnp.dot(attended, io_ref[...], preferred_element_type=F32)
        for at in range(0, width, 512):
            branch_out[:, at : at + 512] = nt(attended, w_s[at : at + 512, :q_cols]).astype(BF)
        keep.wait()

    return pl.pallas_call(
        kernel,
        out_shape=[
            jax.ShapeDtypeStruct((k_cols, tokens), BF),
            jax.ShapeDtypeStruct((tokens, q_cols), BF),
            jax.ShapeDtypeStruct((kv_heads, group, tokens), F32),
            jax.ShapeDtypeStruct((tokens, width), BF),
            jax.ShapeDtypeStruct((tokens, in_output.shape[1]), F32),
            jax.ShapeDtypeStruct((width, cols), BF),
        ],
        in_specs=[SMEM] + [VMEM] * 6 + [HBM] * count,
        out_specs=[VMEM] * 5 + [HBM],
        scratch_shapes=[
            pltpu.VMEM((width, cols), BF),
            pltpu.VMEM((q_cols, tokens), BF),
            pltpu.SemaphoreType.DMA((places.shape[0],)),
            pltpu.SemaphoreType.DMA,
        ],
        compiler_params=pltpu.CompilerParams(vmem_limit_bytes=48 * 2**20),
        cost_estimate=pl.CostEstimate(
            flops=4 * tokens * width * cols, transcendentals=0, bytes_accessed=4 * width * cols
        ),
    )(places, normed, low_value, second_value, query, key, in_output, *blocks)


def attention_back(
    core, halves, select, second_output, low_output, attended, in_output, full_a0, full_a1, query,
    key, value, lse, cos, sin, second_query, second_key, second_value, low_query, low_key, low_value,
):
    half_tokens, width = halves[0].shape
    tokens = 2 * half_tokens
    cols = full_a0.shape[1]
    q_cols, k_cols = query.shape[0], key.shape[0]
    rank = second_query.shape[0]
    kv_heads = k_cols // HEAD_DIM
    group = q_cols // k_cols
    scale = 1.0 / math.sqrt(HEAD_DIM)

    def kernel(
        core_ref, mine_hbm, other_hbm, sel_ref, so_ref, lo_ref, att_ref, io_ref, a0_hbm, a1_hbm, q_ref, k_ref, v_ref, lse_ref, cos_ref, sin_ref,
        sq_ref, sk_ref, sv_ref, lq_ref, lk_ref, lv_ref, back_out, low_out, second_out,
        first_out, second_o_out, a0, a1, gb_ref, glo_ref, ga_s, g_s, gw_s, sems,
    ):
        mine = core_ref[0]
        copies = [
            pltpu.make_async_copy(a1_hbm, a1, sems.at[0]),
            pltpu.make_async_copy(a0_hbm, a0, sems.at[1]),
            pltpu.make_async_copy(
                mine_hbm, gb_ref.at[pl.ds(pl.multiple_of(mine * half_tokens, 16), half_tokens)], sems.at[2]
            ),
            pltpu.make_async_copy(
                other_hbm,
                gb_ref.at[pl.ds(pl.multiple_of((1 - mine) * half_tokens, 16), half_tokens)],
                sems.at[3],
            ),
        ]
        for i in (2, 3, 0, 1):
            copies[i].start()
        for i in (2, 3):
            copies[i].wait()
        glo_ref[...] = (adapter_scale * nt(gb_ref[...], so_ref[...]) * sel_ref[...]).astype(BF)
        first_out[...] = jnp.dot(
            att_ref[...].T, glo_ref[...], preferred_element_type=F32
        ).astype(BF)
        part = jnp.dot(
            lo_ref[...].T,
            gb_ref[:, pl.ds(pl.multiple_of(mine * (width // 2), 128), width // 2)],
            preferred_element_type=F32,
        )
        for at in range(0, width // 2, rank):
            second_o_out[at : at + rank, :] = (adapter_scale * part[:, at : at + rank]).astype(BF)
        copies[0].wait()
        step = 4 * HEAD_DIM
        for at in range(0, q_cols, step):
            part = jnp.dot(gb_ref[...], a1[:, at : at + step], preferred_element_type=F32)
            part += nt(glo_ref[...], io_ref[at : at + step, :])
            ga_s[at : at + step, :] = part.astype(BF).T
        seen_first = seen(PROMPT, PROMPT, 0, 0)
        seen_second = seen(tokens - PROMPT, tokens - PROMPT, PROMPT, PROMPT)

        def one_head(g, _):
            k_rows = pl.ds(pl.multiple_of(g * HEAD_DIM, 16), HEAD_DIM)
            keys_up = k_ref[k_rows, :]
            keys = keys_up.T
            values = v_ref[k_rows, :].T
            grad_k, grad_v = [0.0, 0.0], [0.0, 0.0]
            for h in range(group):
                rows = pl.ds(pl.multiple_of((g * group + h) * HEAD_DIM, 16), HEAD_DIM)
                head, grad = q_ref[rows, :], ga_s[rows, :]
                lse_h = lse_ref[g, h : h + 1, :]
                score = jnp.dot(keys[:PROMPT], head[:, :PROMPT], preferred_element_type=F32)
                prob = jnp.where(seen_first, jnp.exp(score * scale - lse_h[:, :PROMPT]), 0.0)
                grad_prob = jnp.dot(values[:PROMPT], grad[:, :PROMPT], preferred_element_type=F32)
                row_term = jnp.sum(prob * grad_prob, axis=0, keepdims=True)
                grad_score = (prob * (grad_prob - row_term)).astype(BF)
                prob = prob.astype(BF)
                grad_q_early = jnp.dot(
                    keys_up[:, :PROMPT], grad_score, preferred_element_type=F32
                )
                grad_v[0] += nt(grad[:, :PROMPT], prob)
                grad_k[0] += nt(head[:, :PROMPT], grad_score)
                score = jnp.dot(keys, head[:, PROMPT:], preferred_element_type=F32)
                expo = jnp.exp(score * scale - lse_h[:, PROMPT:])
                prob_p = expo[:PROMPT]
                prob_o = jnp.where(seen_second, expo[PROMPT:], 0.0)
                grad_prob = jnp.dot(values, grad[:, PROMPT:], preferred_element_type=F32)
                row_term = jnp.sum(prob_p * grad_prob[:PROMPT], axis=0, keepdims=True) + jnp.sum(
                    prob_o * grad_prob[PROMPT:], axis=0, keepdims=True
                )
                score_p = (prob_p * (grad_prob[:PROMPT] - row_term)).astype(BF)
                score_o = (prob_o * (grad_prob[PROMPT:] - row_term)).astype(BF)
                grad_q_late = jnp.dot(
                    keys_up, jnp.concatenate([score_p, score_o], axis=0), preferred_element_type=F32
                )
                grad_v[0] += nt(grad[:, PROMPT:], prob_p.astype(BF))
                grad_v[1] += nt(grad[:, PROMPT:], prob_o.astype(BF))
                grad_k[0] += nt(head[:, PROMPT:], score_p)
                grad_k[1] += nt(head[:, PROMPT:], score_o)
                grad_q = jnp.concatenate([grad_q_early, grad_q_late], axis=1) * scale
                g_s[rows, :] = turn(grad_q, cos_ref, sin_ref, -1.0, 0).astype(BF)
            grad_key = jnp.concatenate(grad_k, axis=1) * scale
            g_s[pl.ds(pl.multiple_of(q_cols + g * HEAD_DIM, 16), HEAD_DIM), :] = turn(
                grad_key, cos_ref, sin_ref, -1.0, 0
            ).astype(BF)
            g_s[pl.ds(pl.multiple_of(q_cols + k_cols + g * HEAD_DIM, 16), HEAD_DIM), :] = (
                jnp.concatenate(grad_v, axis=1).astype(BF)
            )
            return 0

        lax.fori_loop(0, kv_heads, one_head, 0)
        gw_s[...] = g_s[...].T
        part = [
            jnp.dot(low[...].T, gw_s[:, at : at + size], preferred_element_type=F32)
            for at, size, low in (
                (0, q_cols, lq_ref),
                (q_cols, k_cols, lk_ref),
                (q_cols + k_cols, k_cols, lv_ref),
            )
        ]
        part = jnp.concatenate(part, axis=1).astype(BF)
        for at in range(0, q_cols + 2 * k_cols, rank):
            second_out[at : at + rank, :] = part[:, at : at + rank]
        for i, (at, size, second) in enumerate(
            ((0, q_cols, sq_ref), (q_cols, k_cols, sk_ref), (q_cols + k_cols, k_cols, sv_ref))
        ):
            low_out[:, i * rank : (i + 1) * rank] = adapter_scale * nt(
                gw_s[:, at : at + size], second[...]
            )
        copies[1].wait()
        for at in range(0, width, 512):
            rows = slice(at, at + 512)
            part = nt(gw_s[:, :cols], a0[rows, :]) + nt(gw_s[:, cols:], a1[rows, q_cols:])
            back_out[:, rows] = part.astype(BF)

    return pl.pallas_call(
        kernel,
        out_shape=[
            jax.ShapeDtypeStruct((tokens, width), BF),
            jax.ShapeDtypeStruct((tokens, 3 * rank), F32),
            jax.ShapeDtypeStruct((q_cols + 2 * k_cols, rank), BF),
            jax.ShapeDtypeStruct((q_cols, rank), BF),
            jax.ShapeDtypeStruct((width // 2, rank), BF),
        ],
        in_specs=[SMEM, HBM, HBM] + [VMEM] * 5 + [HBM] * 2 + [VMEM] * 12,
        out_specs=[VMEM] * 5,
        scratch_shapes=[
            pltpu.VMEM((width, cols), BF),
            pltpu.VMEM((width, cols), BF),
            pltpu.VMEM((tokens, width), BF),
            pltpu.VMEM((tokens, rank), BF),
            pltpu.VMEM((q_cols, tokens), BF),
            pltpu.VMEM((q_cols + 2 * k_cols, tokens), BF),
            pltpu.VMEM((tokens, q_cols + 2 * k_cols), BF),
            pltpu.SemaphoreType.DMA((4,)),
        ],
        compiler_params=pltpu.CompilerParams(vmem_limit_bytes=56 * 2**20),
        cost_estimate=pl.CostEstimate(
            flops=20 * tokens * width * cols, transcendentals=0, bytes_accessed=4 * width * cols
        ),
    )(
        core, *halves, select, second_output, low_output, attended, in_output, full_a0, full_a1, query,
        key, value, lse, cos, sin, second_query, second_key, second_value, low_query, low_key, low_value,
    )


def after_attention(
    hidden, branches, branch_lows, select, second_output, gain, mlp_in
):
    tokens, width = hidden.shape
    rank = select.shape[1]
    tile = 128

    def kernel(h_ref, b0, b1, l0, l1, sel_ref, so_ref, gain_ref, in_ref, mid_out, ext_out, low_out):
        def one(t, _):
            r = pl.ds(pl.multiple_of(t * tile, tile), tile)
            sel = sel_ref[r, :]
            low = ((l0[r, :] + l1[r, :]) * sel).astype(BF)
            low_out[r, :] = low
            middle = h_ref[r, :].astype(F32) + (b0[r, :].astype(F32) + b1[r, :].astype(F32))
            middle += adapter_scale * jnp.dot(low, so_ref[...], preferred_element_type=F32)
            mid_out[r, :] = middle
            scale = lax.rsqrt(jnp.mean(middle * middle, axis=1, keepdims=True) + norm_eps)
            normed = (middle * scale * gain_ref[...]).astype(BF)
            ext_out[r, :width] = normed
            part = jnp.dot(normed, in_ref[...], preferred_element_type=F32)
            part = (part * jnp.concatenate([sel, sel], axis=1)).astype(BF)
            ext_out[r, width:] = part * jnp.array(adapter_scale, BF)
            return 0

        lax.fori_loop(0, tokens // tile, one, 0)

    return pl.pallas_call(
        kernel,
        out_shape=[
            jax.ShapeDtypeStruct((tokens, width), F32),
            jax.ShapeDtypeStruct((tokens, width + 2 * rank), BF),
            jax.ShapeDtypeStruct((tokens, rank), BF),
        ],
        in_specs=[VMEM] * 9,
        out_specs=[VMEM] * 3,
        compiler_params=pltpu.CompilerParams(vmem_limit_bytes=40 * 2**20),
        cost_estimate=pl.CostEstimate(
            flops=6 * tokens * width * rank, transcendentals=0, bytes_accessed=14 * tokens * width
        ),
    )(hidden, *branches, *branch_lows, select, second_output, gain, mlp_in)


def after_feed_forward(core, parts, middle, cotangent, select, gain, mlp_in):
    half, wide = parts[0].shape
    tokens, width = middle.shape
    rank = select.shape[1]
    tile = 128

    def kernel(
        core_ref, p0, p1, p2, mid_hbm, cot_hbm, sel_ref, gain_ref, in_ref, mid_out, branch_out, low_out,
        mid_s, cot_s, sems,
    ):
        start = pl.multiple_of(core_ref[0] * half, 16)
        copies = [
            pltpu.make_async_copy(mid_hbm.at[pl.ds(start, half)], mid_s, sems.at[0]),
            pltpu.make_async_copy(cot_hbm.at[pl.ds(start, half)], cot_s, sems.at[1]),
        ]
        for copy in copies:
            copy.start()
        for copy in copies:
            copy.wait()

        def one(t, _):
            r = pl.ds(pl.multiple_of(t * tile, tile), tile)
            sel = sel_ref[pl.ds(pl.multiple_of(start + t * tile, tile), tile), :]
            total = p0[r, :].astype(F32) + p1[r, :].astype(F32) + p2[r, :].astype(F32)
            low = (
                adapter_scale * total[:, width:] * jnp.concatenate([sel, sel], axis=1)
            ).astype(BF)
            low_out[r, :] = low
            grad = (total[:, :width] + nt(low, in_ref[...])) * gain_ref[...]
            middle = mid_s[r, :]
            scale = lax.rsqrt(jnp.mean(middle * middle, axis=1, keepdims=True) + norm_eps)
            inner = jnp.mean(middle * grad, axis=1, keepdims=True)
            out = cot_s[r, :].astype(F32) + scale * grad - middle * (scale * scale * scale * inner)
            mid_out[r, :] = out
            branch_out[r, :] = out.astype(BF)
            return 0

        lax.fori_loop(0, half // tile, one, 0)

    return pl.pallas_call(
        kernel,
        out_shape=[
            jax.ShapeDtypeStruct((half, width), F32),
            jax.ShapeDtypeStruct((half, width), BF),
            jax.ShapeDtypeStruct((half, 2 * rank), BF),
        ],
        in_specs=[SMEM] + [VMEM] * 3 + [HBM] * 2 + [VMEM] * 3,
        out_specs=[VMEM] * 3,
        scratch_shapes=[
            pltpu.VMEM((half, width), F32),
            pltpu.VMEM((half, width), BF),
            pltpu.SemaphoreType.DMA((2,)),
        ],
        compiler_params=pltpu.CompilerParams(vmem_limit_bytes=40 * 2**20),
        cost_estimate=pl.CostEstimate(
            flops=6 * half * width * rank, transcendentals=0, bytes_accessed=20 * half * width
        ),
    )(core, *parts, middle, cotangent, select, gain, mlp_in)


def feed_forward(places, core, normed, cot, new, old, totals, last):
    sums = totals != "none"
    first = totals is None
    before = list(totals) if sums and not first else []
    n_new, n_old = len(new), len(old)
    blocks = [list(unit[-1]) for unit in new + old]
    factors = [unit[-2] for unit in new + old]
    count, per = len(blocks), len(blocks[0])
    part_rows, wide = blocks[0][0].shape
    group, n_wide = normed[0].shape
    c_wide = cot[0].shape[1]
    rank = n_wide - c_wide
    width = c_wide - rank
    rows = 2 * group
    tile = group // 2
    tiles = rows // tile
    flat = [v for unit, factor in zip(blocks, factors) for v in unit + [factor]]
    old_flat = [v for unit in old for v in unit[:2]]
    n_sums = (4 if last else 2) if sums else 0

    def kernel(place_ref, core_ref, *refs):
        it = iter(refs)

        def take(n):
            return [next(it) for _ in range(n)]

        old_ref = take(2 * n_old)
        normed_hbm, cot_hbm = take(3), take(3)
        block_hbm = [take(per + 1) for _ in range(count)]
        before_hbm = take(len(before))
        sum_hbm = take(n_sums)
        act_ref, grad_ref, own_ref = (take(n_new) for _ in range(3))
        w_s, sem_w = take(2)
        if n_new:
            normed_s, cot_s, sem_x = take(3)
        if sums:
            acc_g, acc_o, sem_t, sem_out = take(4)
            fin_g, fin_o = (normed_s, cot_s) if last else (acc_g, acc_o)
        mine = core_ref[0]

        def fetch(k):
            slot = w_s.at[k % 2]
            return bring(block_hbm[k][:per], place_ref, slot, sem_w.at[k % 2]) + [
                pltpu.make_async_copy(
                    block_hbm[k][per], slot.at[pl.ds(width, 2 * rank)], sem_w.at[k % 2, places.shape[0]]
                )
            ]

        def load_x(t):
            copies = []
            for i, (src, dst) in enumerate(((normed_hbm, normed_s), (cot_hbm, cot_s))):
                if t < 2:
                    part, to = src[0].at[pl.ds(t * tile, tile)], t * tile
                else:
                    part = src[t - 1]
                    to = group + tile * (mine if t == 2 else 1 - mine)
                    to = pl.multiple_of(to, 16)
                copies.append(pltpu.make_async_copy(part, dst.at[pl.ds(to, tile)], sem_x.at[i, t]))
            return copies

        def load_t(t):
            r = pl.ds(t * tile, tile)
            return [
                pltpu.make_async_copy(src.at[r], dst.at[r], sem_t.at[i, t])
                for i, (src, dst) in enumerate(zip(before_hbm, (acc_g, acc_o)))
            ]

        def store_t(t, to):
            r = pl.ds(t * tile, tile)
            copies = []
            for i, src in enumerate((fin_g, fin_o)):
                dst = sum_hbm[2 * i + to].at[t // 2] if last else sum_hbm[i].at[r]
                copies.append(pltpu.make_async_copy(src.at[r], dst, sem_out.at[i, t]))
            return copies

        if n_new:
            for copy in load_x(0):
                copy.start()
        for copy in fetch(0):
            copy.start()
        if n_new:
            for copy in fetch(0):
                copy.wait()
            for t in range(1, tiles):
                for copy in load_x(t):
                    copy.start()
        if before:
            for t in range(tiles):
                for copy in load_t(t):
                    copy.start()
        for k in range(count):
            if k + 1 < count:
                for copy in fetch(k + 1):
                    copy.start()
            if k or not n_new:
                for copy in fetch(k):
                    copy.wait()
            slot = k % 2
            if k < n_new:
                act, grad = act_ref[k], grad_ref[k]
                for t in range(tiles):
                    r = pl.ds(t * tile, tile)
                    if k == 0 and t < 2:
                        for copy in load_x(t):
                            copy.wait()
                    if k == 0 and t == 2:
                        for copy in load_x(2) + load_x(3):
                            copy.wait()
                    x = normed_s[r, :]
                    gate = jnp.dot(x, w_s[slot, :, 0:WIDTH], preferred_element_type=F32)
                    up = jnp.dot(x, w_s[slot, :, WIDTH : 2 * WIDTH], preferred_element_type=F32)
                    back = jnp.dot(
                        cot_s[r, :],
                        w_s[slot, :c_wide, 2 * WIDTH : 3 * WIDTH],
                        preferred_element_type=F32,
                    )
                    sig = 1.0 / (1.0 + jnp.exp(-gate))
                    silu = gate * sig
                    act[r, :] = (silu * up).astype(BF)
                    grad[r, :WIDTH] = (back * up * (sig * (1.0 + gate * (1.0 - sig)))).astype(BF)
                    grad[r, WIDTH:] = (back * silu).astype(BF)
                low = normed_s[:, width:].T
                for part in range(2):
                    second = jnp.dot(
                        low[part * rank : (part + 1) * rank],
                        grad[:, part * WIDTH : (part + 1) * WIDTH],
                        preferred_element_type=F32,
                    ).astype(BF)
                    for at in range(0, WIDTH, rank):
                        to = part * WIDTH + at
                        own_ref[k][to : to + rank, :] = second[:, at : at + rank]
                own_ref[k][2 * WIDTH :, :] = jnp.dot(
                    act[...].T, cot_s[:, width:c_wide], preferred_element_type=F32
                ).astype(BF)
            else:
                act, grad = old_ref[2 * (k - n_new)], old_ref[2 * (k - n_new) + 1]
            if not sums:
                continue
            for t in range(tiles):
                r = pl.ds(t * tile, tile)
                if before and k == 0:
                    for copy in load_t(t):
                        copy.wait()
                for acc, fin, val, lo, hi, top in (
                    (acc_g, fin_g, grad, 0, 2 * WIDTH, n_wide),
                    (acc_o, fin_o, act, 2 * WIDTH, 3 * WIDTH, c_wide),
                ):
                    for at in range(0, top, 512):
                        n = slice(at, min(at + 512, top))
                        part = nt(val[r, :], w_s[slot, n, lo:hi])
                        if k or not first:
                            part = acc[r, n] + part
                        if k == count - 1:
                            fin[r, n] = part.astype(fin.dtype)
                        else:
                            acc[r, n] = part
                if k == count - 1 and last:
                    side = mine if t % 2 == 0 else 1 - mine
                    for to in range(2):

                        @pl.when(side == to)
                        def _():
                            for copy in store_t(t, to):
                                copy.start()

                elif k == count - 1:
                    for copy in store_t(t, 0):
                        copy.start()
        if sums:
            for t in range(tiles):
                for copy in store_t(t, 0):
                    copy.wait()

    scratch = [
        pltpu.VMEM((2, n_wide, wide), BF),
        pltpu.SemaphoreType.DMA((2, places.shape[0] + 1)),
    ]
    if n_new:
        scratch += [
            pltpu.VMEM((rows, n_wide), BF),
            pltpu.VMEM((rows, c_wide), BF),
            pltpu.SemaphoreType.DMA((2, tiles)),
        ]
    out_shape = []
    if sums:
        scratch += [
            pltpu.VMEM((rows, n_wide), F32),
            pltpu.VMEM((rows, c_wide), F32),
            pltpu.SemaphoreType.DMA((2, tiles)),
            pltpu.SemaphoreType.DMA((2, tiles)),
        ]
        for columns in (n_wide, c_wide):
            if last:
                out_shape += [jax.ShapeDtypeStruct((2, tile, columns), BF)] * 2
            else:
                out_shape += [jax.ShapeDtypeStruct((rows, columns), F32)]
    out_shape += [jax.ShapeDtypeStruct((rows, WIDTH), BF)] * n_new
    out_shape += [jax.ShapeDtypeStruct((rows, 2 * WIDTH), BF)] * n_new
    out_shape += [jax.ShapeDtypeStruct((3 * WIDTH, rank), BF)] * n_new
    n_hbm = 6 + len(flat)
    at = 2 + len(old_flat) + n_hbm
    out = pl.pallas_call(
        kernel,
        out_shape=out_shape,
        in_specs=[SMEM] * 2 + [VMEM] * len(old_flat) + [HBM] * (n_hbm + len(before)),
        out_specs=[HBM] * n_sums + [VMEM] * (3 * n_new),
        scratch_shapes=scratch,
        input_output_aliases={at: 0, at + 1: 1} if before and not last else {},
        compiler_params=pltpu.CompilerParams(vmem_limit_bytes=60 * 2**20),
        cost_estimate=pl.CostEstimate(
            flops=6 * (n_new + (count if sums else 0)) * rows * width * WIDTH,
            transcendentals=n_new * rows * WIDTH,
            bytes_accessed=4 * rows * width,
        ),
    )(places, core, *old_flat, *normed, *cot, *flat, *before)
    rest = out[n_sums:]
    return tuple(out[:n_sums]), list(zip(*(rest[i * n_new : (i + 1) * n_new] for i in range(3))))


DP = ("ring", "second", "first")


def make_body(n):
    ring_size = n // 4
    perms = ring_and_swaps(n)

    def move(value, link):
        return lax.ppermute(value, DP, perms[link])

    def other_core(value):
        return lax.ppermute(value, "tensor", [(0, 1), (1, 0)])

    def take(value, start, size, axis=0):
        return lax.dynamic_slice_in_dim(value, start, size, axis)

    def body(
        hidden_in, adapter_ids, attn_gain, mlp_gain, w_query, w_key, w_value, w_output, w_gate,
        w_up, w_down, in_query, second_query, in_key, second_key, in_value, second_value,
        in_output, second_output, in_gate, second_gate, in_up, second_up, in_down, second_down,
        cotangent,
    ):
        num_rows, width = hidden_in.shape
        half_rows = num_rows // 2
        half_width = width // 2
        rank_cols = in_query.shape[1]
        units = w_gate.shape[1] // 2
        chunks = units // WIDTH
        shard = w_query.shape[0]

        ring_at, bit_y, bit_x = (lax.axis_index(name) for name in DP)
        core = lax.axis_index("tensor")
        core_at = core.astype(jnp.int32).reshape(1)
        bits = {"x": bit_x, "y": bit_y}

        def in_order(bit, value, received, axis=0):
            first = jnp.where(bit == 0, value, received)
            return jnp.concatenate([first, jnp.where(bit == 0, received, value)], axis=axis)

        def half_of(value):
            return take(value, core * half_rows, half_rows)

        def both_halves(value):
            return in_order(core, value, other_core(value))

        def cols_of_core(value):
            return take(value, core * half_width, half_width, 1)

        row_index = lax.iota(jnp.int32, num_rows)
        is_later = row_index >= PROMPT
        seq_of = jnp.where(is_later, 1 + (row_index - PROMPT) // CONT_LEN, 0)
        position = jnp.where(is_later, PROMPT + (row_index - PROMPT) % CONT_LEN, row_index)
        seq_ids = lax.iota(jnp.int32, adapter_ids.shape[1])
        row_adapter = jnp.sum(
            jnp.where(seq_of[:, None] == seq_ids[None, :], adapter_ids[0][None, :], 0), axis=1
        )
        select = (lax.iota(jnp.int32, rank_cols)[None, :] // RANK == row_adapter[:, None]).astype(F32)
        select_three = jnp.concatenate([select] * 3, axis=1)
        inv_freq = rope_base ** (-2.0 * lax.iota(F32, HEAD_DIM // 2) / HEAD_DIM)
        angles = inv_freq[:, None] * position.astype(F32)[None, :]
        cos_table, sin_table = jnp.cos(angles), jnp.sin(angles)
        attn_in = jnp.concatenate([in_query, in_key, in_value], axis=1)
        mlp_in = jnp.concatenate([in_gate, in_up], axis=1)
        attn_gain_f = attn_gain.astype(F32)
        mlp_gain_f = mlp_gain.astype(F32).reshape(1, width)
        two = jnp.array(adapter_scale, BF)

        unit_start = bit_x * units

        def half_units(start):
            return (
                take(w_gate, start, units, 1),
                take(w_up, start, units, 1),
                take(w_down, start, units, 0).T,
            )

        mine, others = half_units(unit_start), half_units(units - unit_start)

        def chunk_of(parts, j):
            return jnp.concatenate([p[:, j * WIDTH : (j + 1) * WIDTH] for p in parts], axis=1)

        factor_parts = (
            take(second_gate, unit_start, units, 1),
            take(second_up, unit_start, units, 1),
            take(in_down, unit_start, units, 0),
        )
        blank = jnp.zeros((rank_cols, WIDTH), BF)
        chunk_cols = 3 * WIDTH

        def factors_of(j):
            cols = slice(j * WIDTH, (j + 1) * WIDTH)
            gate, up, down = factor_parts
            upper = jnp.concatenate([gate[:, cols], blank, down[cols].T], axis=1)
            return jnp.concatenate(
                [upper, jnp.concatenate([blank, up[:, cols], blank], axis=1)], axis=0
            )

        grad_low_down = (
            adapter_scale * product_with_transpose(cotangent, second_down) * select
        ).astype(BF)
        cot_wide = jnp.concatenate([cotangent, grad_low_down], axis=1)

        held = {
            "A0.o": jnp.concatenate([w_query, w_key], axis=1),
            "A1.p0": jnp.concatenate([w_output.T, w_value], axis=1),
            "C.o": half_of(cot_wide),
        }
        groups = exchanges_of(chunks)
        for i, group in enumerate(groups):
            held[f"E{i}.o"] = jnp.concatenate([chunk_of(others, j) for j in group], axis=1)
        plan = plan_transfers(ring_size, chunks)
        steps, arrivals = schedule(plan, chunks)
        when = {name: s for s, names in arrivals.items() for name in names}
        last_step = len(steps) - 1

        def there(tag):
            return max(s for name, s in when.items() if name.split(".")[0] == tag)

        def pieces(tag):
            found, places = [], []
            for r in range(ring_size):
                ring = (ring_at - r + ring_size) % ring_size
                if tag[0] == "A":
                    for other in range(2):
                        found.append(held[f"{tag}.{'x' if other else 'b'}{r}"])
                        bit = 1 - bit_x if other else bit_x
                        places += [(ring * 2 + bit_y) * 2 + bit, (ring * 2 + 1 - bit_y) * 2 + bit]
                else:
                    for other in range(2):
                        name = f"{tag}.q{r}" if other else f"{tag}.p{r}" if r else tag
                        found.append(held[name])
                        pair = ring * 2 + (1 - bit_y if other else bit_y)
                        places += [pair * 2 + bit_x, pair * 2 + 1 - bit_x]
            places = jnp.stack(places).astype(jnp.int32)
            if shard % 16:
                whole = jnp.zeros((n, shard, found[0].shape[1]), BF)
                for i in range(n):
                    part = found[i // 2][(i % 2) * shard : (i % 2 + 1) * shard]
                    whole = lax.dynamic_update_slice(whole, part[None], (places[i], 0, 0))
                return [whole.reshape(n * shard, -1)], jnp.zeros((1,), jnp.int32)
            return found, places

        v = {}
        hidden_wide = hidden_in.astype(F32)
        normed_a = rms_norm(hidden_wide, attn_gain_f).astype(BF)
        low_attn = (matrix_product(normed_a, attn_in) * select_three).astype(BF)
        lows = [low_attn[:, i * rank_cols : (i + 1) * rank_cols] * two for i in range(3)]

        def start_attention():
            found, places = pieces("A0")
            v["query"], v["key"], v["a0"] = queries_and_keys(
                places, found, normed_a, lows[0], lows[1], second_query, second_key, cos_table,
                sin_table,
            )
            return [v["key"]]

        def finish_attention():
            found, places = pieces("A1")
            v["value"], v["attended"], v["lse"], branch, branch_low, v["a1"] = attention(
                places, found, normed_a, lows[2], second_value, v["query"], v["key"], in_output
            )
            v["branches"] = (branch, other_core(branch))
            v["branch_lows"] = (branch_low, other_core(branch_low))
            return [v["value"]]

        def start_feed_forward():
            v["middle"], v["normed"], v["low_output"] = after_attention(
                hidden_in, v["branches"], v["branch_lows"], select, second_output, mlp_gain_f, mlp_in
            )
            held["N.o"] = half_of(v["normed"])
            return [v["low_output"]]

        def meet_neighbour():
            v["normed_all"] = (v["normed"], held["N.x"], other_core(held["N.x"]))
            v["cot_all"] = (cot_wide, held["C.x"], other_core(held["C.x"]))
            return [v["normed_all"][2], v["cot_all"][2]]

        unit_out = {}

        def feed(new, old, totals, last):
            found = {j: pieces(f"M{j}") for j in new + old}
            sums, results = feed_forward(
                found[(new + old)[0]][1],
                core_at,
                v["normed_all"],
                v["cot_all"],
                [(factors_of(j), found[j][0]) for j in new],
                [unit_out[j][:2] + (factors_of(j), found[j][0]) for j in old],
                totals,
                last,
            )
            unit_out.update(zip(new, results))
            return sums

        def units_only(new):
            def run():
                feed(new, [], "none", False)
                return [unit_out[new[-1]][0]]

            return run

        def sums_only(old):
            def run():
                v["totals"] = feed([], old, None, False)
                return [v["totals"][0]]

            return run

        order = sorted(range(chunks), key=lambda j: there(f"M{j}"))
        events = {}

        def at_step(s, run):
            events.setdefault(min(s, last_step), []).append(run)

        at_step(there("A0"), start_attention)
        at_step(there("A1"), finish_attention)
        at_step(there("A1") + NORMED_AFTER - 1, start_feed_forward)
        begin = there("N")
        at_step(begin, meet_neighbour)
        early, later, final = order[: chunks - 3], order[chunks - 3 : chunks - 1], order[-1]
        at = begin
        for i in range(0, len(early), 2):
            pair = early[i : i + 2]
            at = max([at] + [there(f"M{j}") for j in pair])
            at_step(at, units_only(pair))
            at += 1
        at_step(max(at, last_step - 4), sums_only(early))
        for j in later:
            at_step(max(at, there(f"M{j}")), units_only([j]))

        waits = []
        for s, step in enumerate(steps):
            sources = sorted({plan[name][1] for name in step})
            if s:
                arrived = [name for name in arrivals.get(s, []) if name not in sources]
                if sources and arrived + waits:
                    tied = tie([held[k] for k in sources], [held[k] for k in arrived] + waits)
                    held.update(zip(sources, tied))
                    waits = []
            for name in step:
                held[name] = move(held[plan[name][1]], plan[name][0])
            for name in arrivals.get(s + 1, []):
                if name.endswith(".e"):
                    for i, j in enumerate(groups[int(name[1:-2])]):
                        got = held[name][:, i * chunk_cols : (i + 1) * chunk_cols]
                        held[f"M{j}"] = jnp.concatenate([chunk_of(mine, j), got], axis=0)
                elif name == "A0.y":
                    held["A0.b0"] = jnp.concatenate([held["A0.o"], held[name]], axis=0)
                elif name.startswith("A1") and name[3] in "pq":
                    pair = [f"A1.{side}{name[4:]}" for side in "pq"]
                    if f"A1.b{name[4:]}" not in held and all(p in held for p in pair):
                        if max(when.get(p, 0) for p in pair) <= s + 1:
                            held[f"A1.b{name[4:]}"] = jnp.concatenate([held[p] for p in pair], axis=0)
            for run in events.get(s, []):
                waits += run()

        totals = feed([final], later, v["totals"], True)
        grad_keep, grad_send, out_keep, out_send = totals

        def after(values, *others):
            return tie(list(values), list(others), 0)

        def exchange(value, axes, parts):
            share = value.shape[0] // parts
            return lax.all_to_all(value.reshape(parts, share, rank_cols), axes, 0, 0)

        def total(parts):
            return jnp.sum(parts.astype(F32), axis=0).astype(BF)

        grad_got = other_core(grad_send)
        grad_out = (grad_keep[1].astype(F32) + grad_got[1].astype(F32)).astype(BF)
        grad_in_parts = (grad_keep[0], grad_got[0], move(grad_out, "x"))
        out_send, *own = after([out_send] + [unit_out[j][2] for j in range(chunks)], grad_out)
        out_got = other_core(out_send)
        out_out = (out_keep[1].astype(F32) + out_got[1].astype(F32)).astype(BF)
        got_units = exchange(jnp.concatenate(own, axis=0), DP[:2], n // 2)

        grad_middle, grad_branch, grad_low_mlp = after_feed_forward(
            core_at, grad_in_parts, v["middle"], cotangent, select, mlp_gain_f, mlp_in
        )
        out_in = move(after([out_out], grad_branch)[0], "x")
        grad_branch_other = other_core(grad_branch)
        grad_low_mlp = both_halves(grad_low_mlp)
        delta_mlp = transpose_then_product(
            cols_of_core(v["normed"][:, :width]), grad_low_mlp
        ).astype(BF)
        got_mlp = exchange(
            jnp.concatenate([delta_mlp[:, :rank_cols], delta_mlp[:, rank_cols:]], axis=0), DP, n
        )

        back, back_low, seconds, first_output, second_output_blocks = attention_back(
            core_at, (grad_branch, grad_branch_other), select, second_output, v["low_output"],
            v["attended"], in_output, v["a0"], v["a1"], v["query"], v["key"], v["value"], v["lse"],
            cos_table, sin_table, second_query, second_key, second_value, *lows,
        )
        back_low, got_units, got_mlp, out_in = after([back_low, got_units, got_mlp, out_in])
        back_low = back_low + other_core(back_low)
        grad_low_attn = (back_low * select_three).astype(BF)
        delta_attn = transpose_then_product(cols_of_core(normed_a), grad_low_attn).astype(BF)

        out_sum = out_keep[0].astype(F32) + out_got[0].astype(F32) + out_in.astype(F32)
        low_down = (out_sum[:, width:] * half_of(select)).astype(BF)
        second_down_part = (
            adapter_scale * transpose_then_product(both_halves(low_down), cols_of_core(cotangent))
        ).astype(BF)
        late = jnp.concatenate(
            [seconds]
            + [delta_attn[:, i * rank_cols : (i + 1) * rank_cols] for i in range(3)]
            + [second_down_part[:, at : at + rank_cols] for at in range(0, half_width, rank_cols)]
            + [second_output_blocks, first_output],
            axis=0,
        )
        got_late = exchange(late, DP, n)
        got_units, got_mlp, back, out_sum, grad_middle = after(
            [got_units, got_mlp, back, out_sum, grad_middle], late
        )

        def join_ring(value):
            found = [value] + [move(value, f"z{r}") for r in range(1, ring_size)]
            back = jnp.stack(found[::-1] + found[::-1], axis=0)
            return take(back, ring_size - 1 - ring_at, ring_size)

        def pair(bit, value, received):
            return jnp.stack([jnp.where(bit == 0, value, received), jnp.where(bit == 0, received, value)])

        def of_core_pair(value):
            return pair(core, value, other_core(value))

        units_all = join_ring(total(got_units))
        units_all = jnp.swapaxes(pair(bit_y, units_all, move(units_all, "y")), 0, 1)
        units_all = units_all.reshape(chunks, 3 * WIDTH, rank_cols)
        units_all = of_core_pair(pair(bit_x, units_all, move(units_all, "x"))).astype(F32)

        def unit_columns(start):
            return jnp.concatenate(
                [
                    units_all[c, h, j, at : at + rank_cols]
                    for c in range(2)
                    for h in range(2)
                    for j in range(chunks)
                    for at in range(start, start + WIDTH, rank_cols)
                ],
                axis=1,
            )

        gradient_second_gate, gradient_second_up = unit_columns(0), unit_columns(WIDTH)
        delta_in_down = units_all[:, :, :, 2 * WIDTH :].reshape(-1, rank_cols)

        layer_output = both_halves(
            (
                half_of(v["middle"])
                + out_sum[:, :width]
                + adapter_scale * matrix_product(low_down, second_down)
            ).astype(BF)
        )
        back_half = half_of(back).astype(F32) + other_core(
            take(back, (1 - core) * half_rows, half_rows)
        ).astype(F32)
        grad_normed_a = back_half + product_with_transpose(half_of(grad_low_attn), attn_in)
        grad_in = both_halves(
            (grad_middle + rms_back(half_of(hidden_wide), attn_gain_f, grad_normed_a)).astype(BF)
        )

        sums = jnp.concatenate([total(got_mlp), total(got_late)], axis=0)
        cut = got_mlp.shape[1]
        sums = join_ring(sums)
        by_x, by_y, by_both = (move(sums, link) for link in ("x", "y", "xy"))
        sums = pair(bit_y, pair(bit_x, sums, by_x), pair(bit_x, by_y, by_both))
        sums = of_core_pair(jnp.transpose(sums, (2, 0, 1, 3, 4)))

        def parts_of(value, sizes):
            value = value.reshape(2, -1, rank_cols)
            at, parts = 0, []
            for size in sizes:
                parts.append(value[:, at : at + size].astype(F32))
                at += size
            return parts

        query_cols, key_cols = second_query.shape[1], second_key.shape[1]
        mlp_parts = parts_of(sums[..., :cut, :], [half_width] * 2)
        late_parts = parts_of(sums[..., cut:, :], [seconds.shape[0]] + [half_width] * 6)

        def rows(part):
            return part.reshape(-1, rank_cols)

        def columns(part):
            return jnp.concatenate(
                [part[c, at : at + rank_cols] for c in range(2) for at in range(0, part.shape[1], rank_cols)],
                axis=1,
            )

        late_seconds = columns(late_parts[0])

        def second_of(start, size):
            per_core = late_seconds.shape[1] // 2
            return jnp.concatenate(
                [late_seconds[:, c * per_core + start : c * per_core + start + size] for c in range(2)],
                axis=1,
            )

        return (
            layer_output,
            grad_in,
            rows(late_parts[1]),
            second_of(0, query_cols),
            rows(late_parts[2]),
            second_of(query_cols, key_cols),
            rows(late_parts[3]),
            second_of(query_cols + key_cols, key_cols),
            rows(late_parts[6]),
            columns(late_parts[5]),
            rows(mlp_parts[0]),
            gradient_second_gate,
            rows(mlp_parts[1]),
            gradient_second_up,
            delta_in_down,
            columns(late_parts[4]),
        )

    return body


def solution(mesh):
    n, tensor = mesh.shape["dp"], mesh.shape["tensor"]
    split = jax.sharding.Mesh(mesh.devices.reshape(n // 4, 2, 2, tensor), DP + ("tensor",))
    return jax.shard_map(
        make_body(n),
        mesh=split,
        in_specs=(
            P(DP, None), P(DP, None), P(), P(), P(DP, "tensor"), P(DP, "tensor"), P(DP, "tensor"),
            P("tensor", DP), P(DP, "tensor"), P(DP, "tensor"), P("tensor", DP), P(),
            P(None, "tensor"), P(), P(None, "tensor"), P(), P(None, "tensor"), P("tensor", None),
            P(), P(), P(None, "tensor"), P(), P(None, "tensor"), P("tensor", None), P(), P(DP, None),
        ),
        out_specs=(P(DP, None), P(DP, None)) + (P(),) * 14,
        check_vma=False,
    )
```

```python
import math

import jax
import jax.numpy as jnp
from jax import lax
from jax.experimental import pallas as pl
from jax.experimental.pallas import tpu as pltpu
from jax.sharding import PartitionSpec as P

HEAD_DIM = 80
RANK = 16
PROMPT = 256
CONT_LEN = 128
WIDTH = 256
ADAPTER_COLS = 128
BLOCKS = 8

adapter_scale = 2.0
norm_eps = 1e-05
rope_base = 1000000.0

BF = jnp.bfloat16
F32 = jnp.float32

LAG = 2
STEP_FLOPS = 20_000_000_000
NORMED_AFTER = 4
EXCHANGES = ((0, 1), (2, 3), (4, 5, 6))
EXCHANGE_PRIORITY = (-40, -39, 8)
ATTN_PRIORITY = (-20, -10)
YZ_CHUNKS = ()
LAST_WIDE = 30


def matrix_product(left, right):
    return jnp.dot(left, right, preferred_element_type=F32)


def product_with_transpose(left, right):
    return lax.dot_general(left, right, (((1,), (1,)), ((), ())), preferred_element_type=F32)


def transpose_then_product(left, right):
    return lax.dot_general(left, right, (((0,), (0,)), ((), ())), preferred_element_type=F32)


def rms_norm(values, gain_vec):
    return (
        values * lax.rsqrt(jnp.mean(values * values, axis=-1, keepdims=True) + norm_eps) * gain_vec
    )


def rms_back(values, gain_vec, grad):
    scale = lax.rsqrt(jnp.mean(values * values, axis=-1, keepdims=True) + norm_eps)
    e = gain_vec * grad
    return scale * e - values * (scale * scale * scale) * jnp.mean(values * e, axis=-1, keepdims=True)


def ring_and_swaps(n):
    perms = {
        "y": [(i, i ^ 2) for i in range(n)],
        "x": [(i, i ^ 1) for i in range(n)],
        "xy": [(i, i ^ 3) for i in range(n)],
    }
    for r in range(1, n // 4):
        perms[f"z{r}"] = [(i, (i + 4 * r) % n) for i in range(n)]
    perms["z"] = perms["z1"]
    return perms


def plan_transfers(ring_size, chunks):
    plan = {}
    first, second = ATTN_PRIORITY
    plan["A0.y"] = ("y", "A0.o", first, 1)
    for r in range(ring_size):
        if r:
            plan[f"A0.b{r}"] = ("z", f"A0.b{r - 1}", first + 0.01 * r, 2)
            plan[f"A1.p{r}"] = ("z", f"A1.p{r - 1}", second + 0.01 * r, 1)
        plan[f"A1.q{r}"] = ("y", f"A1.p{r}", second + 0.01 * r, 1)
        plan[f"A0.x{r}"] = ("x", f"A0.b{r}", first + 0.01 * r, 2)
        plan[f"A1.x{r}"] = ("x", f"A1.b{r}", second + 0.01 * r, 2)
    for i, group in enumerate(exchanges_of(chunks)):
        plan[f"E{i}.e"] = ("x", f"E{i}.o", EXCHANGE_PRIORITY[min(i, 2)], (len(group) + 1) // 2)
    for j in range(chunks):
        tag = f"M{j}"
        for r in range(ring_size):
            source = (f"{tag}.p{r}" if r else tag)
            if r:
                before = f"{tag}.p{r - 1}" if r > 1 else tag
                plan[f"{tag}.p{r}"] = ("z", before, j + 0.01 * r, 1)
            plan[f"{tag}.q{r}"] = ("y", source, j + 0.01 * r, 1)
    plan["C.x"] = ("x", "C.o", LAST_WIDE, 3)
    plan["N.x"] = ("x", "N.o", -50, 3)
    return plan


def exchanges_of(chunks):
    return EXCHANGES[:2] + (tuple(range(4, chunks)),)


def schedule(plan, chunks):
    makes = {"A0.y": ["A0.b0"]}
    for i, group in enumerate(exchanges_of(chunks)):
        makes[f"E{i}.e"] = [f"M{j}" for j in group]
    ready, busy, arrivals = {}, {}, {}
    for _, source, _, _ in plan.values():
        if source.endswith(".o") and source != "N.o":
            ready[source] = 0
    ready["A1.p0"] = 0
    steps, waiting, now = [], dict(plan), 0
    while waiting:
        step = []
        if "N.o" not in ready and not any(name.startswith("A1") for name in waiting):
            ready["N.o"] = max(s for s, names in arrivals.items() if "A1.x" in str(names))
            ready["N.o"] += NORMED_AFTER
        for link in "xyz":
            able = [
                (entry[2], name)
                for name, entry in waiting.items()
                if entry[0] == link
                and busy.get(link, 0) <= now
                and ready.get(entry[1], 1 << 30) <= now
            ]
            if able:
                name = min(able)[1]
                length = waiting.pop(name)[3]
                step.append(name)
                busy[link] = now + length
                ready[name] = now + (LAG if length == 1 else length)
                arrivals.setdefault(ready[name], []).append(name)
                for made in makes.get(name, []):
                    ready[made] = ready[name]
                if name.startswith("A1") and name[3] in "pq":
                    pair = (f"A1.p{name[4:]}", f"A1.q{name[4:]}")
                    if pair[0] in ready and pair[1] in ready:
                        ready[f"A1.b{name[4:]}"] = max(ready[p] for p in pair)
        steps.append(step)
        now += 1
    return steps, arrivals


def tie(values, others, flops=STEP_FLOPS):
    def kernel(*refs):
        pass

    spec = pl.BlockSpec(memory_space=pltpu.HBM)
    n = len(values)
    return pl.pallas_call(
        kernel,
        out_shape=[jax.ShapeDtypeStruct(v.shape, v.dtype) for v in values],
        in_specs=[spec] * (n + len(others)),
        out_specs=[spec] * n,
        input_output_aliases={i: i for i in range(n)},
        cost_estimate=pl.CostEstimate(flops=flops, transcendentals=0, bytes_accessed=0),
    )(*values, *others)


def bring(blocks, place_ref, target, sems):
    total = sum(block.shape[0] for block in blocks)
    rows = total // place_ref.shape[0]
    copies = []
    for block in blocks:
        for start in range(0, block.shape[0], rows):
            i = len(copies)
            to = pl.multiple_of(place_ref[i] * rows, math.gcd(rows, 16))
            copies.append(
                pltpu.make_async_copy(
                    block.at[pl.ds(start, rows)], target.at[pl.ds(to, rows)], sems.at[i]
                )
            )
    return copies


HBM = pl.BlockSpec(memory_space=pl.ANY)
VMEM = pl.BlockSpec(memory_space=pltpu.VMEM)
SMEM = pl.BlockSpec(memory_space=pltpu.SMEM)


def nt(left, right):
    return lax.dot_general(left, right, (((1,), (1,)), ((), ())), preferred_element_type=F32)


def turn(upright, cos_ref, sin_ref, sign, row):
    half = HEAD_DIM // 2
    first, second = upright[row : row + half], upright[row + half : row + 2 * half]
    cos, sin = cos_ref[...], sin_ref[...] * sign
    return jnp.concatenate([first * cos - second * sin, second * cos + first * sin], axis=0)


def queries_and_keys(places, blocks, normed, low_query, low_key, second_query, second_key, cos, sin):
    count = len(blocks)
    tokens, width = normed.shape
    cols = blocks[0].shape[1]
    q_cols, k_cols = second_query.shape[1], second_key.shape[1]

    def kernel(place_ref, x_ref, lq_ref, lk_ref, sq_ref, sk_ref, cos_ref, sin_ref, *refs):
        parts, (q_out, k_out, w_out, w_s, sems, sem_out) = refs[:count], refs[count:]
        copies = bring(parts, place_ref, w_s, sems)
        for copy in copies:
            copy.start()
        for copy in copies:
            copy.wait()
        keep = pltpu.make_async_copy(w_s, w_out, sem_out)
        keep.start()
        x = x_ref[...]
        step = 4 * HEAD_DIM
        for start, low, second, out, shift in [
            (at, lq_ref, sq_ref, q_out, 0) for at in range(0, q_cols, step)
        ] + [(q_cols + at, lk_ref, sk_ref, k_out, q_cols) for at in range(0, k_cols, step)]:
            own = start - shift
            part = jnp.dot(x, w_s[:, start : start + step], preferred_element_type=F32)
            part += jnp.dot(low[...], second[:, own : own + step], preferred_element_type=F32)
            upright = part.T
            for row in range(0, step, HEAD_DIM):
                out[own + row : own + row + HEAD_DIM, :] = turn(
                    upright, cos_ref, sin_ref, 1.0, row
                ).astype(BF)
        keep.wait()

    return pl.pallas_call(
        kernel,
        out_shape=[
            jax.ShapeDtypeStruct((q_cols, tokens), BF),
            jax.ShapeDtypeStruct((k_cols, tokens), BF),
            jax.ShapeDtypeStruct((width, cols), BF),
        ],
        in_specs=[SMEM] + [VMEM] * 7 + [HBM] * count,
        out_specs=[VMEM, VMEM, HBM],
        scratch_shapes=[
            pltpu.VMEM((width, cols), BF),
            pltpu.SemaphoreType.DMA((places.shape[0],)),
            pltpu.SemaphoreType.DMA,
        ],
        compiler_params=pltpu.CompilerParams(vmem_limit_bytes=48 * 2**20),
        cost_estimate=pl.CostEstimate(
            flops=2 * tokens * width * cols, transcendentals=0, bytes_accessed=4 * width * cols
        ),
    )(places, normed, low_query, low_key, second_query, second_key, cos, sin, *blocks)


def seen(rows, columns, row_start, column_start):
    key = lax.broadcasted_iota(jnp.int32, (rows, columns), 0)
    query = lax.broadcasted_iota(jnp.int32, (rows, columns), 1)
    causal = key <= query
    if row_start >= PROMPT:
        causal = causal & (key // CONT_LEN == query // CONT_LEN)
    return causal


def attention(places, blocks, normed, low_value, second_value, query, key, in_output):
    count = len(blocks)
    tokens, width = normed.shape
    cols = blocks[0].shape[1]
    q_cols, k_cols = query.shape[0], key.shape[0]
    kv_heads = k_cols // HEAD_DIM
    group = q_cols // k_cols
    scale = 1.0 / math.sqrt(HEAD_DIM)

    def kernel(place_ref, x_ref, lv_ref, sv_ref, q_ref, k_ref, io_ref, *refs):
        parts = refs[:count]
        v_out, att_out, lse_out, branch_out, low_out, w_out, w_s, att_s, sems, sem_out = refs[count:]
        copies = bring(parts, place_ref, w_s, sems)
        for copy in copies:
            copy.start()
        for copy in copies:
            copy.wait()
        keep = pltpu.make_async_copy(w_s, w_out, sem_out)
        keep.start()
        value = jnp.dot(x_ref[...], w_s[:, q_cols:cols], preferred_element_type=F32)
        value += jnp.dot(lv_ref[...], sv_ref[...], preferred_element_type=F32)
        v_out[...] = value.T.astype(BF)
        seen_first = seen(PROMPT, PROMPT, 0, 0)
        seen_second = seen(tokens - PROMPT, tokens - PROMPT, PROMPT, PROMPT)

        def one_head(g, _):
            k_rows = pl.ds(pl.multiple_of(g * HEAD_DIM, 16), HEAD_DIM)
            keys = k_ref[k_rows, :].T
            values = v_out[k_rows, :]
            for h in range(group):
                rows = pl.ds(pl.multiple_of((g * group + h) * HEAD_DIM, 16), HEAD_DIM)
                head = q_ref[rows, :]
                early = jnp.dot(keys[:PROMPT], head[:, :PROMPT], preferred_element_type=F32)
                late = jnp.dot(keys, head[:, PROMPT:], preferred_element_type=F32)
                early = jnp.where(seen_first, early * scale, -1e30)
                late_prompt = late[:PROMPT] * scale
                late_own = jnp.where(seen_second, late[PROMPT:] * scale, -1e30)
                top = jnp.max(early, axis=0, keepdims=True)
                expo = jnp.exp(early - top)
                total = jnp.sum(expo, axis=0, keepdims=True)
                prob = (expo * (1.0 / total)).astype(BF)
                lse_out[g, h : h + 1, :PROMPT] = top + jnp.log(total)
                att_s[rows, :PROMPT] = jnp.dot(
                    values[:, :PROMPT], prob, preferred_element_type=F32
                ).astype(BF)
                top = jnp.maximum(
                    jnp.max(late_prompt, axis=0, keepdims=True),
                    jnp.max(late_own, axis=0, keepdims=True),
                )
                expo_p, expo_o = jnp.exp(late_prompt - top), jnp.exp(late_own - top)
                total = jnp.sum(expo_p, axis=0, keepdims=True) + jnp.sum(
                    expo_o, axis=0, keepdims=True
                )
                inverse = 1.0 / total
                prob = jnp.concatenate(
                    [(expo_p * inverse).astype(BF), (expo_o * inverse).astype(BF)], axis=0
                )
                lse_out[g, h : h + 1, PROMPT:] = top + jnp.log(total)
                att_s[rows, PROMPT:] = jnp.dot(
                    values, prob, preferred_element_type=F32
                ).astype(BF)
            return 0

        lax.fori_loop(0, kv_heads, one_head, 0)
        att_out[...] = att_s[...].T
        attended = att_out[...]
        low_out[...] = jnp.dot(attended, io_ref[...], preferred_element_type=F32)
        for at in range(0, width, 512):
            branch_out[:, at : at + 512] = nt(attended, w_s[at : at + 512, :q_cols]).astype(BF)
        keep.wait()

    return pl.pallas_call(
        kernel,
        out_shape=[
            jax.ShapeDtypeStruct((k_cols, tokens), BF),
            jax.ShapeDtypeStruct((tokens, q_cols), BF),
            jax.ShapeDtypeStruct((kv_heads, group, tokens), F32),
            jax.ShapeDtypeStruct((tokens, width), BF),
            jax.ShapeDtypeStruct((tokens, in_output.shape[1]), F32),
            jax.ShapeDtypeStruct((width, cols), BF),
        ],
        in_specs=[SMEM] + [VMEM] * 6 + [HBM] * count,
        out_specs=[VMEM] * 5 + [HBM],
        scratch_shapes=[
            pltpu.VMEM((width, cols), BF),
            pltpu.VMEM((q_cols, tokens), BF),
            pltpu.SemaphoreType.DMA((places.shape[0],)),
            pltpu.SemaphoreType.DMA,
        ],
        compiler_params=pltpu.CompilerParams(vmem_limit_bytes=48 * 2**20),
        cost_estimate=pl.CostEstimate(
            flops=4 * tokens * width * cols, transcendentals=0, bytes_accessed=4 * width * cols
        ),
    )(places, normed, low_value, second_value, query, key, in_output, *blocks)


def attention_back(
    core, halves, select, second_output, low_output, attended, in_output, full_a0, full_a1, query,
    key, value, lse, cos, sin, second_query, second_key, second_value, low_query, low_key, low_value,
):
    half_tokens, width = halves[0].shape
    tokens = 2 * half_tokens
    cols = full_a0.shape[1]
    q_cols, k_cols = query.shape[0], key.shape[0]
    rank = second_query.shape[0]
    kv_heads = k_cols // HEAD_DIM
    group = q_cols // k_cols
    scale = 1.0 / math.sqrt(HEAD_DIM)

    def kernel(
        core_ref, mine_hbm, other_hbm, sel_ref, so_ref, lo_ref, att_ref, io_ref, a0_hbm, a1_hbm, q_ref, k_ref, v_ref, lse_ref, cos_ref, sin_ref,
        sq_ref, sk_ref, sv_ref, lq_ref, lk_ref, lv_ref, back_out, low_out, factor_out, a0, a1, gb_ref, glo_ref, ga_s, g_s, gw_s, sems,
    ):
        mine = core_ref[0]
        copies = [
            pltpu.make_async_copy(a1_hbm, a1, sems.at[0]),
            pltpu.make_async_copy(a0_hbm, a0, sems.at[1]),
            pltpu.make_async_copy(
                mine_hbm, gb_ref.at[pl.ds(pl.multiple_of(mine * half_tokens, 16), half_tokens)], sems.at[2]
            ),
            pltpu.make_async_copy(
                other_hbm,
                gb_ref.at[pl.ds(pl.multiple_of((1 - mine) * half_tokens, 16), half_tokens)],
                sems.at[3],
            ),
        ]
        for i in (2, 3, 0, 1):
            copies[i].start()
        for i in (2, 3):
            copies[i].wait()
        glo_ref[...] = (adapter_scale * nt(gb_ref[...], so_ref[...]) * sel_ref[...]).astype(BF)
        at_second = q_cols + 2 * k_cols
        at_first = at_second + width // 2
        factor_out[at_first : at_first + q_cols, :] = jnp.dot(
            att_ref[...].T, glo_ref[...], preferred_element_type=F32
        ).astype(BF)
        own = gb_ref[:, pl.ds(pl.multiple_of(mine * (width // 2), 128), width // 2)]
        factor_out[at_second:at_first, :] = (
            adapter_scale * jnp.dot(own.T, lo_ref[...], preferred_element_type=F32)
        ).astype(BF)
        factor_out[at_first + q_cols :, :] = jnp.zeros(
            (4 * q_cols - at_first - q_cols, rank), BF
        )
        copies[0].wait()
        step = 4 * HEAD_DIM
        for at in range(0, q_cols, step):
            part = jnp.dot(gb_ref[...], a1[:, at : at + step], preferred_element_type=F32)
            part += nt(glo_ref[...], io_ref[at : at + step, :])
            ga_s[at : at + step, :] = part.astype(BF).T
        seen_first = seen(PROMPT, PROMPT, 0, 0)
        seen_second = seen(tokens - PROMPT, tokens - PROMPT, PROMPT, PROMPT)

        def one_head(g, _):
            k_rows = pl.ds(pl.multiple_of(g * HEAD_DIM, 16), HEAD_DIM)
            keys_up = k_ref[k_rows, :]
            keys = keys_up.T
            values = v_ref[k_rows, :].T
            grad_k, grad_v = [0.0, 0.0], [0.0, 0.0]
            for h in range(group):
                rows = pl.ds(pl.multiple_of((g * group + h) * HEAD_DIM, 16), HEAD_DIM)
                head, grad = q_ref[rows, :], ga_s[rows, :]
                lse_h = lse_ref[g, h : h + 1, :]
                score = jnp.dot(keys[:PROMPT], head[:, :PROMPT], preferred_element_type=F32)
                prob = jnp.where(seen_first, jnp.exp(score * scale - lse_h[:, :PROMPT]), 0.0)
                grad_prob = jnp.dot(values[:PROMPT], grad[:, :PROMPT], preferred_element_type=F32)
                row_term = jnp.sum(prob * grad_prob, axis=0, keepdims=True)
                grad_score = (prob * (grad_prob - row_term)).astype(BF)
                prob = prob.astype(BF)
                grad_q_early = jnp.dot(
                    keys_up[:, :PROMPT], grad_score, preferred_element_type=F32
                )
                grad_v[0] += nt(grad[:, :PROMPT], prob)
                grad_k[0] += nt(head[:, :PROMPT], grad_score)
                score = jnp.dot(keys, head[:, PROMPT:], preferred_element_type=F32)
                expo = jnp.exp(score * scale - lse_h[:, PROMPT:])
                prob_p = expo[:PROMPT]
                prob_o = jnp.where(seen_second, expo[PROMPT:], 0.0)
                grad_prob = jnp.dot(values, grad[:, PROMPT:], preferred_element_type=F32)
                row_term = jnp.sum(prob_p * grad_prob[:PROMPT], axis=0, keepdims=True) + jnp.sum(
                    prob_o * grad_prob[PROMPT:], axis=0, keepdims=True
                )
                score_p = (prob_p * (grad_prob[:PROMPT] - row_term)).astype(BF)
                score_o = (prob_o * (grad_prob[PROMPT:] - row_term)).astype(BF)
                grad_q_late = jnp.dot(
                    keys_up, jnp.concatenate([score_p, score_o], axis=0), preferred_element_type=F32
                )
                grad_v[0] += nt(grad[:, PROMPT:], prob_p.astype(BF))
                grad_v[1] += nt(grad[:, PROMPT:], prob_o.astype(BF))
                grad_k[0] += nt(head[:, PROMPT:], score_p)
                grad_k[1] += nt(head[:, PROMPT:], score_o)
                grad_q = jnp.concatenate([grad_q_early, grad_q_late], axis=1) * scale
                g_s[rows, :] = turn(grad_q, cos_ref, sin_ref, -1.0, 0).astype(BF)
            grad_key = jnp.concatenate(grad_k, axis=1) * scale
            g_s[pl.ds(pl.multiple_of(q_cols + g * HEAD_DIM, 16), HEAD_DIM), :] = turn(
                grad_key, cos_ref, sin_ref, -1.0, 0
            ).astype(BF)
            g_s[pl.ds(pl.multiple_of(q_cols + k_cols + g * HEAD_DIM, 16), HEAD_DIM), :] = (
                jnp.concatenate(grad_v, axis=1).astype(BF)
            )
            return 0

        lax.fori_loop(0, kv_heads, one_head, 0)
        gw_s[...] = g_s[...].T
        for at, size, low in (
            (0, q_cols, lq_ref),
            (q_cols, k_cols, lk_ref),
            (q_cols + k_cols, k_cols, lv_ref),
        ):
            factor_out[at : at + size, :] = jnp.dot(
                g_s[at : at + size, :], low[...], preferred_element_type=F32
            ).astype(BF)
        for i, (at, size, second) in enumerate(
            ((0, q_cols, sq_ref), (q_cols, k_cols, sk_ref), (q_cols + k_cols, k_cols, sv_ref))
        ):
            low_out[:, i * rank : (i + 1) * rank] = adapter_scale * nt(
                gw_s[:, at : at + size], second[...]
            )
        copies[1].wait()
        for at in range(0, width, 512):
            rows = slice(at, at + 512)
            part = nt(gw_s[:, :cols], a0[rows, :]) + nt(gw_s[:, cols:], a1[rows, q_cols:])
            back_out[:, rows] = part.astype(BF)

    return pl.pallas_call(
        kernel,
        out_shape=[
            jax.ShapeDtypeStruct((tokens, width), BF),
            jax.ShapeDtypeStruct((tokens, 3 * rank), F32),
            jax.ShapeDtypeStruct((4 * q_cols, rank), BF),
        ],
        in_specs=[SMEM, HBM, HBM] + [VMEM] * 5 + [HBM] * 2 + [VMEM] * 12,
        out_specs=[VMEM] * 3,
        scratch_shapes=[
            pltpu.VMEM((width, cols), BF),
            pltpu.VMEM((width, cols), BF),
            pltpu.VMEM((tokens, width), BF),
            pltpu.VMEM((tokens, rank), BF),
            pltpu.VMEM((q_cols, tokens), BF),
            pltpu.VMEM((q_cols + 2 * k_cols, tokens), BF),
            pltpu.VMEM((tokens, q_cols + 2 * k_cols), BF),
            pltpu.SemaphoreType.DMA((4,)),
        ],
        compiler_params=pltpu.CompilerParams(vmem_limit_bytes=56 * 2**20),
        cost_estimate=pl.CostEstimate(
            flops=20 * tokens * width * cols, transcendentals=0, bytes_accessed=4 * width * cols
        ),
    )(
        core, *halves, select, second_output, low_output, attended, in_output, full_a0, full_a1, query,
        key, value, lse, cos, sin, second_query, second_key, second_value, low_query, low_key, low_value,
    )


def after_attention(
    hidden, branches, branch_lows, select, second_output, gain, mlp_in
):
    tokens, width = hidden.shape
    rank = select.shape[1]
    tile = 128

    def kernel(h_ref, b0, b1, l0, l1, sel_ref, so_ref, gain_ref, in_ref, mid_out, ext_out, low_out):
        def one(t, _):
            r = pl.ds(pl.multiple_of(t * tile, tile), tile)
            sel = sel_ref[r, :]
            low = ((l0[r, :] + l1[r, :]) * sel).astype(BF)
            low_out[r, :] = low
            middle = h_ref[r, :].astype(F32) + (b0[r, :].astype(F32) + b1[r, :].astype(F32))
            middle += adapter_scale * jnp.dot(low, so_ref[...], preferred_element_type=F32)
            mid_out[r, :] = middle
            scale = lax.rsqrt(jnp.mean(middle * middle, axis=1, keepdims=True) + norm_eps)
            normed = (middle * scale * gain_ref[...]).astype(BF)
            ext_out[r, :width] = normed
            part = jnp.dot(normed, in_ref[...], preferred_element_type=F32)
            part = (part * jnp.concatenate([sel, sel], axis=1)).astype(BF)
            ext_out[r, width:] = part * jnp.array(adapter_scale, BF)
            return 0

        lax.fori_loop(0, tokens // tile, one, 0)

    return pl.pallas_call(
        kernel,
        out_shape=[
            jax.ShapeDtypeStruct((tokens, width), F32),
            jax.ShapeDtypeStruct((tokens, width + 2 * rank), BF),
            jax.ShapeDtypeStruct((tokens, rank), BF),
        ],
        in_specs=[VMEM] * 9,
        out_specs=[VMEM] * 3,
        compiler_params=pltpu.CompilerParams(vmem_limit_bytes=40 * 2**20),
        cost_estimate=pl.CostEstimate(
            flops=6 * tokens * width * rank, transcendentals=0, bytes_accessed=14 * tokens * width
        ),
    )(hidden, *branches, *branch_lows, select, second_output, gain, mlp_in)


def after_feed_forward(core, parts, middle, cotangent, select, gain, mlp_in):
    half, wide = parts[0].shape
    tokens, width = middle.shape
    rank = select.shape[1]
    tile = 128

    def kernel(
        core_ref, p0, p1, p2, mid_hbm, cot_hbm, sel_ref, gain_ref, in_ref, mid_out, branch_out, low_out,
        mid_s, cot_s, sems,
    ):
        start = pl.multiple_of(core_ref[0] * half, 16)
        copies = [
            pltpu.make_async_copy(mid_hbm.at[pl.ds(start, half)], mid_s, sems.at[0]),
            pltpu.make_async_copy(cot_hbm.at[pl.ds(start, half)], cot_s, sems.at[1]),
        ]
        for copy in copies:
            copy.start()
        for copy in copies:
            copy.wait()

        def one(t, _):
            r = pl.ds(pl.multiple_of(t * tile, tile), tile)
            sel = sel_ref[pl.ds(pl.multiple_of(start + t * tile, tile), tile), :]
            total = p0[r, :].astype(F32) + p1[r, :].astype(F32) + p2[r, :].astype(F32)
            low = (
                adapter_scale * total[:, width:] * jnp.concatenate([sel, sel], axis=1)
            ).astype(BF)
            low_out[r, :] = low
            grad = (total[:, :width] + nt(low, in_ref[...])) * gain_ref[...]
            middle = mid_s[r, :]
            scale = lax.rsqrt(jnp.mean(middle * middle, axis=1, keepdims=True) + norm_eps)
            inner = jnp.mean(middle * grad, axis=1, keepdims=True)
            out = cot_s[r, :].astype(F32) + scale * grad - middle * (scale * scale * scale * inner)
            mid_out[r, :] = out
            branch_out[r, :] = out.astype(BF)
            return 0

        lax.fori_loop(0, half // tile, one, 0)

    return pl.pallas_call(
        kernel,
        out_shape=[
            jax.ShapeDtypeStruct((half, width), F32),
            jax.ShapeDtypeStruct((half, width), BF),
            jax.ShapeDtypeStruct((half, 2 * rank), BF),
        ],
        in_specs=[SMEM] + [VMEM] * 3 + [HBM] * 2 + [VMEM] * 3,
        out_specs=[VMEM] * 3,
        scratch_shapes=[
            pltpu.VMEM((half, width), F32),
            pltpu.VMEM((half, width), BF),
            pltpu.SemaphoreType.DMA((2,)),
        ],
        compiler_params=pltpu.CompilerParams(vmem_limit_bytes=40 * 2**20),
        cost_estimate=pl.CostEstimate(
            flops=6 * half * width * rank, transcendentals=0, bytes_accessed=20 * half * width
        ),
    )(core, *parts, middle, cotangent, select, gain, mlp_in)


def feed_forward(places, core, normed, cot, new, old, totals, last):
    sums = totals != "none"
    first = totals is None
    before = list(totals) if sums and not first else []
    n_new, n_old = len(new), len(old)
    blocks = [list(unit[-1]) for unit in new + old]
    factors = [unit[-2] for unit in new + old]
    count, per = len(blocks), len(blocks[0])
    part_rows, wide = blocks[0][0].shape
    group, n_wide = normed[0].shape
    c_wide = cot[0].shape[1]
    rank = n_wide - c_wide
    width = c_wide - rank
    rows = 2 * group
    tile = group // 2
    tiles = rows // tile
    flat = [v for unit, factor in zip(blocks, factors) for v in unit + [factor]]
    old_flat = [v for unit in old for v in unit[:2]]
    n_sums = (4 if last else 2) if sums else 0

    def kernel(place_ref, core_ref, *refs):
        it = iter(refs)

        def take(n):
            return [next(it) for _ in range(n)]

        old_ref = take(2 * n_old)
        normed_hbm, cot_hbm = take(3), take(3)
        block_hbm = [take(per + 1) for _ in range(count)]
        before_hbm = take(len(before))
        sum_hbm = take(n_sums)
        act_ref, grad_ref, own_ref = (take(n_new) for _ in range(3))
        w_s, sem_w = take(2)
        if n_new:
            normed_s, cot_s, sem_x = take(3)
        if sums:
            acc_g, acc_o, sem_t, sem_out = take(4)
            fin_g, fin_o = (normed_s, cot_s) if last else (acc_g, acc_o)
        mine = core_ref[0]

        def fetch(k):
            slot = w_s.at[k % 2]
            return bring(block_hbm[k][:per], place_ref, slot, sem_w.at[k % 2]) + [
                pltpu.make_async_copy(
                    block_hbm[k][per], slot.at[pl.ds(width, 2 * rank)], sem_w.at[k % 2, places.shape[0]]
                )
            ]

        def load_x(t):
            copies = []
            for i, (src, dst) in enumerate(((normed_hbm, normed_s), (cot_hbm, cot_s))):
                if t < 2:
                    part, to = src[0].at[pl.ds(t * tile, tile)], t * tile
                else:
                    part = src[t - 1]
                    to = group + tile * (mine if t == 2 else 1 - mine)
                    to = pl.multiple_of(to, 16)
                copies.append(pltpu.make_async_copy(part, dst.at[pl.ds(to, tile)], sem_x.at[i, t]))
            return copies

        def load_t(t):
            r = pl.ds(t * tile, tile)
            return [
                pltpu.make_async_copy(src.at[r], dst.at[r], sem_t.at[i, t])
                for i, (src, dst) in enumerate(zip(before_hbm, (acc_g, acc_o)))
            ]

        def store_t(t, to):
            r = pl.ds(t * tile, tile)
            copies = []
            for i, src in enumerate((fin_g, fin_o)):
                dst = sum_hbm[2 * i + to].at[t // 2] if last else sum_hbm[i].at[r]
                copies.append(pltpu.make_async_copy(src.at[r], dst, sem_out.at[i, t]))
            return copies

        if n_new:
            for copy in load_x(0):
                copy.start()
        for copy in fetch(0):
            copy.start()
        if n_new:
            for copy in fetch(0):
                copy.wait()
            for t in range(1, tiles):
                for copy in load_x(t):
                    copy.start()
        if before:
            for t in range(tiles):
                for copy in load_t(t):
                    copy.start()
        for k in range(count):
            if k + 1 < count:
                for copy in fetch(k + 1):
                    copy.start()
            if k or not n_new:
                for copy in fetch(k):
                    copy.wait()
            slot = k % 2
            if k < n_new:
                act, grad = act_ref[k], grad_ref[k]
                for t in range(tiles):
                    r = pl.ds(t * tile, tile)
                    if k == 0 and t < 2:
                        for copy in load_x(t):
                            copy.wait()
                    if k == 0 and t == 2:
                        for copy in load_x(2) + load_x(3):
                            copy.wait()
                    x = normed_s[r, :]
                    gate = jnp.dot(x, w_s[slot, :, 0:WIDTH], preferred_element_type=F32)
                    up = jnp.dot(x, w_s[slot, :, WIDTH : 2 * WIDTH], preferred_element_type=F32)
                    back = jnp.dot(
                        cot_s[r, :],
                        w_s[slot, :c_wide, 2 * WIDTH : 3 * WIDTH],
                        preferred_element_type=F32,
                    )
                    sig = 1.0 / (1.0 + jnp.exp(-gate))
                    silu = gate * sig
                    act[r, :] = (silu * up).astype(BF)
                    grad[r, :WIDTH] = (back * up * (sig * (1.0 + gate * (1.0 - sig)))).astype(BF)
                    grad[r, WIDTH:] = (back * silu).astype(BF)
                low = normed_s[:, width:].T
                for part in range(2):
                    second = jnp.dot(
                        low[part * rank : (part + 1) * rank],
                        grad[:, part * WIDTH : (part + 1) * WIDTH],
                        preferred_element_type=F32,
                    ).astype(BF)
                    for at in range(0, WIDTH, rank):
                        to = part * WIDTH + at
                        own_ref[k][to : to + rank, :] = second[:, at : at + rank]
                own_ref[k][2 * WIDTH :, :] = jnp.dot(
                    act[...].T, cot_s[:, width:c_wide], preferred_element_type=F32
                ).astype(BF)
            else:
                act, grad = old_ref[2 * (k - n_new)], old_ref[2 * (k - n_new) + 1]
            if not sums:
                continue
            for t in range(tiles):
                r = pl.ds(t * tile, tile)
                if before and k == 0:
                    for copy in load_t(t):
                        copy.wait()
                for acc, fin, val, lo, hi, top in (
                    (acc_g, fin_g, grad, 0, 2 * WIDTH, n_wide),
                    (acc_o, fin_o, act, 2 * WIDTH, 3 * WIDTH, c_wide),
                ):
                    for at in range(0, top, 512):
                        n = slice(at, min(at + 512, top))
                        part = nt(val[r, :], w_s[slot, n, lo:hi])
                        if k or not first:
                            part = acc[r, n] + part
                        if k == count - 1:
                            fin[r, n] = part.astype(fin.dtype)
                        else:
                            acc[r, n] = part
                if k == count - 1 and last:
                    side = mine if t % 2 == 0 else 1 - mine
                    for to in range(2):

                        @pl.when(side == to)
                        def _():
                            for copy in store_t(t, to):
                                copy.start()

                elif k == count - 1:
                    for copy in store_t(t, 0):
                        copy.start()
        if sums:
            for t in range(tiles):
                for copy in store_t(t, 0):
                    copy.wait()

    scratch = [
        pltpu.VMEM((2, n_wide, wide), BF),
        pltpu.SemaphoreType.DMA((2, places.shape[0] + 1)),
    ]
    if n_new:
        scratch += [
            pltpu.VMEM((rows, n_wide), BF),
            pltpu.VMEM((rows, c_wide), BF),
            pltpu.SemaphoreType.DMA((2, tiles)),
        ]
    out_shape = []
    if sums:
        scratch += [
            pltpu.VMEM((rows, n_wide), F32),
            pltpu.VMEM((rows, c_wide), F32),
            pltpu.SemaphoreType.DMA((2, tiles)),
            pltpu.SemaphoreType.DMA((2, tiles)),
        ]
        for columns in (n_wide, c_wide):
            if last:
                out_shape += [jax.ShapeDtypeStruct((2, tile, columns), BF)] * 2
            else:
                out_shape += [jax.ShapeDtypeStruct((rows, columns), F32)]
    out_shape += [jax.ShapeDtypeStruct((rows, WIDTH), BF)] * n_new
    out_shape += [jax.ShapeDtypeStruct((rows, 2 * WIDTH), BF)] * n_new
    out_shape += [jax.ShapeDtypeStruct((3 * WIDTH, rank), BF)] * n_new
    n_hbm = 6 + len(flat)
    at = 2 + len(old_flat) + n_hbm
    out = pl.pallas_call(
        kernel,
        out_shape=out_shape,
        in_specs=[SMEM] * 2 + [VMEM] * len(old_flat) + [HBM] * (n_hbm + len(before)),
        out_specs=[HBM] * n_sums + [VMEM] * (3 * n_new),
        scratch_shapes=scratch,
        input_output_aliases={at: 0, at + 1: 1} if before and not last else {},
        compiler_params=pltpu.CompilerParams(vmem_limit_bytes=60 * 2**20),
        cost_estimate=pl.CostEstimate(
            flops=6 * (n_new + (count if sums else 0)) * rows * width * WIDTH,
            transcendentals=n_new * rows * WIDTH,
            bytes_accessed=4 * rows * width,
        ),
    )(places, core, *old_flat, *normed, *cot, *flat, *before)
    rest = out[n_sums:]
    return tuple(out[:n_sums]), list(zip(*(rest[i * n_new : (i + 1) * n_new] for i in range(3))))
def adapter_columns(ids_ref):
    sequences = ids_ref.shape[1]
    shape = (sequences * RANK, ADAPTER_COLS)
    row = lax.broadcasted_iota(jnp.int32, shape, 0)
    column = lax.broadcasted_iota(jnp.int32, shape, 1)
    start = jnp.zeros(shape, jnp.int32)
    for i in range(sequences):
        start = jnp.where(row // RANK == i, ids_ref[0, i] * RANK, start)
    return (column == start + row % RANK).astype(F32).astype(BF)


def pack(ids, factors, firsts):
    block = factors.shape[0] // BLOCKS
    sequences = ids.shape[1]
    lanes = BLOCKS * sequences * RANK

    def kernel(ids_ref, factor_ref, first_ref, factor_out, first_out, chosen_out):
        chosen = adapter_columns(ids_ref)
        chosen_out[...] = jnp.concatenate(
            [chosen[i * RANK : (i + 1) * RANK] for i in range(sequences)], axis=1
        )
        parts = [
            nt(factor_ref[i * block : (i + 1) * block, :], chosen) for i in range(BLOCKS)
        ]
        factor_out[...] = jnp.concatenate(parts, axis=1).astype(BF)
        parts = []
        for i in range(BLOCKS):
            q, s = i // 2, i % 2
            parts.append(
                nt(
                    first_ref[s * block : (s + 1) * block, q * ADAPTER_COLS : (q + 1) * ADAPTER_COLS],
                    chosen,
                )
            )
        first_out[...] = jnp.concatenate(parts, axis=1).astype(BF)

    return pl.pallas_call(
        kernel,
        out_shape=[jax.ShapeDtypeStruct((block, lanes), BF)] * 2
        + [jax.ShapeDtypeStruct((RANK, sequences * ADAPTER_COLS), BF)],
        in_specs=[SMEM, VMEM, VMEM],
        out_specs=[VMEM] * 3,
        compiler_params=pltpu.CompilerParams(vmem_limit_bytes=32 * 2**20),
        cost_estimate=pl.CostEstimate(flops=5_000_000_000, transcendentals=0, bytes_accessed=0),
    )(ids, factors, firsts)


def unpack(got):
    groups, share, lanes = got.shape
    share -= RANK
    each = lanes // BLOCKS
    sequences = each // RANK

    def kernel(got_ref, out_ref, total):
        total[...] = jnp.zeros_like(total)

        def one(g, _):
            packed = got_ref[g]
            chosen = jnp.concatenate(
                [
                    packed[share:, i * ADAPTER_COLS : (i + 1) * ADAPTER_COLS]
                    for i in range(sequences)
                ],
                axis=0,
            )
            for i in range(BLOCKS):
                total[i] += jnp.dot(
                    packed[:share, i * each : (i + 1) * each], chosen, preferred_element_type=F32
                )
            return 0

        lax.fori_loop(0, groups, one, 0)
        out_ref[...] = total[...].astype(BF)

    return pl.pallas_call(
        kernel,
        out_shape=jax.ShapeDtypeStruct((BLOCKS, share, ADAPTER_COLS), BF),
        in_specs=[VMEM],
        out_specs=VMEM,
        scratch_shapes=[pltpu.VMEM((BLOCKS, share, ADAPTER_COLS), F32)],
        compiler_params=pltpu.CompilerParams(vmem_limit_bytes=32 * 2**20),
        cost_estimate=pl.CostEstimate(flops=5_000_000_000, transcendentals=0, bytes_accessed=0),
    )(got)


def unit_results(at, parts, chunks):
    rows = parts[0].shape[0]
    units = chunks * WIDTH

    def kernel(at_ref, *refs):
        gate_out, up_out, down_out = refs[4:]
        for i in range(4):
            core = at_ref[0] if i < 2 else 1 - at_ref[0]
            bit = at_ref[1] if i % 2 == 0 else 1 - at_ref[1]
            start = pl.multiple_of((core * 2 + bit) * units, 128)
            for j in range(chunks):
                for at in range(0, WIDTH, ADAPTER_COLS):
                    to = pl.ds(pl.multiple_of(start + j * WIDTH + at, 128), ADAPTER_COLS)
                    row = j * 3 * WIDTH + at
                    gate_out[:, to] = refs[i][row : row + ADAPTER_COLS, :].astype(F32)
                    row += WIDTH
                    up_out[:, to] = refs[i][row : row + ADAPTER_COLS, :].astype(F32)
                row = (j * 3 + 2) * WIDTH
                to = pl.ds(pl.multiple_of(start + j * WIDTH, 128), WIDTH)
                down_out[to, :] = refs[i][row : row + WIDTH, :].astype(F32)

    return pl.pallas_call(
        kernel,
        out_shape=[
            jax.ShapeDtypeStruct((ADAPTER_COLS, 4 * units), F32),
            jax.ShapeDtypeStruct((ADAPTER_COLS, 4 * units), F32),
            jax.ShapeDtypeStruct((4 * units, ADAPTER_COLS), F32),
        ],
        in_specs=[SMEM] + [VMEM] * 4,
        out_specs=[VMEM] * 3,
        compiler_params=pltpu.CompilerParams(vmem_limit_bytes=48 * 2**20),
        cost_estimate=pl.CostEstimate(flops=8_000_000_000, transcendentals=0, bytes_accessed=0),
    )(at, *parts)


def other_results(at, parts, share, second_cols):
    ring, rows, cols = parts[0].shape
    chips = 4 * ring
    late_rows = BLOCKS * 2 * share
    pair_rows = (rows - late_rows) // 2
    block = chips * share
    half = 2 * block
    query_cols, key_cols = second_cols

    def kernel(at_ref, *refs):
        part_refs, outs = refs[:8], refs[8:19]
        query_s, pair_s, output_s, down_s = refs[19:]
        (
            in_q, second_q, in_k, second_k, in_v, second_v, in_o, second_o, in_g, in_u, second_d,
        ) = outs
        homes = (query_s, pair_s, output_s, in_o, None)
        for i in range(8):
            core = at_ref[0] if i < 4 else 1 - at_ref[0]
            bit_y = at_ref[1] if i // 2 % 2 == 0 else 1 - at_ref[1]
            bit_x = at_ref[2] if i % 2 == 0 else 1 - at_ref[2]

            def one(r, _):
                chip = lax.rem(at_ref[3] + ring - r, ring) * 4 + bit_y * 2 + bit_x
                found = part_refs[i][r].astype(F32)
                for b, (home, s) in enumerate(
                    ((query_s, 0), (query_s, 1), (pair_s, 0), (output_s, 0), (output_s, 1), (in_o, 0), (in_o, 1))
                ):
                    size = block if home is pair_s else half
                    to = pl.multiple_of(core * size + s * block + chip * share, 8)
                    home[pl.ds(to, share), :] = found[2 * b * share : (2 * b + 1) * share]
                for b in range(BLOCKS):
                    home, s = (in_q, in_k, in_v, down_s)[b // 2], b % 2
                    to = pl.multiple_of(core * half + s * block + chip * share, 8)
                    home[pl.ds(to, share), :] = found[(2 * b + 1) * share : (2 * b + 2) * share]
                for k, home in enumerate((in_g, in_u)):
                    to = pl.multiple_of(core * half + chip * pair_rows, 8)
                    start = late_rows + k * pair_rows
                    home[pl.ds(to, pair_rows), :] = found[start : start + pair_rows]
                return 0

            lax.fori_loop(0, ring, one, 0)
        second_q[...] = query_s[...].T
        second_o[...] = output_s[...].T
        second_d[...] = down_s[...].T
        both = pair_s[...].T
        for out, start in ((second_k, 0), (second_v, key_cols)):
            out[...] = jnp.concatenate(
                [both[:, c * block + start : c * block + start + key_cols] for c in range(2)], axis=1
            )

    width = 2 * half

    def shape(*dims):
        return jax.ShapeDtypeStruct(dims, F32)

    return pl.pallas_call(
        kernel,
        out_shape=[
            shape(width, cols), shape(cols, 2 * query_cols), shape(width, cols),
            shape(cols, 2 * key_cols), shape(width, cols), shape(cols, 2 * key_cols),
            shape(width, cols), shape(cols, width), shape(width, cols), shape(width, cols),
            shape(cols, width),
        ],
        in_specs=[SMEM] + [VMEM] * 8,
        out_specs=[VMEM] * 11,
        scratch_shapes=[
            pltpu.VMEM((width, cols), F32),
            pltpu.VMEM((half, cols), F32),
            pltpu.VMEM((width, cols), F32),
            pltpu.VMEM((width, cols), F32),
        ],
        compiler_params=pltpu.CompilerParams(vmem_limit_bytes=48 * 2**20),
        cost_estimate=pl.CostEstimate(flops=8_000_000_000, transcendentals=0, bytes_accessed=0),
    )(at, *parts)


DP = ("ring", "second", "first")


def make_body(n):
    ring_size = n // 4
    perms = ring_and_swaps(n)

    def move(value, link):
        return lax.ppermute(value, DP, perms[link])

    def other_core(value):
        return lax.ppermute(value, "tensor", [(0, 1), (1, 0)])

    def take(value, start, size, axis=0):
        return lax.dynamic_slice_in_dim(value, start, size, axis)

    def body(
        hidden_in, adapter_ids, attn_gain, mlp_gain, w_query, w_key, w_value, w_output, w_gate,
        w_up, w_down, in_query, second_query, in_key, second_key, in_value, second_value,
        in_output, second_output, in_gate, second_gate, in_up, second_up, in_down, second_down,
        cotangent,
    ):
        num_rows, width = hidden_in.shape
        half_rows = num_rows // 2
        half_width = width // 2
        rank_cols = in_query.shape[1]
        units = w_gate.shape[1] // 2
        chunks = units // WIDTH
        shard = w_query.shape[0]

        ring_at, bit_y, bit_x = (lax.axis_index(name) for name in DP)
        core = lax.axis_index("tensor")
        core_at = core.astype(jnp.int32).reshape(1)
        bits = {"x": bit_x, "y": bit_y}

        def in_order(bit, value, received, axis=0):
            first = jnp.where(bit == 0, value, received)
            return jnp.concatenate([first, jnp.where(bit == 0, received, value)], axis=axis)

        def half_of(value):
            return take(value, core * half_rows, half_rows)

        def both_halves(value):
            return in_order(core, value, other_core(value))

        def cols_of_core(value):
            return take(value, core * half_width, half_width, 1)

        row_index = lax.iota(jnp.int32, num_rows)
        is_later = row_index >= PROMPT
        seq_of = jnp.where(is_later, 1 + (row_index - PROMPT) // CONT_LEN, 0)
        position = jnp.where(is_later, PROMPT + (row_index - PROMPT) % CONT_LEN, row_index)
        seq_ids = lax.iota(jnp.int32, adapter_ids.shape[1])
        row_adapter = jnp.sum(
            jnp.where(seq_of[:, None] == seq_ids[None, :], adapter_ids[0][None, :], 0), axis=1
        )
        select = (lax.iota(jnp.int32, rank_cols)[None, :] // RANK == row_adapter[:, None]).astype(F32)
        select_three = jnp.concatenate([select] * 3, axis=1)
        inv_freq = rope_base ** (-2.0 * lax.iota(F32, HEAD_DIM // 2) / HEAD_DIM)
        angles = inv_freq[:, None] * position.astype(F32)[None, :]
        cos_table, sin_table = jnp.cos(angles), jnp.sin(angles)
        attn_in = jnp.concatenate([in_query, in_key, in_value], axis=1)
        mlp_in = jnp.concatenate([in_gate, in_up], axis=1)
        attn_gain_f = attn_gain.astype(F32)
        mlp_gain_f = mlp_gain.astype(F32).reshape(1, width)
        two = jnp.array(adapter_scale, BF)

        unit_start = bit_x * units

        def half_units(start):
            return (
                take(w_gate, start, units, 1),
                take(w_up, start, units, 1),
                take(w_down, start, units, 0).T,
            )

        mine, others = half_units(unit_start), half_units(units - unit_start)

        def chunk_of(parts, j):
            return jnp.concatenate([p[:, j * WIDTH : (j + 1) * WIDTH] for p in parts], axis=1)

        factor_parts = (
            take(second_gate, unit_start, units, 1),
            take(second_up, unit_start, units, 1),
            take(in_down, unit_start, units, 0),
        )
        blank = jnp.zeros((rank_cols, WIDTH), BF)
        chunk_cols = 3 * WIDTH

        def factors_of(j):
            cols = slice(j * WIDTH, (j + 1) * WIDTH)
            gate, up, down = factor_parts
            upper = jnp.concatenate([gate[:, cols], blank, down[cols].T], axis=1)
            return jnp.concatenate(
                [upper, jnp.concatenate([blank, up[:, cols], blank], axis=1)], axis=0
            )

        grad_low_down = (
            adapter_scale * product_with_transpose(cotangent, second_down) * select
        ).astype(BF)
        cot_wide = jnp.concatenate([cotangent, grad_low_down], axis=1)

        held = {
            "A0.o": jnp.concatenate([w_query, w_key], axis=1),
            "A1.p0": jnp.concatenate([w_output.T, w_value], axis=1),
            "C.o": half_of(cot_wide),
        }
        groups = exchanges_of(chunks)
        for i, group in enumerate(groups):
            held[f"E{i}.o"] = jnp.concatenate([chunk_of(others, j) for j in group], axis=1)
        plan = plan_transfers(ring_size, chunks)
        steps, arrivals = schedule(plan, chunks)
        when = {name: s for s, names in arrivals.items() for name in names}
        last_step = len(steps) - 1

        def there(tag):
            return max(s for name, s in when.items() if name.split(".")[0] == tag)

        def pieces(tag):
            found, places = [], []
            for r in range(ring_size):
                ring = (ring_at - r + ring_size) % ring_size
                if tag[0] == "A":
                    for other in range(2):
                        found.append(held[f"{tag}.{'x' if other else 'b'}{r}"])
                        bit = 1 - bit_x if other else bit_x
                        places += [(ring * 2 + bit_y) * 2 + bit, (ring * 2 + 1 - bit_y) * 2 + bit]
                else:
                    for other in range(2):
                        name = f"{tag}.q{r}" if other else f"{tag}.p{r}" if r else tag
                        found.append(held[name])
                        pair = ring * 2 + (1 - bit_y if other else bit_y)
                        places += [pair * 2 + bit_x, pair * 2 + 1 - bit_x]
            places = jnp.stack(places).astype(jnp.int32)
            if shard % 16:
                whole = jnp.zeros((n, shard, found[0].shape[1]), BF)
                for i in range(n):
                    part = found[i // 2][(i % 2) * shard : (i % 2 + 1) * shard]
                    whole = lax.dynamic_update_slice(whole, part[None], (places[i], 0, 0))
                return [whole.reshape(n * shard, -1)], jnp.zeros((1,), jnp.int32)
            return found, places

        v = {}
        hidden_wide = hidden_in.astype(F32)
        normed_a = rms_norm(hidden_wide, attn_gain_f).astype(BF)
        low_attn = (matrix_product(normed_a, attn_in) * select_three).astype(BF)
        lows = [low_attn[:, i * rank_cols : (i + 1) * rank_cols] * two for i in range(3)]

        def start_attention():
            found, places = pieces("A0")
            v["query"], v["key"], v["a0"] = queries_and_keys(
                places, found, normed_a, lows[0], lows[1], second_query, second_key, cos_table,
                sin_table,
            )
            return [v["key"]]

        def finish_attention():
            found, places = pieces("A1")
            v["value"], v["attended"], v["lse"], branch, branch_low, v["a1"] = attention(
                places, found, normed_a, lows[2], second_value, v["query"], v["key"], in_output
            )
            v["branches"] = (branch, other_core(branch))
            v["branch_lows"] = (branch_low, other_core(branch_low))
            return [v["value"]]

        def start_feed_forward():
            v["middle"], v["normed"], v["low_output"] = after_attention(
                hidden_in, v["branches"], v["branch_lows"], select, second_output, mlp_gain_f, mlp_in
            )
            held["N.o"] = half_of(v["normed"])
            return [v["low_output"]]

        def meet_neighbour():
            v["normed_all"] = (v["normed"], held["N.x"], other_core(held["N.x"]))
            v["cot_all"] = (cot_wide, held["C.x"], other_core(held["C.x"]))
            return [v["normed_all"][2], v["cot_all"][2]]

        unit_out = {}

        def feed(new, old, totals, last):
            found = {j: pieces(f"M{j}") for j in new + old}
            sums, results = feed_forward(
                found[(new + old)[0]][1],
                core_at,
                v["normed_all"],
                v["cot_all"],
                [(factors_of(j), found[j][0]) for j in new],
                [unit_out[j][:2] + (factors_of(j), found[j][0]) for j in old],
                totals,
                last,
            )
            unit_out.update(zip(new, results))
            return sums

        def units_only(new):
            def run():
                feed(new, [], "none", False)
                return [unit_out[new[-1]][0]]

            return run

        order = sorted(range(chunks), key=lambda j: there(f"M{j}"))
        events = {}

        def at_step(s, run):
            events.setdefault(min(s, last_step), []).append(run)

        at_step(there("A0"), start_attention)
        at_step(there("A1"), finish_attention)
        at_step(there("A1") + NORMED_AFTER - 1, start_feed_forward)
        begin = there("N")
        at_step(begin, meet_neighbour)
        early, later, final = order[: chunks - 3], order[chunks - 3 : chunks - 1], order[-1]
        at = begin
        for i in range(0, len(early), 2):
            pair = early[i : i + 2]
            at = max([at] + [there(f"M{j}") for j in pair])
            at_step(at, units_only(pair))
            at += 1
        for j in later:
            at_step(max(at, there(f"M{j}")), units_only([j]))

        waits = []
        for s, step in enumerate(steps):
            sources = sorted({plan[name][1] for name in step})
            if s:
                arrived = [name for name in arrivals.get(s, []) if name not in sources]
                if sources and arrived + waits:
                    tied = tie([held[k] for k in sources], [held[k] for k in arrived] + waits)
                    held.update(zip(sources, tied))
                    waits = []
            for name in step:
                held[name] = move(held[plan[name][1]], plan[name][0])
            for name in arrivals.get(s + 1, []):
                if name.endswith(".e"):
                    for i, j in enumerate(groups[int(name[1:-2])]):
                        got = held[name][:, i * chunk_cols : (i + 1) * chunk_cols]
                        held[f"M{j}"] = jnp.concatenate([chunk_of(mine, j), got], axis=0)
                elif name == "A0.y":
                    held["A0.b0"] = jnp.concatenate([held["A0.o"], held[name]], axis=0)
                elif name.startswith("A1") and name[3] in "pq":
                    pair = [f"A1.{side}{name[4:]}" for side in "pq"]
                    if f"A1.b{name[4:]}" not in held and all(p in held for p in pair):
                        if max(when.get(p, 0) for p in pair) <= s + 1:
                            held[f"A1.b{name[4:]}"] = jnp.concatenate([held[p] for p in pair], axis=0)
            for run in events.get(s, []):
                waits += run()

        totals = feed([final], early + later, None, True)
        grad_keep, grad_send, out_keep, out_send = totals

        def after(values, *others):
            return tie(list(values), list(others), 0)

        def total(parts):
            return jnp.sum(parts.astype(F32), axis=0).astype(BF)

        grad_got = other_core(grad_send)
        grad_out = (grad_keep[1].astype(F32) + grad_got[1].astype(F32)).astype(BF)
        grad_in_parts = (grad_keep[0], grad_got[0], move(grad_out, "x"))
        out_send, *own = after([out_send] + [unit_out[j][2] for j in range(chunks)], grad_out)
        out_got = other_core(out_send)
        out_out = (out_keep[1].astype(F32) + out_got[1].astype(F32)).astype(BF)
        units_all = lax.psum(jnp.concatenate(own, axis=0), DP[:2])

        grad_middle, grad_branch, grad_low_mlp = after_feed_forward(
            core_at, grad_in_parts, v["middle"], cotangent, select, mlp_gain_f, mlp_in
        )
        out_in = move(after([out_out], grad_branch)[0], "x")
        grad_branch_other = other_core(grad_branch)
        grad_low_mlp = both_halves(grad_low_mlp)
        delta_mlp = transpose_then_product(
            cols_of_core(v["normed"][:, :width]), grad_low_mlp
        ).astype(BF)
        got_mlp = lax.all_to_all(delta_mlp.reshape(n, half_width // n, 2 * rank_cols), DP, 0, 0)

        back, back_low, factors = attention_back(
            core_at, (grad_branch, grad_branch_other), select, second_output, v["low_output"],
            v["attended"], in_output, v["a0"], v["a1"], v["query"], v["key"], v["value"], v["lse"],
            cos_table, sin_table, second_query, second_key, second_value, *lows,
        )
        back_low, out_in = after([back_low, out_in])
        back_low = back_low + other_core(back_low)
        grad_low_attn = (back_low * select_three).astype(BF)
        out_sum = out_keep[0].astype(F32) + out_got[0].astype(F32) + out_in.astype(F32)
        low_down = (out_sum[:, width:] * half_of(select)).astype(BF)
        firsts = jnp.concatenate(
            [
                transpose_then_product(cols_of_core(normed_a), grad_low_attn).astype(BF),
                (
                    adapter_scale
                    * transpose_then_product(cols_of_core(cotangent), both_halves(low_down))
                ).astype(BF),
            ],
            axis=1,
        )
        *packed, chosen = pack(adapter_ids, factors, firsts)
        share = packed[0].shape[0] // n
        packed = jnp.concatenate(
            [part.reshape(n, share, part.shape[1]) for part in packed]
            + [jnp.broadcast_to(chosen[None], (n,) + chosen.shape)],
            axis=1,
        )
        got_late = lax.all_to_all(packed, DP, 0, 0)
        units_all, got_mlp, back, out_sum, grad_middle = after(
            [units_all, got_mlp, back, out_sum, grad_middle], packed
        )

        pair = (units_all, move(units_all, "x"))
        gradient_second_gate, gradient_second_up, delta_in_down = unit_results(
            jnp.stack([core, bit_x]).astype(jnp.int32),
            pair + tuple(other_core(part) for part in pair),
            chunks,
        )

        layer_output = both_halves(
            (
                half_of(v["middle"])
                + out_sum[:, :width]
                + adapter_scale * matrix_product(low_down, second_down)
            ).astype(BF)
        )
        back_half = half_of(back).astype(F32) + other_core(
            take(back, (1 - core) * half_rows, half_rows)
        ).astype(F32)
        grad_normed_a = back_half + product_with_transpose(half_of(grad_low_attn), attn_in)
        grad_in = both_halves(
            (grad_middle + rms_back(half_of(hidden_wide), attn_gain_f, grad_normed_a)).astype(BF)
        )

        sums_mlp = total(got_mlp)
        sums = jnp.concatenate(
            [unpack(got_late).reshape(-1, rank_cols), sums_mlp[:, :rank_cols], sums_mlp[:, rank_cols:]],
            axis=0,
        )
        sums = jnp.stack([sums] + [move(sums, f"z{r}") for r in range(1, ring_size)], axis=0)
        parts = [sums] + [move(sums, link) for link in ("x", "y", "xy")]
        parts += [other_core(part) for part in parts]
        others = other_results(
            jnp.stack([core, bit_y, bit_x, ring_at]).astype(jnp.int32),
            parts,
            share,
            (second_query.shape[1], second_key.shape[1]),
        )
        return (
            layer_output,
            grad_in,
            *others[:9],
            gradient_second_gate,
            others[9],
            gradient_second_up,
            delta_in_down,
            others[10],
        )

    return body


def solution(mesh):
    n, tensor = mesh.shape["dp"], mesh.shape["tensor"]
    split = jax.sharding.Mesh(mesh.devices.reshape(n // 4, 2, 2, tensor), DP + ("tensor",))
    return jax.shard_map(
        make_body(n),
        mesh=split,
        in_specs=(
            P(DP, None), P(DP, None), P(), P(), P(DP, "tensor"), P(DP, "tensor"), P(DP, "tensor"),
            P("tensor", DP), P(DP, "tensor"), P(DP, "tensor"), P("tensor", DP), P(),
            P(None, "tensor"), P(), P(None, "tensor"), P(), P(None, "tensor"), P("tensor", None),
            P(), P(), P(None, "tensor"), P(), P(None, "tensor"), P("tensor", None), P(), P(DP, None),
        ),
        out_specs=(P(DP, None), P(DP, None)) + (P(),) * 14,
        check_vma=False,
    )
```

```python
import math

import jax
import jax.numpy as jnp
from jax import lax
from jax.experimental import pallas as pl
from jax.experimental.pallas import tpu as pltpu
from jax.sharding import PartitionSpec as P

HEAD_DIM = 80
RANK = 16
PROMPT = 256
CONT_LEN = 128
WIDTH = 256
ADAPTER_COLS = 128
BLOCKS = 8

adapter_scale = 2.0
norm_eps = 1e-05
rope_base = 1000000.0

BF = jnp.bfloat16
F32 = jnp.float32

LAG = 2
STEP_FLOPS = 20_000_000_000
NORMED_AFTER = 4
EXCHANGES = ((0, 1), (2, 3), (4, 5, 6))
EXCHANGE_PRIORITY = (-40, -39, 8)
ATTN_PRIORITY = (-20, -10)
YZ_CHUNKS = ()
LAST_WIDE = 30


def matrix_product(left, right):
    return jnp.dot(left, right, preferred_element_type=F32)


def product_with_transpose(left, right):
    return lax.dot_general(left, right, (((1,), (1,)), ((), ())), preferred_element_type=F32)


def transpose_then_product(left, right):
    return lax.dot_general(left, right, (((0,), (0,)), ((), ())), preferred_element_type=F32)


def rms_norm(values, gain_vec):
    return (
        values * lax.rsqrt(jnp.mean(values * values, axis=-1, keepdims=True) + norm_eps) * gain_vec
    )


def rms_back(values, gain_vec, grad):
    scale = lax.rsqrt(jnp.mean(values * values, axis=-1, keepdims=True) + norm_eps)
    e = gain_vec * grad
    return scale * e - values * (scale * scale * scale) * jnp.mean(values * e, axis=-1, keepdims=True)


def ring_and_swaps(n):
    perms = {
        "y": [(i, i ^ 2) for i in range(n)],
        "x": [(i, i ^ 1) for i in range(n)],
        "xy": [(i, i ^ 3) for i in range(n)],
    }
    for r in range(1, n // 4):
        perms[f"z{r}"] = [(i, (i + 4 * r) % n) for i in range(n)]
    perms["z"] = perms["z1"]
    return perms


def plan_transfers(ring_size, chunks):
    plan = {}
    first, second = ATTN_PRIORITY
    plan["A0.y"] = ("y", "A0.o", first, 1)
    for r in range(ring_size):
        if r:
            plan[f"A0.b{r}"] = ("z", f"A0.b{r - 1}", first + 0.01 * r, 2)
            plan[f"A1.p{r}"] = ("z", f"A1.p{r - 1}", second + 0.01 * r, 1)
        plan[f"A1.q{r}"] = ("y", f"A1.p{r}", second + 0.01 * r, 1)
        plan[f"A0.x{r}"] = ("x", f"A0.b{r}", first + 0.01 * r, 2)
        plan[f"A1.x{r}"] = ("x", f"A1.b{r}", second + 0.01 * r, 2)
    for i, group in enumerate(exchanges_of(chunks)):
        plan[f"E{i}.e"] = ("x", f"E{i}.o", EXCHANGE_PRIORITY[min(i, 2)], (len(group) + 1) // 2)
    for j in range(chunks):
        tag = f"M{j}"
        for r in range(ring_size):
            source = (f"{tag}.p{r}" if r else tag)
            if r:
                before = f"{tag}.p{r - 1}" if r > 1 else tag
                plan[f"{tag}.p{r}"] = ("z", before, j + 0.01 * r, 1)
            plan[f"{tag}.q{r}"] = ("y", source, j + 0.01 * r, 1)
    plan["C.x"] = ("x", "C.o", LAST_WIDE, 3)
    plan["N.x"] = ("x", "N.o", -50, 3)
    return plan


def exchanges_of(chunks):
    return EXCHANGES[:2] + (tuple(range(4, chunks)),)


def schedule(plan, chunks):
    makes = {"A0.y": ["A0.b0"]}
    for i, group in enumerate(exchanges_of(chunks)):
        makes[f"E{i}.e"] = [f"M{j}" for j in group]
    ready, busy, arrivals = {}, {}, {}
    for _, source, _, _ in plan.values():
        if source.endswith(".o") and source != "N.o":
            ready[source] = 0
    ready["A1.p0"] = 0
    steps, waiting, now = [], dict(plan), 0
    while waiting:
        step = []
        if "N.o" not in ready and not any(name.startswith("A1") for name in waiting):
            ready["N.o"] = max(s for s, names in arrivals.items() if "A1.x" in str(names))
            ready["N.o"] += NORMED_AFTER
        for link in "xyz":
            able = [
                (entry[2], name)
                for name, entry in waiting.items()
                if entry[0] == link
                and busy.get(link, 0) <= now
                and ready.get(entry[1], 1 << 30) <= now
            ]
            if able:
                name = min(able)[1]
                length = waiting.pop(name)[3]
                step.append(name)
                busy[link] = now + length
                ready[name] = now + (LAG if length == 1 else length)
                arrivals.setdefault(ready[name], []).append(name)
                for made in makes.get(name, []):
                    ready[made] = ready[name]
                if name.startswith("A1") and name[3] in "pq":
                    pair = (f"A1.p{name[4:]}", f"A1.q{name[4:]}")
                    if pair[0] in ready and pair[1] in ready:
                        ready[f"A1.b{name[4:]}"] = max(ready[p] for p in pair)
        steps.append(step)
        now += 1
    return steps, arrivals


def tie(values, others, flops=STEP_FLOPS):
    def kernel(*refs):
        pass

    spec = pl.BlockSpec(memory_space=pltpu.HBM)
    n = len(values)
    return pl.pallas_call(
        kernel,
        out_shape=[jax.ShapeDtypeStruct(v.shape, v.dtype) for v in values],
        in_specs=[spec] * (n + len(others)),
        out_specs=[spec] * n,
        input_output_aliases={i: i for i in range(n)},
        cost_estimate=pl.CostEstimate(flops=flops, transcendentals=0, bytes_accessed=0),
    )(*values, *others)


def bring(blocks, place_ref, target, sems):
    total = sum(block.shape[0] for block in blocks)
    rows = total // place_ref.shape[0]
    copies = []
    for block in blocks:
        for start in range(0, block.shape[0], rows):
            i = len(copies)
            to = pl.multiple_of(place_ref[i] * rows, math.gcd(rows, 16))
            copies.append(
                pltpu.make_async_copy(
                    block.at[pl.ds(start, rows)], target.at[pl.ds(to, rows)], sems.at[i]
                )
            )
    return copies


HBM = pl.BlockSpec(memory_space=pl.ANY)
VMEM = pl.BlockSpec(memory_space=pltpu.VMEM)
SMEM = pl.BlockSpec(memory_space=pltpu.SMEM)


def nt(left, right):
    return lax.dot_general(left, right, (((1,), (1,)), ((), ())), preferred_element_type=F32)


def turn(upright, cos_ref, sin_ref, sign, row):
    half = HEAD_DIM // 2
    first, second = upright[row : row + half], upright[row + half : row + 2 * half]
    cos, sin = cos_ref[...], sin_ref[...] * sign
    return jnp.concatenate([first * cos - second * sin, second * cos + first * sin], axis=0)


def queries_and_keys(places, blocks, normed, low_query, low_key, second_query, second_key, cos, sin):
    count = len(blocks)
    tokens, width = normed.shape
    cols = blocks[0].shape[1]
    q_cols, k_cols = second_query.shape[1], second_key.shape[1]

    def kernel(place_ref, x_ref, lq_ref, lk_ref, sq_ref, sk_ref, cos_ref, sin_ref, *refs):
        parts, (q_out, k_out, w_out, w_s, sems, sem_out) = refs[:count], refs[count:]
        copies = bring(parts, place_ref, w_s, sems)
        for copy in copies:
            copy.start()
        for copy in copies:
            copy.wait()
        keep = pltpu.make_async_copy(w_s, w_out, sem_out)
        keep.start()
        x = x_ref[...]
        step = 4 * HEAD_DIM
        for start, low, second, out, shift in [
            (at, lq_ref, sq_ref, q_out, 0) for at in range(0, q_cols, step)
        ] + [(q_cols + at, lk_ref, sk_ref, k_out, q_cols) for at in range(0, k_cols, step)]:
            own = start - shift
            part = jnp.dot(x, w_s[:, start : start + step], preferred_element_type=F32)
            part += jnp.dot(low[...], second[:, own : own + step], preferred_element_type=F32)
            upright = part.T
            for row in range(0, step, HEAD_DIM):
                out[own + row : own + row + HEAD_DIM, :] = turn(
                    upright, cos_ref, sin_ref, 1.0, row
                ).astype(BF)
        keep.wait()

    return pl.pallas_call(
        kernel,
        out_shape=[
            jax.ShapeDtypeStruct((q_cols, tokens), BF),
            jax.ShapeDtypeStruct((k_cols, tokens), BF),
            jax.ShapeDtypeStruct((width, cols), BF),
        ],
        in_specs=[SMEM] + [VMEM] * 7 + [HBM] * count,
        out_specs=[VMEM, VMEM, HBM],
        scratch_shapes=[
            pltpu.VMEM((width, cols), BF),
            pltpu.SemaphoreType.DMA((places.shape[0],)),
            pltpu.SemaphoreType.DMA,
        ],
        compiler_params=pltpu.CompilerParams(vmem_limit_bytes=48 * 2**20),
        cost_estimate=pl.CostEstimate(
            flops=2 * tokens * width * cols, transcendentals=0, bytes_accessed=4 * width * cols
        ),
    )(places, normed, low_query, low_key, second_query, second_key, cos, sin, *blocks)


def seen(rows, columns, row_start, column_start):
    key = lax.broadcasted_iota(jnp.int32, (rows, columns), 0)
    query = lax.broadcasted_iota(jnp.int32, (rows, columns), 1)
    causal = key <= query
    if row_start >= PROMPT:
        causal = causal & (key // CONT_LEN == query // CONT_LEN)
    return causal


def attention(places, blocks, normed, low_value, second_value, query, key, in_output):
    count = len(blocks)
    tokens, width = normed.shape
    cols = blocks[0].shape[1]
    q_cols, k_cols = query.shape[0], key.shape[0]
    kv_heads = k_cols // HEAD_DIM
    group = q_cols // k_cols
    scale = 1.0 / math.sqrt(HEAD_DIM)

    def kernel(place_ref, x_ref, lv_ref, sv_ref, q_ref, k_ref, io_ref, *refs):
        parts = refs[:count]
        v_out, att_out, lse_out, branch_out, low_out, w_out, w_s, att_s, sems, sem_out = refs[count:]
        copies = bring(parts, place_ref, w_s, sems)
        for copy in copies:
            copy.start()
        for copy in copies:
            copy.wait()
        keep = pltpu.make_async_copy(w_s, w_out, sem_out)
        keep.start()
        value = jnp.dot(x_ref[...], w_s[:, q_cols:cols], preferred_element_type=F32)
        value += jnp.dot(lv_ref[...], sv_ref[...], preferred_element_type=F32)
        v_out[...] = value.T.astype(BF)
        seen_first = seen(PROMPT, PROMPT, 0, 0)
        seen_second = seen(tokens - PROMPT, tokens - PROMPT, PROMPT, PROMPT)

        def one_head(g, _):
            k_rows = pl.ds(pl.multiple_of(g * HEAD_DIM, 16), HEAD_DIM)
            keys = k_ref[k_rows, :].T
            values = v_out[k_rows, :]
            for h in range(group):
                rows = pl.ds(pl.multiple_of((g * group + h) * HEAD_DIM, 16), HEAD_DIM)
                head = q_ref[rows, :]
                early = jnp.dot(keys[:PROMPT], head[:, :PROMPT], preferred_element_type=F32)
                late = jnp.dot(keys, head[:, PROMPT:], preferred_element_type=F32)
                early = jnp.where(seen_first, early * scale, -1e30)
                late_prompt = late[:PROMPT] * scale
                late_own = jnp.where(seen_second, late[PROMPT:] * scale, -1e30)
                top = jnp.max(early, axis=0, keepdims=True)
                expo = jnp.exp(early - top)
                total = jnp.sum(expo, axis=0, keepdims=True)
                prob = (expo * (1.0 / total)).astype(BF)
                lse_out[g, h : h + 1, :PROMPT] = top + jnp.log(total)
                att_s[rows, :PROMPT] = jnp.dot(
                    values[:, :PROMPT], prob, preferred_element_type=F32
                ).astype(BF)
                top = jnp.maximum(
                    jnp.max(late_prompt, axis=0, keepdims=True),
                    jnp.max(late_own, axis=0, keepdims=True),
                )
                expo_p, expo_o = jnp.exp(late_prompt - top), jnp.exp(late_own - top)
                total = jnp.sum(expo_p, axis=0, keepdims=True) + jnp.sum(
                    expo_o, axis=0, keepdims=True
                )
                inverse = 1.0 / total
                prob = jnp.concatenate(
                    [(expo_p * inverse).astype(BF), (expo_o * inverse).astype(BF)], axis=0
                )
                lse_out[g, h : h + 1, PROMPT:] = top + jnp.log(total)
                att_s[rows, PROMPT:] = jnp.dot(
                    values, prob, preferred_element_type=F32
                ).astype(BF)
            return 0

        lax.fori_loop(0, kv_heads, one_head, 0)
        att_out[...] = att_s[...].T
        attended = att_out[...]
        low_out[...] = jnp.dot(attended, io_ref[...], preferred_element_type=F32)
        for at in range(0, width, 512):
            branch_out[:, at : at + 512] = nt(attended, w_s[at : at + 512, :q_cols]).astype(BF)
        keep.wait()

    return pl.pallas_call(
        kernel,
        out_shape=[
            jax.ShapeDtypeStruct((k_cols, tokens), BF),
            jax.ShapeDtypeStruct((tokens, q_cols), BF),
            jax.ShapeDtypeStruct((kv_heads, group, tokens), F32),
            jax.ShapeDtypeStruct((tokens, width), BF),
            jax.ShapeDtypeStruct((tokens, in_output.shape[1]), F32),
            jax.ShapeDtypeStruct((width, cols), BF),
        ],
        in_specs=[SMEM] + [VMEM] * 6 + [HBM] * count,
        out_specs=[VMEM] * 5 + [HBM],
        scratch_shapes=[
            pltpu.VMEM((width, cols), BF),
            pltpu.VMEM((q_cols, tokens), BF),
            pltpu.SemaphoreType.DMA((places.shape[0],)),
            pltpu.SemaphoreType.DMA,
        ],
        compiler_params=pltpu.CompilerParams(vmem_limit_bytes=48 * 2**20),
        cost_estimate=pl.CostEstimate(
            flops=4 * tokens * width * cols, transcendentals=0, bytes_accessed=4 * width * cols
        ),
    )(places, normed, low_value, second_value, query, key, in_output, *blocks)


def attention_back(
    core, halves, select, second_output, low_output, attended, in_output, full_a0, full_a1, query,
    key, value, lse, cos, sin, second_query, second_key, second_value, low_query, low_key, low_value,
):
    half_tokens, width = halves[0].shape
    tokens = 2 * half_tokens
    cols = full_a0.shape[1]
    q_cols, k_cols = query.shape[0], key.shape[0]
    rank = second_query.shape[0]
    kv_heads = k_cols // HEAD_DIM
    group = q_cols // k_cols
    scale = 1.0 / math.sqrt(HEAD_DIM)

    def kernel(
        core_ref, mine_hbm, other_hbm, sel_ref, so_ref, lo_ref, att_ref, io_ref, a0_hbm, a1_hbm, q_ref, k_ref, v_ref, lse_ref, cos_ref, sin_ref,
        sq_ref, sk_ref, sv_ref, lq_ref, lk_ref, lv_ref, back_out, low_out, factor_out, a0, a1, gb_ref, glo_ref, ga_s, g_s, gw_s, sems,
    ):
        mine = core_ref[0]
        copies = [
            pltpu.make_async_copy(a1_hbm, a1, sems.at[0]),
            pltpu.make_async_copy(a0_hbm, a0, sems.at[1]),
            pltpu.make_async_copy(
                mine_hbm, gb_ref.at[pl.ds(pl.multiple_of(mine * half_tokens, 16), half_tokens)], sems.at[2]
            ),
            pltpu.make_async_copy(
                other_hbm,
                gb_ref.at[pl.ds(pl.multiple_of((1 - mine) * half_tokens, 16), half_tokens)],
                sems.at[3],
            ),
        ]
        for i in (2, 3, 0, 1):
            copies[i].start()
        for i in (2, 3):
            copies[i].wait()
        glo_ref[...] = (adapter_scale * nt(gb_ref[...], so_ref[...]) * sel_ref[...]).astype(BF)
        at_second = q_cols + 2 * k_cols
        at_first = at_second + width // 2
        factor_out[at_first : at_first + q_cols, :] = jnp.dot(
            att_ref[...].T, glo_ref[...], preferred_element_type=F32
        ).astype(BF)
        own = gb_ref[:, pl.ds(pl.multiple_of(mine * (width // 2), 128), width // 2)]
        factor_out[at_second:at_first, :] = (
            adapter_scale * jnp.dot(own.T, lo_ref[...], preferred_element_type=F32)
        ).astype(BF)
        factor_out[at_first + q_cols :, :] = jnp.zeros(
            (4 * q_cols - at_first - q_cols, rank), BF
        )
        copies[0].wait()
        step = 4 * HEAD_DIM
        for at in range(0, q_cols, step):
            part = jnp.dot(gb_ref[...], a1[:, at : at + step], preferred_element_type=F32)
            part += nt(glo_ref[...], io_ref[at : at + step, :])
            ga_s[at : at + step, :] = part.astype(BF).T
        seen_first = seen(PROMPT, PROMPT, 0, 0)
        seen_second = seen(tokens - PROMPT, tokens - PROMPT, PROMPT, PROMPT)

        def one_head(g, _):
            k_rows = pl.ds(pl.multiple_of(g * HEAD_DIM, 16), HEAD_DIM)
            keys_up = k_ref[k_rows, :]
            keys = keys_up.T
            values = v_ref[k_rows, :].T
            grad_k, grad_v = [0.0, 0.0], [0.0, 0.0]
            for h in range(group):
                rows = pl.ds(pl.multiple_of((g * group + h) * HEAD_DIM, 16), HEAD_DIM)
                head, grad = q_ref[rows, :], ga_s[rows, :]
                lse_h = lse_ref[g, h : h + 1, :]
                score = jnp.dot(keys[:PROMPT], head[:, :PROMPT], preferred_element_type=F32)
                prob = jnp.where(seen_first, jnp.exp(score * scale - lse_h[:, :PROMPT]), 0.0)
                grad_prob = jnp.dot(values[:PROMPT], grad[:, :PROMPT], preferred_element_type=F32)
                row_term = jnp.sum(prob * grad_prob, axis=0, keepdims=True)
                grad_score = (prob * (grad_prob - row_term)).astype(BF)
                prob = prob.astype(BF)
                grad_q_early = jnp.dot(
                    keys_up[:, :PROMPT], grad_score, preferred_element_type=F32
                )
                grad_v[0] += nt(grad[:, :PROMPT], prob)
                grad_k[0] += nt(head[:, :PROMPT], grad_score)
                score = jnp.dot(keys, head[:, PROMPT:], preferred_element_type=F32)
                expo = jnp.exp(score * scale - lse_h[:, PROMPT:])
                prob_p = expo[:PROMPT]
                prob_o = jnp.where(seen_second, expo[PROMPT:], 0.0)
                grad_prob = jnp.dot(values, grad[:, PROMPT:], preferred_element_type=F32)
                row_term = jnp.sum(prob_p * grad_prob[:PROMPT], axis=0, keepdims=True) + jnp.sum(
                    prob_o * grad_prob[PROMPT:], axis=0, keepdims=True
                )
                score_p = (prob_p * (grad_prob[:PROMPT] - row_term)).astype(BF)
                score_o = (prob_o * (grad_prob[PROMPT:] - row_term)).astype(BF)
                grad_q_late = jnp.dot(
                    keys_up, jnp.concatenate([score_p, score_o], axis=0), preferred_element_type=F32
                )
                grad_v[0] += nt(grad[:, PROMPT:], prob_p.astype(BF))
                grad_v[1] += nt(grad[:, PROMPT:], prob_o.astype(BF))
                grad_k[0] += nt(head[:, PROMPT:], score_p)
                grad_k[1] += nt(head[:, PROMPT:], score_o)
                grad_q = jnp.concatenate([grad_q_early, grad_q_late], axis=1) * scale
                g_s[rows, :] = turn(grad_q, cos_ref, sin_ref, -1.0, 0).astype(BF)
            grad_key = jnp.concatenate(grad_k, axis=1) * scale
            g_s[pl.ds(pl.multiple_of(q_cols + g * HEAD_DIM, 16), HEAD_DIM), :] = turn(
                grad_key, cos_ref, sin_ref, -1.0, 0
            ).astype(BF)
            g_s[pl.ds(pl.multiple_of(q_cols + k_cols + g * HEAD_DIM, 16), HEAD_DIM), :] = (
                jnp.concatenate(grad_v, axis=1).astype(BF)
            )
            return 0

        lax.fori_loop(0, kv_heads, one_head, 0)
        gw_s[...] = g_s[...].T
        for at, size, low in (
            (0, q_cols, lq_ref),
            (q_cols, k_cols, lk_ref),
            (q_cols + k_cols, k_cols, lv_ref),
        ):
            factor_out[at : at + size, :] = jnp.dot(
                g_s[at : at + size, :], low[...], preferred_element_type=F32
            ).astype(BF)
        for i, (at, size, second) in enumerate(
            ((0, q_cols, sq_ref), (q_cols, k_cols, sk_ref), (q_cols + k_cols, k_cols, sv_ref))
        ):
            low_out[:, i * rank : (i + 1) * rank] = adapter_scale * nt(
                gw_s[:, at : at + size], second[...]
            )
        copies[1].wait()
        for at in range(0, width, 512):
            rows = slice(at, at + 512)
            part = nt(gw_s[:, :cols], a0[rows, :]) + nt(gw_s[:, cols:], a1[rows, q_cols:])
            back_out[:, rows] = part.astype(BF)

    return pl.pallas_call(
        kernel,
        out_shape=[
            jax.ShapeDtypeStruct((tokens, width), BF),
            jax.ShapeDtypeStruct((tokens, 3 * rank), F32),
            jax.ShapeDtypeStruct((4 * q_cols, rank), BF),
        ],
        in_specs=[SMEM, HBM, HBM] + [VMEM] * 5 + [HBM] * 2 + [VMEM] * 12,
        out_specs=[VMEM] * 3,
        scratch_shapes=[
            pltpu.VMEM((width, cols), BF),
            pltpu.VMEM((width, cols), BF),
            pltpu.VMEM((tokens, width), BF),
            pltpu.VMEM((tokens, rank), BF),
            pltpu.VMEM((q_cols, tokens), BF),
            pltpu.VMEM((q_cols + 2 * k_cols, tokens), BF),
            pltpu.VMEM((tokens, q_cols + 2 * k_cols), BF),
            pltpu.SemaphoreType.DMA((4,)),
        ],
        compiler_params=pltpu.CompilerParams(vmem_limit_bytes=56 * 2**20),
        cost_estimate=pl.CostEstimate(
            flops=20 * tokens * width * cols, transcendentals=0, bytes_accessed=4 * width * cols
        ),
    )(
        core, *halves, select, second_output, low_output, attended, in_output, full_a0, full_a1, query,
        key, value, lse, cos, sin, second_query, second_key, second_value, low_query, low_key, low_value,
    )


def after_attention(
    hidden, branches, branch_lows, select, second_output, gain, mlp_in
):
    tokens, width = hidden.shape
    rank = select.shape[1]
    tile = 128

    def kernel(h_ref, b0, b1, l0, l1, sel_ref, so_ref, gain_ref, in_ref, mid_out, ext_out, low_out):
        def one(t, _):
            r = pl.ds(pl.multiple_of(t * tile, tile), tile)
            sel = sel_ref[r, :]
            low = ((l0[r, :] + l1[r, :]) * sel).astype(BF)
            low_out[r, :] = low
            middle = h_ref[r, :].astype(F32) + (b0[r, :].astype(F32) + b1[r, :].astype(F32))
            middle += adapter_scale * jnp.dot(low, so_ref[...], preferred_element_type=F32)
            mid_out[r, :] = middle
            scale = lax.rsqrt(jnp.mean(middle * middle, axis=1, keepdims=True) + norm_eps)
            normed = (middle * scale * gain_ref[...]).astype(BF)
            ext_out[r, :width] = normed
            part = jnp.dot(normed, in_ref[...], preferred_element_type=F32)
            part = (part * jnp.concatenate([sel, sel], axis=1)).astype(BF)
            ext_out[r, width:] = part * jnp.array(adapter_scale, BF)
            return 0

        lax.fori_loop(0, tokens // tile, one, 0)

    return pl.pallas_call(
        kernel,
        out_shape=[
            jax.ShapeDtypeStruct((tokens, width), F32),
            jax.ShapeDtypeStruct((tokens, width + 2 * rank), BF),
            jax.ShapeDtypeStruct((tokens, rank), BF),
        ],
        in_specs=[VMEM] * 9,
        out_specs=[VMEM] * 3,
        compiler_params=pltpu.CompilerParams(vmem_limit_bytes=40 * 2**20),
        cost_estimate=pl.CostEstimate(
            flops=6 * tokens * width * rank, transcendentals=0, bytes_accessed=14 * tokens * width
        ),
    )(hidden, *branches, *branch_lows, select, second_output, gain, mlp_in)


def after_feed_forward(core, parts, middle, cotangent, select, gain, mlp_in):
    half, wide = parts[0].shape
    tokens, width = middle.shape
    rank = select.shape[1]
    tile = 128

    def kernel(
        core_ref, p0, p1, p2, mid_hbm, cot_hbm, sel_ref, gain_ref, in_ref, mid_out, branch_out, low_out,
        mid_s, cot_s, sems,
    ):
        start = pl.multiple_of(core_ref[0] * half, 16)
        copies = [
            pltpu.make_async_copy(mid_hbm.at[pl.ds(start, half)], mid_s, sems.at[0]),
            pltpu.make_async_copy(cot_hbm.at[pl.ds(start, half)], cot_s, sems.at[1]),
        ]
        for copy in copies:
            copy.start()
        for copy in copies:
            copy.wait()

        def one(t, _):
            r = pl.ds(pl.multiple_of(t * tile, tile), tile)
            sel = sel_ref[pl.ds(pl.multiple_of(start + t * tile, tile), tile), :]
            total = p0[r, :].astype(F32) + p1[r, :].astype(F32) + p2[r, :].astype(F32)
            low = (
                adapter_scale * total[:, width:] * jnp.concatenate([sel, sel], axis=1)
            ).astype(BF)
            low_out[r, :] = low
            grad = (total[:, :width] + nt(low, in_ref[...])) * gain_ref[...]
            middle = mid_s[r, :]
            scale = lax.rsqrt(jnp.mean(middle * middle, axis=1, keepdims=True) + norm_eps)
            inner = jnp.mean(middle * grad, axis=1, keepdims=True)
            out = cot_s[r, :].astype(F32) + scale * grad - middle * (scale * scale * scale * inner)
            mid_out[r, :] = out
            branch_out[r, :] = out.astype(BF)
            return 0

        lax.fori_loop(0, half // tile, one, 0)

    return pl.pallas_call(
        kernel,
        out_shape=[
            jax.ShapeDtypeStruct((half, width), F32),
            jax.ShapeDtypeStruct((half, width), BF),
            jax.ShapeDtypeStruct((half, 2 * rank), BF),
        ],
        in_specs=[SMEM] + [VMEM] * 3 + [HBM] * 2 + [VMEM] * 3,
        out_specs=[VMEM] * 3,
        scratch_shapes=[
            pltpu.VMEM((half, width), F32),
            pltpu.VMEM((half, width), BF),
            pltpu.SemaphoreType.DMA((2,)),
        ],
        compiler_params=pltpu.CompilerParams(vmem_limit_bytes=40 * 2**20),
        cost_estimate=pl.CostEstimate(
            flops=6 * half * width * rank, transcendentals=0, bytes_accessed=20 * half * width
        ),
    )(core, *parts, middle, cotangent, select, gain, mlp_in)


def feed_forward(places, core, normed, cot, new, old, totals, last):
    sums = totals != "none"
    first = totals is None
    before = list(totals) if sums and not first else []
    n_new, n_old = len(new), len(old)
    blocks = [list(unit[-1]) for unit in new + old]
    factors = [unit[-2] for unit in new + old]
    count, per = len(blocks), len(blocks[0])
    part_rows, wide = blocks[0][0].shape
    group, n_wide = normed[0].shape
    c_wide = cot[0].shape[1]
    rank = n_wide - c_wide
    width = c_wide - rank
    rows = 2 * group
    tile = group // 2
    tiles = rows // tile
    flat = [v for unit, factor in zip(blocks, factors) for v in unit + [factor]]
    old_flat = [v for unit in old for v in unit[:2]]
    n_sums = (4 if last else 2) if sums else 0

    def kernel(place_ref, core_ref, *refs):
        it = iter(refs)

        def take(n):
            return [next(it) for _ in range(n)]

        old_ref = take(2 * n_old)
        normed_hbm, cot_hbm = take(3), take(3)
        block_hbm = [take(per + 1) for _ in range(count)]
        before_hbm = take(len(before))
        sum_hbm = take(n_sums)
        act_ref, grad_ref, own_ref = (take(n_new) for _ in range(3))
        w_s, sem_w = take(2)
        if n_new:
            normed_s, cot_s, sem_x = take(3)
        if sums:
            acc_g, acc_o, sem_t, sem_out = take(4)
            fin_g, fin_o = (normed_s, cot_s) if last else (acc_g, acc_o)
        mine = core_ref[0]

        def fetch(k):
            slot = w_s.at[k % 2]
            return bring(block_hbm[k][:per], place_ref, slot, sem_w.at[k % 2]) + [
                pltpu.make_async_copy(
                    block_hbm[k][per], slot.at[pl.ds(width, 2 * rank)], sem_w.at[k % 2, places.shape[0]]
                )
            ]

        def load_x(t):
            copies = []
            for i, (src, dst) in enumerate(((normed_hbm, normed_s), (cot_hbm, cot_s))):
                if t < 2:
                    part, to = src[0].at[pl.ds(t * tile, tile)], t * tile
                else:
                    part = src[t - 1]
                    to = group + tile * (mine if t == 2 else 1 - mine)
                    to = pl.multiple_of(to, 16)
                copies.append(pltpu.make_async_copy(part, dst.at[pl.ds(to, tile)], sem_x.at[i, t]))
            return copies

        def load_t(t):
            r = pl.ds(t * tile, tile)
            return [
                pltpu.make_async_copy(src.at[r], dst.at[r], sem_t.at[i, t])
                for i, (src, dst) in enumerate(zip(before_hbm, (acc_g, acc_o)))
            ]

        def store_t(t, to):
            r = pl.ds(t * tile, tile)
            copies = []
            for i, src in enumerate((fin_g, fin_o)):
                dst = sum_hbm[2 * i + to].at[t // 2] if last else sum_hbm[i].at[r]
                copies.append(pltpu.make_async_copy(src.at[r], dst, sem_out.at[i, t]))
            return copies

        if n_new:
            for copy in load_x(0):
                copy.start()
        for copy in fetch(0):
            copy.start()
        if n_new:
            for copy in fetch(0):
                copy.wait()
            for t in range(1, tiles):
                for copy in load_x(t):
                    copy.start()
        if before:
            for t in range(tiles):
                for copy in load_t(t):
                    copy.start()
        for k in range(count):
            if k + 1 < count:
                for copy in fetch(k + 1):
                    copy.start()
            if k or not n_new:
                for copy in fetch(k):
                    copy.wait()
            slot = k % 2
            if k < n_new:
                act, grad = act_ref[k], grad_ref[k]
                for t in range(tiles):
                    r = pl.ds(t * tile, tile)
                    if k == 0 and t < 2:
                        for copy in load_x(t):
                            copy.wait()
                    if k == 0 and t == 2:
                        for copy in load_x(2) + load_x(3):
                            copy.wait()
                    x = normed_s[r, :]
                    gate = jnp.dot(x, w_s[slot, :, 0:WIDTH], preferred_element_type=F32)
                    up = jnp.dot(x, w_s[slot, :, WIDTH : 2 * WIDTH], preferred_element_type=F32)
                    back = jnp.dot(
                        cot_s[r, :],
                        w_s[slot, :c_wide, 2 * WIDTH : 3 * WIDTH],
                        preferred_element_type=F32,
                    )
                    sig = 1.0 / (1.0 + jnp.exp(-gate))
                    silu = gate * sig
                    act[r, :] = (silu * up).astype(BF)
                    grad[r, :WIDTH] = (back * up * (sig * (1.0 + gate * (1.0 - sig)))).astype(BF)
                    grad[r, WIDTH:] = (back * silu).astype(BF)
                low = normed_s[:, width:].T
                for part in range(2):
                    second = jnp.dot(
                        low[part * rank : (part + 1) * rank],
                        grad[:, part * WIDTH : (part + 1) * WIDTH],
                        preferred_element_type=F32,
                    ).astype(BF)
                    for at in range(0, WIDTH, rank):
                        to = part * WIDTH + at
                        own_ref[k][to : to + rank, :] = second[:, at : at + rank]
                own_ref[k][2 * WIDTH :, :] = jnp.dot(
                    act[...].T, cot_s[:, width:c_wide], preferred_element_type=F32
                ).astype(BF)
            else:
                act, grad = old_ref[2 * (k - n_new)], old_ref[2 * (k - n_new) + 1]
            if not sums:
                continue
            for t in range(tiles):
                r = pl.ds(t * tile, tile)
                if before and k == 0:
                    for copy in load_t(t):
                        copy.wait()
                for acc, fin, val, lo, hi, top in (
                    (acc_g, fin_g, grad, 0, 2 * WIDTH, n_wide),
                    (acc_o, fin_o, act, 2 * WIDTH, 3 * WIDTH, c_wide),
                ):
                    for at in range(0, top, 512):
                        n = slice(at, min(at + 512, top))
                        part = nt(val[r, :], w_s[slot, n, lo:hi])
                        if k or not first:
                            part = acc[r, n] + part
                        if k == count - 1:
                            fin[r, n] = part.astype(fin.dtype)
                        else:
                            acc[r, n] = part
                if k == count - 1 and last:
                    side = mine if t % 2 == 0 else 1 - mine
                    for to in range(2):

                        @pl.when(side == to)
                        def _():
                            for copy in store_t(t, to):
                                copy.start()

                elif k == count - 1:
                    for copy in store_t(t, 0):
                        copy.start()
        if sums:
            for t in range(tiles):
                for copy in store_t(t, 0):
                    copy.wait()

    scratch = [
        pltpu.VMEM((2, n_wide, wide), BF),
        pltpu.SemaphoreType.DMA((2, places.shape[0] + 1)),
    ]
    if n_new:
        scratch += [
            pltpu.VMEM((rows, n_wide), BF),
            pltpu.VMEM((rows, c_wide), BF),
            pltpu.SemaphoreType.DMA((2, tiles)),
        ]
    out_shape = []
    if sums:
        scratch += [
            pltpu.VMEM((rows, n_wide), F32),
            pltpu.VMEM((rows, c_wide), F32),
            pltpu.SemaphoreType.DMA((2, tiles)),
            pltpu.SemaphoreType.DMA((2, tiles)),
        ]
        for columns in (n_wide, c_wide):
            if last:
                out_shape += [jax.ShapeDtypeStruct((2, tile, columns), BF)] * 2
            else:
                out_shape += [jax.ShapeDtypeStruct((rows, columns), F32)]
    out_shape += [jax.ShapeDtypeStruct((rows, WIDTH), BF)] * n_new
    out_shape += [jax.ShapeDtypeStruct((rows, 2 * WIDTH), BF)] * n_new
    out_shape += [jax.ShapeDtypeStruct((3 * WIDTH, rank), BF)] * n_new
    n_hbm = 6 + len(flat)
    at = 2 + len(old_flat) + n_hbm
    out = pl.pallas_call(
        kernel,
        out_shape=out_shape,
        in_specs=[SMEM] * 2 + [VMEM] * len(old_flat) + [HBM] * (n_hbm + len(before)),
        out_specs=[HBM] * n_sums + [VMEM] * (3 * n_new),
        scratch_shapes=scratch,
        input_output_aliases={at: 0, at + 1: 1} if before and not last else {},
        compiler_params=pltpu.CompilerParams(vmem_limit_bytes=60 * 2**20),
        cost_estimate=pl.CostEstimate(
            flops=6 * (n_new + (count if sums else 0)) * rows * width * WIDTH,
            transcendentals=n_new * rows * WIDTH,
            bytes_accessed=4 * rows * width,
        ),
    )(places, core, *old_flat, *normed, *cot, *flat, *before)
    rest = out[n_sums:]
    return tuple(out[:n_sums]), list(zip(*(rest[i * n_new : (i + 1) * n_new] for i in range(3))))
def adapter_columns(ids_ref):
    sequences = ids_ref.shape[1]
    shape = (sequences * RANK, ADAPTER_COLS)
    row = lax.broadcasted_iota(jnp.int32, shape, 0)
    column = lax.broadcasted_iota(jnp.int32, shape, 1)
    start = jnp.zeros(shape, jnp.int32)
    for i in range(sequences):
        start = jnp.where(row // RANK == i, ids_ref[0, i] * RANK, start)
    return (column == start + row % RANK).astype(F32).astype(BF)


def pack(ids, factors, firsts):
    block = factors.shape[0] // BLOCKS
    sequences = ids.shape[1]
    lanes = BLOCKS * sequences * RANK

    def kernel(ids_ref, factor_ref, first_ref, factor_out, first_out, chosen_out):
        chosen = adapter_columns(ids_ref)
        chosen_out[...] = jnp.concatenate(
            [chosen[i * RANK : (i + 1) * RANK] for i in range(sequences)], axis=1
        )
        parts = [
            nt(factor_ref[i * block : (i + 1) * block, :], chosen) for i in range(BLOCKS)
        ]
        factor_out[...] = jnp.concatenate(parts, axis=1).astype(BF)
        parts = []
        for i in range(BLOCKS):
            q, s = i // 2, i % 2
            parts.append(
                nt(
                    first_ref[s * block : (s + 1) * block, q * ADAPTER_COLS : (q + 1) * ADAPTER_COLS],
                    chosen,
                )
            )
        first_out[...] = jnp.concatenate(parts, axis=1).astype(BF)

    return pl.pallas_call(
        kernel,
        out_shape=[jax.ShapeDtypeStruct((block, lanes), BF)] * 2
        + [jax.ShapeDtypeStruct((RANK, sequences * ADAPTER_COLS), BF)],
        in_specs=[SMEM, VMEM, VMEM],
        out_specs=[VMEM] * 3,
        compiler_params=pltpu.CompilerParams(vmem_limit_bytes=32 * 2**20),
        cost_estimate=pl.CostEstimate(flops=5_000_000_000, transcendentals=0, bytes_accessed=0),
    )(ids, factors, firsts)


def unpack(got):
    groups, share, lanes = got.shape
    share -= RANK
    each = lanes // BLOCKS
    sequences = each // RANK

    def kernel(got_ref, out_ref, total):
        total[...] = jnp.zeros_like(total)

        def one(g, _):
            packed = got_ref[g]
            chosen = jnp.concatenate(
                [
                    packed[share:, i * ADAPTER_COLS : (i + 1) * ADAPTER_COLS]
                    for i in range(sequences)
                ],
                axis=0,
            )
            for i in range(BLOCKS):
                total[i] += jnp.dot(
                    packed[:share, i * each : (i + 1) * each], chosen, preferred_element_type=F32
                )
            return 0

        lax.fori_loop(0, groups, one, 0)
        out_ref[...] = total[...].astype(BF)

    return pl.pallas_call(
        kernel,
        out_shape=jax.ShapeDtypeStruct((BLOCKS, share, ADAPTER_COLS), BF),
        in_specs=[VMEM],
        out_specs=VMEM,
        scratch_shapes=[pltpu.VMEM((BLOCKS, share, ADAPTER_COLS), F32)],
        compiler_params=pltpu.CompilerParams(vmem_limit_bytes=32 * 2**20),
        cost_estimate=pl.CostEstimate(flops=5_000_000_000, transcendentals=0, bytes_accessed=0),
    )(got)


def unit_results(at, parts, chunks):
    ring, share, cols = parts[0].shape
    units = chunks * WIDTH

    def kernel(at_ref, *refs):
        gate_out, up_out, down_out, all_s = refs[8:]
        for i in range(8):
            core = at_ref[0] if i < 4 else 1 - at_ref[0]
            bit_y = at_ref[1] if i // 2 % 2 == 0 else 1 - at_ref[1]
            bit_x = at_ref[2] if i % 2 == 0 else 1 - at_ref[2]

            def one(r, _):
                place = lax.rem(at_ref[3] + ring - r, ring) * 2 + bit_y
                to = pl.multiple_of(place * share, 8)
                all_s[core * 2 + bit_x, pl.ds(to, share), :] = refs[i][r].astype(F32)
                return 0

            lax.fori_loop(0, ring, one, 0)
        for q in range(4):
            for j in range(chunks):
                start = q * units + j * WIDTH
                row = j * 3 * WIDTH
                for at in range(0, WIDTH, cols):
                    to = slice(start + at, start + at + cols)
                    gate_out[:, to] = all_s[q, row + at : row + at + cols, :]
                    at += WIDTH
                    up_out[:, to] = all_s[q, row + at : row + at + cols, :]
                row += 2 * WIDTH
                down_out[start : start + WIDTH, :] = all_s[q, row : row + WIDTH, :]

    return pl.pallas_call(
        kernel,
        out_shape=[
            jax.ShapeDtypeStruct((cols, 4 * units), F32),
            jax.ShapeDtypeStruct((cols, 4 * units), F32),
            jax.ShapeDtypeStruct((4 * units, cols), F32),
        ],
        in_specs=[SMEM] + [VMEM] * 8,
        out_specs=[VMEM] * 3,
        scratch_shapes=[pltpu.VMEM((4, 3 * units, cols), F32)],
        compiler_params=pltpu.CompilerParams(vmem_limit_bytes=48 * 2**20),
        cost_estimate=pl.CostEstimate(flops=8_000_000_000, transcendentals=0, bytes_accessed=0),
    )(at, *parts)


def other_results(at, parts, share, second_cols):
    ring, rows, cols = parts[0].shape
    chips = 4 * ring
    late_rows = BLOCKS * 2 * share
    pair_rows = (rows - late_rows) // 2
    block = chips * share
    half = 2 * block
    query_cols, key_cols = second_cols

    def kernel(at_ref, *refs):
        part_refs, outs = refs[:8], refs[8:19]
        query_s, pair_s, output_s, down_s = refs[19:]
        (
            in_q, second_q, in_k, second_k, in_v, second_v, in_o, second_o, in_g, in_u, second_d,
        ) = outs
        homes = (query_s, pair_s, output_s, in_o, None)
        for i in range(8):
            core = at_ref[0] if i < 4 else 1 - at_ref[0]
            bit_y = at_ref[1] if i // 2 % 2 == 0 else 1 - at_ref[1]
            bit_x = at_ref[2] if i % 2 == 0 else 1 - at_ref[2]

            def one(r, _):
                chip = lax.rem(at_ref[3] + ring - r, ring) * 4 + bit_y * 2 + bit_x
                found = part_refs[i][r].astype(F32)
                for b, (home, s) in enumerate(
                    ((query_s, 0), (query_s, 1), (pair_s, 0), (output_s, 0), (output_s, 1), (in_o, 0), (in_o, 1))
                ):
                    size = block if home is pair_s else half
                    to = pl.multiple_of(core * size + s * block + chip * share, 8)
                    home[pl.ds(to, share), :] = found[2 * b * share : (2 * b + 1) * share]
                for b in range(BLOCKS):
                    home, s = (in_q, in_k, in_v, down_s)[b // 2], b % 2
                    to = pl.multiple_of(core * half + s * block + chip * share, 8)
                    home[pl.ds(to, share), :] = found[(2 * b + 1) * share : (2 * b + 2) * share]
                for k, home in enumerate((in_g, in_u)):
                    to = pl.multiple_of(core * half + chip * pair_rows, 8)
                    start = late_rows + k * pair_rows
                    home[pl.ds(to, pair_rows), :] = found[start : start + pair_rows]
                return 0

            lax.fori_loop(0, ring, one, 0)
        second_q[...] = query_s[...].T
        second_o[...] = output_s[...].T
        second_d[...] = down_s[...].T
        both = pair_s[...].T
        for out, start in ((second_k, 0), (second_v, key_cols)):
            out[...] = jnp.concatenate(
                [both[:, c * block + start : c * block + start + key_cols] for c in range(2)], axis=1
            )

    width = 2 * half

    def shape(*dims):
        return jax.ShapeDtypeStruct(dims, F32)

    return pl.pallas_call(
        kernel,
        out_shape=[
            shape(width, cols), shape(cols, 2 * query_cols), shape(width, cols),
            shape(cols, 2 * key_cols), shape(width, cols), shape(cols, 2 * key_cols),
            shape(width, cols), shape(cols, width), shape(width, cols), shape(width, cols),
            shape(cols, width),
        ],
        in_specs=[SMEM] + [VMEM] * 8,
        out_specs=[VMEM] * 11,
        scratch_shapes=[
            pltpu.VMEM((width, cols), F32),
            pltpu.VMEM((half, cols), F32),
            pltpu.VMEM((width, cols), F32),
            pltpu.VMEM((width, cols), F32),
        ],
        compiler_params=pltpu.CompilerParams(vmem_limit_bytes=48 * 2**20),
        cost_estimate=pl.CostEstimate(flops=8_000_000_000, transcendentals=0, bytes_accessed=0),
    )(at, *parts)


DP = ("ring", "second", "first")


def make_body(n):
    ring_size = n // 4
    perms = ring_and_swaps(n)

    def move(value, link):
        return lax.ppermute(value, DP, perms[link])

    def other_core(value):
        return lax.ppermute(value, "tensor", [(0, 1), (1, 0)])

    def take(value, start, size, axis=0):
        return lax.dynamic_slice_in_dim(value, start, size, axis)

    def body(
        hidden_in, adapter_ids, attn_gain, mlp_gain, w_query, w_key, w_value, w_output, w_gate,
        w_up, w_down, in_query, second_query, in_key, second_key, in_value, second_value,
        in_output, second_output, in_gate, second_gate, in_up, second_up, in_down, second_down,
        cotangent,
    ):
        num_rows, width = hidden_in.shape
        half_rows = num_rows // 2
        half_width = width // 2
        rank_cols = in_query.shape[1]
        units = w_gate.shape[1] // 2
        chunks = units // WIDTH
        shard = w_query.shape[0]

        ring_at, bit_y, bit_x = (lax.axis_index(name) for name in DP)
        core = lax.axis_index("tensor")
        core_at = core.astype(jnp.int32).reshape(1)
        bits = {"x": bit_x, "y": bit_y}

        def in_order(bit, value, received, axis=0):
            first = jnp.where(bit == 0, value, received)
            return jnp.concatenate([first, jnp.where(bit == 0, received, value)], axis=axis)

        def half_of(value):
            return take(value, core * half_rows, half_rows)

        def both_halves(value):
            return in_order(core, value, other_core(value))

        def cols_of_core(value):
            return take(value, core * half_width, half_width, 1)

        row_index = lax.iota(jnp.int32, num_rows)
        is_later = row_index >= PROMPT
        seq_of = jnp.where(is_later, 1 + (row_index - PROMPT) // CONT_LEN, 0)
        position = jnp.where(is_later, PROMPT + (row_index - PROMPT) % CONT_LEN, row_index)
        seq_ids = lax.iota(jnp.int32, adapter_ids.shape[1])
        row_adapter = jnp.sum(
            jnp.where(seq_of[:, None] == seq_ids[None, :], adapter_ids[0][None, :], 0), axis=1
        )
        select = (lax.iota(jnp.int32, rank_cols)[None, :] // RANK == row_adapter[:, None]).astype(F32)
        select_three = jnp.concatenate([select] * 3, axis=1)
        inv_freq = rope_base ** (-2.0 * lax.iota(F32, HEAD_DIM // 2) / HEAD_DIM)
        angles = inv_freq[:, None] * position.astype(F32)[None, :]
        cos_table, sin_table = jnp.cos(angles), jnp.sin(angles)
        attn_in = jnp.concatenate([in_query, in_key, in_value], axis=1)
        mlp_in = jnp.concatenate([in_gate, in_up], axis=1)
        attn_gain_f = attn_gain.astype(F32)
        mlp_gain_f = mlp_gain.astype(F32).reshape(1, width)
        two = jnp.array(adapter_scale, BF)

        unit_start = bit_x * units

        def half_units(start):
            return (
                take(w_gate, start, units, 1),
                take(w_up, start, units, 1),
                take(w_down, start, units, 0).T,
            )

        mine, others = half_units(unit_start), half_units(units - unit_start)

        def chunk_of(parts, j):
            return jnp.concatenate([p[:, j * WIDTH : (j + 1) * WIDTH] for p in parts], axis=1)

        factor_parts = (
            take(second_gate, unit_start, units, 1),
            take(second_up, unit_start, units, 1),
            take(in_down, unit_start, units, 0),
        )
        blank = jnp.zeros((rank_cols, WIDTH), BF)
        chunk_cols = 3 * WIDTH

        def factors_of(j):
            cols = slice(j * WIDTH, (j + 1) * WIDTH)
            gate, up, down = factor_parts
            upper = jnp.concatenate([gate[:, cols], blank, down[cols].T], axis=1)
            return jnp.concatenate(
                [upper, jnp.concatenate([blank, up[:, cols], blank], axis=1)], axis=0
            )

        grad_low_down = (
            adapter_scale * product_with_transpose(cotangent, second_down) * select
        ).astype(BF)
        cot_wide = jnp.concatenate([cotangent, grad_low_down], axis=1)

        held = {
            "A0.o": jnp.concatenate([w_query, w_key], axis=1),
            "A1.p0": jnp.concatenate([w_output.T, w_value], axis=1),
            "C.o": half_of(cot_wide),
        }
        groups = exchanges_of(chunks)
        for i, group in enumerate(groups):
            held[f"E{i}.o"] = jnp.concatenate([chunk_of(others, j) for j in group], axis=1)
        plan = plan_transfers(ring_size, chunks)
        steps, arrivals = schedule(plan, chunks)
        when = {name: s for s, names in arrivals.items() for name in names}
        last_step = len(steps) - 1

        def there(tag):
            return max(s for name, s in when.items() if name.split(".")[0] == tag)

        def pieces(tag):
            found, places = [], []
            for r in range(ring_size):
                ring = (ring_at - r + ring_size) % ring_size
                if tag[0] == "A":
                    for other in range(2):
                        found.append(held[f"{tag}.{'x' if other else 'b'}{r}"])
                        bit = 1 - bit_x if other else bit_x
                        places += [(ring * 2 + bit_y) * 2 + bit, (ring * 2 + 1 - bit_y) * 2 + bit]
                else:
                    for other in range(2):
                        name = f"{tag}.q{r}" if other else f"{tag}.p{r}" if r else tag
                        found.append(held[name])
                        pair = ring * 2 + (1 - bit_y if other else bit_y)
                        places += [pair * 2 + bit_x, pair * 2 + 1 - bit_x]
            places = jnp.stack(places).astype(jnp.int32)
            if shard % 16:
                whole = jnp.zeros((n, shard, found[0].shape[1]), BF)
                for i in range(n):
                    part = found[i // 2][(i % 2) * shard : (i % 2 + 1) * shard]
                    whole = lax.dynamic_update_slice(whole, part[None], (places[i], 0, 0))
                return [whole.reshape(n * shard, -1)], jnp.zeros((1,), jnp.int32)
            return found, places

        v = {}
        hidden_wide = hidden_in.astype(F32)
        normed_a = rms_norm(hidden_wide, attn_gain_f).astype(BF)
        low_attn = (matrix_product(normed_a, attn_in) * select_three).astype(BF)
        lows = [low_attn[:, i * rank_cols : (i + 1) * rank_cols] * two for i in range(3)]

        def start_attention():
            found, places = pieces("A0")
            v["query"], v["key"], v["a0"] = queries_and_keys(
                places, found, normed_a, lows[0], lows[1], second_query, second_key, cos_table,
                sin_table,
            )
            return [v["key"]]

        def finish_attention():
            found, places = pieces("A1")
            v["value"], v["attended"], v["lse"], branch, branch_low, v["a1"] = attention(
                places, found, normed_a, lows[2], second_value, v["query"], v["key"], in_output
            )
            v["branches"] = (branch, other_core(branch))
            v["branch_lows"] = (branch_low, other_core(branch_low))
            return [v["value"]]

        def start_feed_forward():
            v["middle"], v["normed"], v["low_output"] = after_attention(
                hidden_in, v["branches"], v["branch_lows"], select, second_output, mlp_gain_f, mlp_in
            )
            held["N.o"] = half_of(v["normed"])
            return [v["low_output"]]

        def meet_neighbour():
            v["normed_all"] = (v["normed"], held["N.x"], other_core(held["N.x"]))
            v["cot_all"] = (cot_wide, held["C.x"], other_core(held["C.x"]))
            return [v["normed_all"][2], v["cot_all"][2]]

        unit_out = {}

        def feed(new, old, totals, last):
            found = {j: pieces(f"M{j}") for j in new + old}
            sums, results = feed_forward(
                found[(new + old)[0]][1],
                core_at,
                v["normed_all"],
                v["cot_all"],
                [(factors_of(j), found[j][0]) for j in new],
                [unit_out[j][:2] + (factors_of(j), found[j][0]) for j in old],
                totals,
                last,
            )
            unit_out.update(zip(new, results))
            return sums

        def units_only(new):
            def run():
                feed(new, [], "none", False)
                return [unit_out[new[-1]][0]]

            return run

        order = sorted(range(chunks), key=lambda j: there(f"M{j}"))
        events = {}

        def at_step(s, run):
            events.setdefault(min(s, last_step), []).append(run)

        at_step(there("A0"), start_attention)
        at_step(there("A1"), finish_attention)
        at_step(there("A1") + NORMED_AFTER - 1, start_feed_forward)
        begin = there("N")
        at_step(begin, meet_neighbour)
        early, later, final = order[: chunks - 3], order[chunks - 3 : chunks - 1], order[-1]
        at = begin
        for i in range(0, len(early), 2):
            pair = early[i : i + 2]
            at = max([at] + [there(f"M{j}") for j in pair])
            at_step(at, units_only(pair))
            at += 1
        for j in later:
            at_step(max(at, there(f"M{j}")), units_only([j]))

        waits = []
        for s, step in enumerate(steps):
            sources = sorted({plan[name][1] for name in step})
            if s:
                arrived = [name for name in arrivals.get(s, []) if name not in sources]
                if sources and arrived + waits:
                    tied = tie([held[k] for k in sources], [held[k] for k in arrived] + waits)
                    held.update(zip(sources, tied))
                    waits = []
            for name in step:
                held[name] = move(held[plan[name][1]], plan[name][0])
            for name in arrivals.get(s + 1, []):
                if name.endswith(".e"):
                    for i, j in enumerate(groups[int(name[1:-2])]):
                        got = held[name][:, i * chunk_cols : (i + 1) * chunk_cols]
                        held[f"M{j}"] = jnp.concatenate([chunk_of(mine, j), got], axis=0)
                elif name == "A0.y":
                    held["A0.b0"] = jnp.concatenate([held["A0.o"], held[name]], axis=0)
                elif name.startswith("A1") and name[3] in "pq":
                    pair = [f"A1.{side}{name[4:]}" for side in "pq"]
                    if f"A1.b{name[4:]}" not in held and all(p in held for p in pair):
                        if max(when.get(p, 0) for p in pair) <= s + 1:
                            held[f"A1.b{name[4:]}"] = jnp.concatenate([held[p] for p in pair], axis=0)
            for run in events.get(s, []):
                waits += run()

        totals = feed([final], early + later, None, True)
        grad_keep, grad_send, out_keep, out_send = totals

        def after(values, *others):
            return tie(list(values), list(others), 0)

        def total(parts):
            return jnp.sum(parts.astype(F32), axis=0).astype(BF)

        grad_got = other_core(grad_send)
        grad_out = (grad_keep[1].astype(F32) + grad_got[1].astype(F32)).astype(BF)
        grad_in_parts = (grad_keep[0], grad_got[0], move(grad_out, "x"))
        out_send, *own = after([out_send] + [unit_out[j][2] for j in range(chunks)], grad_out)
        out_got = other_core(out_send)
        out_out = (out_keep[1].astype(F32) + out_got[1].astype(F32)).astype(BF)
        own = jnp.concatenate(own, axis=0)
        got_units = lax.all_to_all(own.reshape(n // 2, -1, rank_cols), DP[:2], 0, 0)

        grad_middle, grad_branch, grad_low_mlp = after_feed_forward(
            core_at, grad_in_parts, v["middle"], cotangent, select, mlp_gain_f, mlp_in
        )
        out_in = move(after([out_out], grad_branch)[0], "x")
        grad_branch_other = other_core(grad_branch)
        grad_low_mlp = both_halves(grad_low_mlp)
        delta_mlp = transpose_then_product(
            cols_of_core(v["normed"][:, :width]), grad_low_mlp
        ).astype(BF)
        got_mlp = lax.all_to_all(delta_mlp.reshape(n, half_width // n, 2 * rank_cols), DP, 0, 0)

        back, back_low, factors = attention_back(
            core_at, (grad_branch, grad_branch_other), select, second_output, v["low_output"],
            v["attended"], in_output, v["a0"], v["a1"], v["query"], v["key"], v["value"], v["lse"],
            cos_table, sin_table, second_query, second_key, second_value, *lows,
        )
        back_low, out_in, got_mlp, got_units = after([back_low, out_in, got_mlp, got_units])
        back_low = back_low + other_core(back_low)
        grad_low_attn = (back_low * select_three).astype(BF)
        out_sum = out_keep[0].astype(F32) + out_got[0].astype(F32) + out_in.astype(F32)
        low_down = (out_sum[:, width:] * half_of(select)).astype(BF)
        firsts = jnp.concatenate(
            [
                transpose_then_product(cols_of_core(normed_a), grad_low_attn).astype(BF),
                (
                    adapter_scale
                    * transpose_then_product(cols_of_core(cotangent), both_halves(low_down))
                ).astype(BF),
            ],
            axis=1,
        )
        *packed, chosen = pack(adapter_ids, factors, firsts)
        share = packed[0].shape[0] // n
        packed = jnp.concatenate(
            [part.reshape(n, share, part.shape[1]) for part in packed]
            + [jnp.broadcast_to(chosen[None], (n,) + chosen.shape)],
            axis=1,
        )
        units_sum = total(got_units)
        units_sum = jnp.stack([units_sum] + [move(units_sum, f"z{r}") for r in range(1, ring_size)])
        packed, units_sum = after([packed, units_sum])
        got_late = lax.all_to_all(packed, DP, 0, 0)
        got_mlp, back, out_sum, grad_middle = after([got_mlp, back, out_sum, grad_middle], packed)
        units_parts = [units_sum] + [move(units_sum, link) for link in ("x", "y", "xy")]
        got_late, *units_parts[1:] = after([got_late] + units_parts[1:])

        device = jnp.stack([core, bit_y, bit_x, ring_at]).astype(jnp.int32)
        gradient_second_gate, gradient_second_up, delta_in_down = unit_results(
            device, units_parts + [other_core(part) for part in units_parts], chunks
        )

        layer_output = both_halves(
            (
                half_of(v["middle"])
                + out_sum[:, :width]
                + adapter_scale * matrix_product(low_down, second_down)
            ).astype(BF)
        )
        back_half = half_of(back).astype(F32) + other_core(
            take(back, (1 - core) * half_rows, half_rows)
        ).astype(F32)
        grad_normed_a = back_half + product_with_transpose(half_of(grad_low_attn), attn_in)
        grad_in = both_halves(
            (grad_middle + rms_back(half_of(hidden_wide), attn_gain_f, grad_normed_a)).astype(BF)
        )

        sums_mlp = total(got_mlp)
        sums = jnp.concatenate(
            [unpack(got_late).reshape(-1, rank_cols), sums_mlp[:, :rank_cols], sums_mlp[:, rank_cols:]],
            axis=0,
        )
        sums = jnp.stack([sums] + [move(sums, f"z{r}") for r in range(1, ring_size)], axis=0)
        parts = [sums] + [move(sums, link) for link in ("x", "y", "xy")]
        parts += [other_core(part) for part in parts]
        others = other_results(
            device,
            parts,
            share,
            (second_query.shape[1], second_key.shape[1]),
        )
        return (
            layer_output,
            grad_in,
            *others[:9],
            gradient_second_gate,
            others[9],
            gradient_second_up,
            delta_in_down,
            others[10],
        )

    return body


def solution(mesh):
    n, tensor = mesh.shape["dp"], mesh.shape["tensor"]
    split = jax.sharding.Mesh(mesh.devices.reshape(n // 4, 2, 2, tensor), DP + ("tensor",))
    return jax.shard_map(
        make_body(n),
        mesh=split,
        in_specs=(
            P(DP, None), P(DP, None), P(), P(), P(DP, "tensor"), P(DP, "tensor"), P(DP, "tensor"),
            P("tensor", DP), P(DP, "tensor"), P(DP, "tensor"), P("tensor", DP), P(),
            P(None, "tensor"), P(), P(None, "tensor"), P(), P(None, "tensor"), P("tensor", None),
            P(), P(), P(None, "tensor"), P(), P(None, "tensor"), P("tensor", None), P(), P(DP, None),
        ),
        out_specs=(P(DP, None), P(DP, None)) + (P(),) * 14,
        check_vma=False,
    )
```

```python
import math

import jax
import jax.numpy as jnp
from jax import lax
from jax.experimental import pallas as pl
from jax.experimental.pallas import tpu as pltpu
from jax.sharding import PartitionSpec as P

HEAD_DIM = 80
RANK = 16
PROMPT = 256
CONT_LEN = 128
WIDTH = 256
ADAPTER_COLS = 128
BLOCKS = 8

adapter_scale = 2.0
norm_eps = 1e-05
rope_base = 1000000.0

BF = jnp.bfloat16
F32 = jnp.float32

LAG = 2
STEP_FLOPS = 20_000_000_000
NORMED_AFTER = 4
EXCHANGES = ((0, 1), (2, 3), (4, 5, 6))
EXCHANGE_PRIORITY = (-40, -39, 8)
ATTN_PRIORITY = (-20, -10)
YZ_CHUNKS = ()
LAST_WIDE = 30
CHUNK_PRIORITY = (0, 1, 2, 3, 4, 5, 6)
BY_RING_FROM = (9, 9, 9, 9, 3, 3, 3)


def matrix_product(left, right):
    return jnp.dot(left, right, preferred_element_type=F32)


def product_with_transpose(left, right):
    return lax.dot_general(left, right, (((1,), (1,)), ((), ())), preferred_element_type=F32)


def transpose_then_product(left, right):
    return lax.dot_general(left, right, (((0,), (0,)), ((), ())), preferred_element_type=F32)


def rms_norm(values, gain_vec):
    return (
        values * lax.rsqrt(jnp.mean(values * values, axis=-1, keepdims=True) + norm_eps) * gain_vec
    )


def rms_back(values, gain_vec, grad):
    scale = lax.rsqrt(jnp.mean(values * values, axis=-1, keepdims=True) + norm_eps)
    e = gain_vec * grad
    return scale * e - values * (scale * scale * scale) * jnp.mean(values * e, axis=-1, keepdims=True)


def ring_and_swaps(n):
    perms = {
        "y": [(i, i ^ 2) for i in range(n)],
        "x": [(i, i ^ 1) for i in range(n)],
        "xy": [(i, i ^ 3) for i in range(n)],
    }
    for r in range(1, n // 4):
        perms[f"z{r}"] = [(i, (i + 4 * r) % n) for i in range(n)]
    perms["z"] = perms["z1"]
    return perms


def plan_transfers(ring_size, chunks):
    plan = {}
    first, second = ATTN_PRIORITY
    plan["A0.y"] = ("y", "A0.o", first, 1)
    for r in range(ring_size):
        if r:
            plan[f"A0.b{r}"] = ("z", f"A0.b{r - 1}", first + 0.01 * r, 2)
            plan[f"A1.p{r}"] = ("z", f"A1.p{r - 1}", second + 0.01 * r, 1)
        plan[f"A1.q{r}"] = ("y", f"A1.p{r}", second + 0.01 * r, 1)
        plan[f"A0.x{r}"] = ("x", f"A0.b{r}", first + 0.01 * r, 2)
        plan[f"A1.x{r}"] = ("x", f"A1.b{r}", second + 0.01 * r, 2)
    for i, group in enumerate(exchanges_of(chunks)):
        plan[f"E{i}.e"] = ("x", f"E{i}.o", EXCHANGE_PRIORITY[min(i, 2)], (len(group) + 1) // 2)
    for j in range(chunks):
        tag = f"M{j}"
        for r in range(ring_size):
            source = (f"{tag}.p{r}" if r else tag)
            if r:
                before = f"{tag}.p{r - 1}" if r > 1 else tag
                plan[f"{tag}.p{r}"] = ("z", before, CHUNK_PRIORITY[min(j, 6)] + 0.01 * r, 1)
            link = "y"
            if r >= BY_RING_FROM[min(j, 6)]:
                link, source = "z", f"{tag}.q{r - 1}"
            plan[f"{tag}.q{r}"] = (link, source, CHUNK_PRIORITY[min(j, 6)] + 0.01 * r, 1)
    plan["C.x"] = ("x", "C.o", LAST_WIDE, 3)
    plan["N.x"] = ("x", "N.o", -50, 3)
    return plan


def exchanges_of(chunks):
    return EXCHANGES[:2] + (tuple(range(4, chunks)),)


def schedule(plan, chunks):
    makes = {"A0.y": ["A0.b0"]}
    for i, group in enumerate(exchanges_of(chunks)):
        makes[f"E{i}.e"] = [f"M{j}" for j in group]
    ready, busy, arrivals = {}, {}, {}
    for _, source, _, _ in plan.values():
        if source.endswith(".o") and source != "N.o":
            ready[source] = 0
    ready["A1.p0"] = 0
    steps, waiting, now = [], dict(plan), 0
    while waiting:
        step = []
        if "N.o" not in ready and not any(name.startswith("A1") for name in waiting):
            ready["N.o"] = max(s for s, names in arrivals.items() if "A1.x" in str(names))
            ready["N.o"] += NORMED_AFTER
        for link in "xyz":
            able = [
                (entry[2], name)
                for name, entry in waiting.items()
                if entry[0] == link
                and busy.get(link, 0) <= now
                and ready.get(entry[1], 1 << 30) <= now
            ]
            if able:
                name = min(able)[1]
                length = waiting.pop(name)[3]
                step.append(name)
                busy[link] = now + length
                ready[name] = now + (LAG if length == 1 else length)
                arrivals.setdefault(ready[name], []).append(name)
                for made in makes.get(name, []):
                    ready[made] = ready[name]
                if name.startswith("A1") and name[3] in "pq":
                    pair = (f"A1.p{name[4:]}", f"A1.q{name[4:]}")
                    if pair[0] in ready and pair[1] in ready:
                        ready[f"A1.b{name[4:]}"] = max(ready[p] for p in pair)
        steps.append(step)
        now += 1
    return steps, arrivals


def tie(values, others, flops=STEP_FLOPS):
    def kernel(*refs):
        pass

    spec = pl.BlockSpec(memory_space=pltpu.HBM)
    n = len(values)
    return pl.pallas_call(
        kernel,
        out_shape=[jax.ShapeDtypeStruct(v.shape, v.dtype) for v in values],
        in_specs=[spec] * (n + len(others)),
        out_specs=[spec] * n,
        input_output_aliases={i: i for i in range(n)},
        cost_estimate=pl.CostEstimate(flops=flops, transcendentals=0, bytes_accessed=0),
    )(*values, *others)


def bring(blocks, place_ref, target, sems):
    total = sum(block.shape[0] for block in blocks)
    rows = total // place_ref.shape[0]
    copies = []
    for block in blocks:
        for start in range(0, block.shape[0], rows):
            i = len(copies)
            to = pl.multiple_of(place_ref[i] * rows, math.gcd(rows, 16))
            copies.append(
                pltpu.make_async_copy(
                    block.at[pl.ds(start, rows)], target.at[pl.ds(to, rows)], sems.at[i]
                )
            )
    return copies


HBM = pl.BlockSpec(memory_space=pl.ANY)
VMEM = pl.BlockSpec(memory_space=pltpu.VMEM)
SMEM = pl.BlockSpec(memory_space=pltpu.SMEM)


def nt(left, right):
    return lax.dot_general(left, right, (((1,), (1,)), ((), ())), preferred_element_type=F32)


def turn(upright, cos_ref, sin_ref, sign, row):
    half = HEAD_DIM // 2
    first, second = upright[row : row + half], upright[row + half : row + 2 * half]
    cos, sin = cos_ref[...], sin_ref[...] * sign
    return jnp.concatenate([first * cos - second * sin, second * cos + first * sin], axis=0)


def queries_and_keys(places, blocks, normed, low_query, low_key, second_query, second_key, cos, sin):
    count = len(blocks)
    tokens, width = normed.shape
    cols = blocks[0].shape[1]
    q_cols, k_cols = second_query.shape[1], second_key.shape[1]

    def kernel(place_ref, x_ref, lq_ref, lk_ref, sq_ref, sk_ref, cos_ref, sin_ref, *refs):
        parts, (q_out, k_out, w_out, w_s, sems, sem_out) = refs[:count], refs[count:]
        copies = bring(parts, place_ref, w_s, sems)
        for copy in copies:
            copy.start()
        for copy in copies:
            copy.wait()
        keep = pltpu.make_async_copy(w_s, w_out, sem_out)
        keep.start()
        x = x_ref[...]
        step = 4 * HEAD_DIM
        for start, low, second, out, shift in [
            (at, lq_ref, sq_ref, q_out, 0) for at in range(0, q_cols, step)
        ] + [(q_cols + at, lk_ref, sk_ref, k_out, q_cols) for at in range(0, k_cols, step)]:
            own = start - shift
            part = jnp.dot(x, w_s[:, start : start + step], preferred_element_type=F32)
            part += jnp.dot(low[...], second[:, own : own + step], preferred_element_type=F32)
            upright = part.T
            for row in range(0, step, HEAD_DIM):
                out[own + row : own + row + HEAD_DIM, :] = turn(
                    upright, cos_ref, sin_ref, 1.0, row
                ).astype(BF)
        keep.wait()

    return pl.pallas_call(
        kernel,
        out_shape=[
            jax.ShapeDtypeStruct((q_cols, tokens), BF),
            jax.ShapeDtypeStruct((k_cols, tokens), BF),
            jax.ShapeDtypeStruct((width, cols), BF),
        ],
        in_specs=[SMEM] + [VMEM] * 7 + [HBM] * count,
        out_specs=[VMEM, VMEM, HBM],
        scratch_shapes=[
            pltpu.VMEM((width, cols), BF),
            pltpu.SemaphoreType.DMA((places.shape[0],)),
            pltpu.SemaphoreType.DMA,
        ],
        compiler_params=pltpu.CompilerParams(vmem_limit_bytes=48 * 2**20),
        cost_estimate=pl.CostEstimate(
            flops=2 * tokens * width * cols, transcendentals=0, bytes_accessed=4 * width * cols
        ),
    )(places, normed, low_query, low_key, second_query, second_key, cos, sin, *blocks)


def seen(rows, columns, row_start, column_start):
    key = lax.broadcasted_iota(jnp.int32, (rows, columns), 0)
    query = lax.broadcasted_iota(jnp.int32, (rows, columns), 1)
    causal = key <= query
    if row_start >= PROMPT:
        causal = causal & (key // CONT_LEN == query // CONT_LEN)
    return causal


def attention(places, blocks, normed, low_value, second_value, query, key, in_output):
    count = len(blocks)
    tokens, width = normed.shape
    cols = blocks[0].shape[1]
    q_cols, k_cols = query.shape[0], key.shape[0]
    kv_heads = k_cols // HEAD_DIM
    group = q_cols // k_cols
    scale = 1.0 / math.sqrt(HEAD_DIM)

    def kernel(place_ref, x_ref, lv_ref, sv_ref, q_ref, k_ref, io_ref, *refs):
        parts = refs[:count]
        v_out, att_out, lse_out, branch_out, low_out, w_out, w_s, att_s, sems, sem_out = refs[count:]
        copies = bring(parts, place_ref, w_s, sems)
        for copy in copies:
            copy.start()
        for copy in copies:
            copy.wait()
        keep = pltpu.make_async_copy(w_s, w_out, sem_out)
        keep.start()
        value = jnp.dot(x_ref[...], w_s[:, q_cols:cols], preferred_element_type=F32)
        value += jnp.dot(lv_ref[...], sv_ref[...], preferred_element_type=F32)
        v_out[...] = value.T.astype(BF)
        seen_first = seen(PROMPT, PROMPT, 0, 0)
        seen_second = seen(tokens - PROMPT, tokens - PROMPT, PROMPT, PROMPT)

        def one_head(g, _):
            k_rows = pl.ds(pl.multiple_of(g * HEAD_DIM, 16), HEAD_DIM)
            keys = k_ref[k_rows, :].T
            values = v_out[k_rows, :]
            for h in range(group):
                rows = pl.ds(pl.multiple_of((g * group + h) * HEAD_DIM, 16), HEAD_DIM)
                head = q_ref[rows, :]
                early = jnp.dot(keys[:PROMPT], head[:, :PROMPT], preferred_element_type=F32)
                late = jnp.dot(keys, head[:, PROMPT:], preferred_element_type=F32)
                early = jnp.where(seen_first, early * scale, -1e30)
                late_prompt = late[:PROMPT] * scale
                late_own = jnp.where(seen_second, late[PROMPT:] * scale, -1e30)
                top = jnp.max(early, axis=0, keepdims=True)
                expo = jnp.exp(early - top)
                total = jnp.sum(expo, axis=0, keepdims=True)
                prob = (expo * (1.0 / total)).astype(BF)
                lse_out[g, h : h + 1, :PROMPT] = top + jnp.log(total)
                att_s[rows, :PROMPT] = jnp.dot(
                    values[:, :PROMPT], prob, preferred_element_type=F32
                ).astype(BF)
                top = jnp.maximum(
                    jnp.max(late_prompt, axis=0, keepdims=True),
                    jnp.max(late_own, axis=0, keepdims=True),
                )
                expo_p, expo_o = jnp.exp(late_prompt - top), jnp.exp(late_own - top)
                total = jnp.sum(expo_p, axis=0, keepdims=True) + jnp.sum(
                    expo_o, axis=0, keepdims=True
                )
                inverse = 1.0 / total
                prob = jnp.concatenate(
                    [(expo_p * inverse).astype(BF), (expo_o * inverse).astype(BF)], axis=0
                )
                lse_out[g, h : h + 1, PROMPT:] = top + jnp.log(total)
                att_s[rows, PROMPT:] = jnp.dot(
                    values, prob, preferred_element_type=F32
                ).astype(BF)
            return 0

        lax.fori_loop(0, kv_heads, one_head, 0)
        att_out[...] = att_s[...].T
        attended = att_out[...]
        low_out[...] = jnp.dot(attended, io_ref[...], preferred_element_type=F32)
        for at in range(0, width, 512):
            branch_out[:, at : at + 512] = nt(attended, w_s[at : at + 512, :q_cols]).astype(BF)
        keep.wait()

    return pl.pallas_call(
        kernel,
        out_shape=[
            jax.ShapeDtypeStruct((k_cols, tokens), BF),
            jax.ShapeDtypeStruct((tokens, q_cols), BF),
            jax.ShapeDtypeStruct((kv_heads, group, tokens), F32),
            jax.ShapeDtypeStruct((tokens, width), BF),
            jax.ShapeDtypeStruct((tokens, in_output.shape[1]), F32),
            jax.ShapeDtypeStruct((width, cols), BF),
        ],
        in_specs=[SMEM] + [VMEM] * 6 + [HBM] * count,
        out_specs=[VMEM] * 5 + [HBM],
        scratch_shapes=[
            pltpu.VMEM((width, cols), BF),
            pltpu.VMEM((q_cols, tokens), BF),
            pltpu.SemaphoreType.DMA((places.shape[0],)),
            pltpu.SemaphoreType.DMA,
        ],
        compiler_params=pltpu.CompilerParams(vmem_limit_bytes=48 * 2**20),
        cost_estimate=pl.CostEstimate(
            flops=4 * tokens * width * cols, transcendentals=0, bytes_accessed=4 * width * cols
        ),
    )(places, normed, low_value, second_value, query, key, in_output, *blocks)


def attention_back(
    core, halves, select, second_output, low_output, attended, in_output, full_a0, full_a1, query,
    key, value, lse, cos, sin, second_query, second_key, second_value, low_query, low_key, low_value,
):
    half_tokens, width = halves[0].shape
    tokens = 2 * half_tokens
    cols = full_a0.shape[1]
    q_cols, k_cols = query.shape[0], key.shape[0]
    rank = second_query.shape[0]
    kv_heads = k_cols // HEAD_DIM
    group = q_cols // k_cols
    scale = 1.0 / math.sqrt(HEAD_DIM)

    def kernel(
        core_ref, mine_hbm, other_hbm, sel_ref, so_ref, lo_ref, att_ref, io_ref, a0_hbm, a1_hbm, q_ref, k_ref, v_ref, lse_ref, cos_ref, sin_ref,
        sq_ref, sk_ref, sv_ref, lq_ref, lk_ref, lv_ref, back_out, low_out, factor_out, a0, a1, gb_ref, glo_ref, ga_s, g_s, gw_s, sems,
    ):
        mine = core_ref[0]
        copies = [
            pltpu.make_async_copy(a1_hbm, a1, sems.at[0]),
            pltpu.make_async_copy(a0_hbm, a0, sems.at[1]),
            pltpu.make_async_copy(
                mine_hbm, gb_ref.at[pl.ds(pl.multiple_of(mine * half_tokens, 16), half_tokens)], sems.at[2]
            ),
            pltpu.make_async_copy(
                other_hbm,
                gb_ref.at[pl.ds(pl.multiple_of((1 - mine) * half_tokens, 16), half_tokens)],
                sems.at[3],
            ),
        ]
        for i in (2, 3, 0, 1):
            copies[i].start()
        for i in (2, 3):
            copies[i].wait()
        glo_ref[...] = (adapter_scale * nt(gb_ref[...], so_ref[...]) * sel_ref[...]).astype(BF)
        at_second = q_cols + 2 * k_cols
        at_first = at_second + width // 2
        factor_out[at_first : at_first + q_cols, :] = jnp.dot(
            att_ref[...].T, glo_ref[...], preferred_element_type=F32
        ).astype(BF)
        own = gb_ref[:, pl.ds(pl.multiple_of(mine * (width // 2), 128), width // 2)]
        factor_out[at_second:at_first, :] = (
            adapter_scale * jnp.dot(own.T, lo_ref[...], preferred_element_type=F32)
        ).astype(BF)
        factor_out[at_first + q_cols :, :] = jnp.zeros(
            (4 * q_cols - at_first - q_cols, rank), BF
        )
        copies[0].wait()
        step = 4 * HEAD_DIM
        for at in range(0, q_cols, step):
            part = jnp.dot(gb_ref[...], a1[:, at : at + step], preferred_element_type=F32)
            part += nt(glo_ref[...], io_ref[at : at + step, :])
            ga_s[at : at + step, :] = part.astype(BF).T
        seen_first = seen(PROMPT, PROMPT, 0, 0)
        seen_second = seen(tokens - PROMPT, tokens - PROMPT, PROMPT, PROMPT)

        def one_head(g, _):
            k_rows = pl.ds(pl.multiple_of(g * HEAD_DIM, 16), HEAD_DIM)
            keys_up = k_ref[k_rows, :]
            keys = keys_up.T
            values = v_ref[k_rows, :].T
            grad_k, grad_v = [0.0, 0.0], [0.0, 0.0]
            for h in range(group):
                rows = pl.ds(pl.multiple_of((g * group + h) * HEAD_DIM, 16), HEAD_DIM)
                head, grad = q_ref[rows, :], ga_s[rows, :]
                lse_h = lse_ref[g, h : h + 1, :]
                score = jnp.dot(keys[:PROMPT], head[:, :PROMPT], preferred_element_type=F32)
                prob = jnp.where(seen_first, jnp.exp(score * scale - lse_h[:, :PROMPT]), 0.0)
                grad_prob = jnp.dot(values[:PROMPT], grad[:, :PROMPT], preferred_element_type=F32)
                row_term = jnp.sum(prob * grad_prob, axis=0, keepdims=True)
                grad_score = (prob * (grad_prob - row_term)).astype(BF)
                prob = prob.astype(BF)
                grad_q_early = jnp.dot(
                    keys_up[:, :PROMPT], grad_score, preferred_element_type=F32
                )
                grad_v[0] += nt(grad[:, :PROMPT], prob)
                grad_k[0] += nt(head[:, :PROMPT], grad_score)
                score = jnp.dot(keys, head[:, PROMPT:], preferred_element_type=F32)
                expo = jnp.exp(score * scale - lse_h[:, PROMPT:])
                prob_p = expo[:PROMPT]
                prob_o = jnp.where(seen_second, expo[PROMPT:], 0.0)
                grad_prob = jnp.dot(values, grad[:, PROMPT:], preferred_element_type=F32)
                row_term = jnp.sum(prob_p * grad_prob[:PROMPT], axis=0, keepdims=True) + jnp.sum(
                    prob_o * grad_prob[PROMPT:], axis=0, keepdims=True
                )
                score_p = (prob_p * (grad_prob[:PROMPT] - row_term)).astype(BF)
                score_o = (prob_o * (grad_prob[PROMPT:] - row_term)).astype(BF)
                grad_q_late = jnp.dot(
                    keys_up, jnp.concatenate([score_p, score_o], axis=0), preferred_element_type=F32
                )
                grad_v[0] += nt(grad[:, PROMPT:], prob_p.astype(BF))
                grad_v[1] += nt(grad[:, PROMPT:], prob_o.astype(BF))
                grad_k[0] += nt(head[:, PROMPT:], score_p)
                grad_k[1] += nt(head[:, PROMPT:], score_o)
                grad_q = jnp.concatenate([grad_q_early, grad_q_late], axis=1) * scale
                g_s[rows, :] = turn(grad_q, cos_ref, sin_ref, -1.0, 0).astype(BF)
            grad_key = jnp.concatenate(grad_k, axis=1) * scale
            g_s[pl.ds(pl.multiple_of(q_cols + g * HEAD_DIM, 16), HEAD_DIM), :] = turn(
                grad_key, cos_ref, sin_ref, -1.0, 0
            ).astype(BF)
            g_s[pl.ds(pl.multiple_of(q_cols + k_cols + g * HEAD_DIM, 16), HEAD_DIM), :] = (
                jnp.concatenate(grad_v, axis=1).astype(BF)
            )
            return 0

        lax.fori_loop(0, kv_heads, one_head, 0)
        gw_s[...] = g_s[...].T
        for at, size, low in (
            (0, q_cols, lq_ref),
            (q_cols, k_cols, lk_ref),
            (q_cols + k_cols, k_cols, lv_ref),
        ):
            factor_out[at : at + size, :] = jnp.dot(
                g_s[at : at + size, :], low[...], preferred_element_type=F32
            ).astype(BF)
        for i, (at, size, second) in enumerate(
            ((0, q_cols, sq_ref), (q_cols, k_cols, sk_ref), (q_cols + k_cols, k_cols, sv_ref))
        ):
            low_out[:, i * rank : (i + 1) * rank] = adapter_scale * nt(
                gw_s[:, at : at + size], second[...]
            )
        copies[1].wait()
        for at in range(0, width, 512):
            rows = slice(at, at + 512)
            part = nt(gw_s[:, :cols], a0[rows, :]) + nt(gw_s[:, cols:], a1[rows, q_cols:])
            back_out[:, rows] = part.astype(BF)

    return pl.pallas_call(
        kernel,
        out_shape=[
            jax.ShapeDtypeStruct((tokens, width), BF),
            jax.ShapeDtypeStruct((tokens, 3 * rank), F32),
            jax.ShapeDtypeStruct((4 * q_cols, rank), BF),
        ],
        in_specs=[SMEM, HBM, HBM] + [VMEM] * 5 + [HBM] * 2 + [VMEM] * 12,
        out_specs=[VMEM] * 3,
        scratch_shapes=[
            pltpu.VMEM((width, cols), BF),
            pltpu.VMEM((width, cols), BF),
            pltpu.VMEM((tokens, width), BF),
            pltpu.VMEM((tokens, rank), BF),
            pltpu.VMEM((q_cols, tokens), BF),
            pltpu.VMEM((q_cols + 2 * k_cols, tokens), BF),
            pltpu.VMEM((tokens, q_cols + 2 * k_cols), BF),
            pltpu.SemaphoreType.DMA((4,)),
        ],
        compiler_params=pltpu.CompilerParams(vmem_limit_bytes=56 * 2**20),
        cost_estimate=pl.CostEstimate(
            flops=20 * tokens * width * cols, transcendentals=0, bytes_accessed=4 * width * cols
        ),
    )(
        core, *halves, select, second_output, low_output, attended, in_output, full_a0, full_a1, query,
        key, value, lse, cos, sin, second_query, second_key, second_value, low_query, low_key, low_value,
    )


def after_attention(
    hidden, branches, branch_lows, select, second_output, gain, mlp_in
):
    tokens, width = hidden.shape
    rank = select.shape[1]
    tile = 128

    def kernel(h_ref, b0, b1, l0, l1, sel_ref, so_ref, gain_ref, in_ref, mid_out, ext_out, low_out):
        def one(t, _):
            r = pl.ds(pl.multiple_of(t * tile, tile), tile)
            sel = sel_ref[r, :]
            low = ((l0[r, :] + l1[r, :]) * sel).astype(BF)
            low_out[r, :] = low
            middle = h_ref[r, :].astype(F32) + (b0[r, :].astype(F32) + b1[r, :].astype(F32))
            middle += adapter_scale * jnp.dot(low, so_ref[...], preferred_element_type=F32)
            mid_out[r, :] = middle
            scale = lax.rsqrt(jnp.mean(middle * middle, axis=1, keepdims=True) + norm_eps)
            normed = (middle * scale * gain_ref[...]).astype(BF)
            ext_out[r, :width] = normed
            part = jnp.dot(normed, in_ref[...], preferred_element_type=F32)
            part = (part * jnp.concatenate([sel, sel], axis=1)).astype(BF)
            ext_out[r, width:] = part * jnp.array(adapter_scale, BF)
            return 0

        lax.fori_loop(0, tokens // tile, one, 0)

    return pl.pallas_call(
        kernel,
        out_shape=[
            jax.ShapeDtypeStruct((tokens, width), F32),
            jax.ShapeDtypeStruct((tokens, width + 2 * rank), BF),
            jax.ShapeDtypeStruct((tokens, rank), BF),
        ],
        in_specs=[VMEM] * 9,
        out_specs=[VMEM] * 3,
        compiler_params=pltpu.CompilerParams(vmem_limit_bytes=40 * 2**20),
        cost_estimate=pl.CostEstimate(
            flops=6 * tokens * width * rank, transcendentals=0, bytes_accessed=14 * tokens * width
        ),
    )(hidden, *branches, *branch_lows, select, second_output, gain, mlp_in)


def after_feed_forward(core, parts, middle, cotangent, select, gain, mlp_in):
    half, wide = parts[0].shape
    tokens, width = middle.shape
    rank = select.shape[1]
    tile = 128

    def kernel(
        core_ref, p0, p1, p2, mid_hbm, cot_hbm, sel_ref, gain_ref, in_ref, mid_out, branch_out, low_out,
        mid_s, cot_s, sems,
    ):
        start = pl.multiple_of(core_ref[0] * half, 16)
        copies = [
            pltpu.make_async_copy(mid_hbm.at[pl.ds(start, half)], mid_s, sems.at[0]),
            pltpu.make_async_copy(cot_hbm.at[pl.ds(start, half)], cot_s, sems.at[1]),
        ]
        for copy in copies:
            copy.start()
        for copy in copies:
            copy.wait()

        def one(t, _):
            r = pl.ds(pl.multiple_of(t * tile, tile), tile)
            sel = sel_ref[pl.ds(pl.multiple_of(start + t * tile, tile), tile), :]
            total = p0[r, :].astype(F32) + p1[r, :].astype(F32) + p2[r, :].astype(F32)
            low = (
                adapter_scale * total[:, width:] * jnp.concatenate([sel, sel], axis=1)
            ).astype(BF)
            low_out[r, :] = low
            grad = (total[:, :width] + nt(low, in_ref[...])) * gain_ref[...]
            middle = mid_s[r, :]
            scale = lax.rsqrt(jnp.mean(middle * middle, axis=1, keepdims=True) + norm_eps)
            inner = jnp.mean(middle * grad, axis=1, keepdims=True)
            out = cot_s[r, :].astype(F32) + scale * grad - middle * (scale * scale * scale * inner)
            mid_out[r, :] = out
            branch_out[r, :] = out.astype(BF)
            return 0

        lax.fori_loop(0, half // tile, one, 0)

    return pl.pallas_call(
        kernel,
        out_shape=[
            jax.ShapeDtypeStruct((half, width), F32),
            jax.ShapeDtypeStruct((half, width), BF),
            jax.ShapeDtypeStruct((half, 2 * rank), BF),
        ],
        in_specs=[SMEM] + [VMEM] * 3 + [HBM] * 2 + [VMEM] * 3,
        out_specs=[VMEM] * 3,
        scratch_shapes=[
            pltpu.VMEM((half, width), F32),
            pltpu.VMEM((half, width), BF),
            pltpu.SemaphoreType.DMA((2,)),
        ],
        compiler_params=pltpu.CompilerParams(vmem_limit_bytes=40 * 2**20),
        cost_estimate=pl.CostEstimate(
            flops=6 * half * width * rank, transcendentals=0, bytes_accessed=20 * half * width
        ),
    )(core, *parts, middle, cotangent, select, gain, mlp_in)


def feed_forward(places, core, normed, cot, new, old, totals, last):
    sums = totals != "none"
    first = totals is None
    before = list(totals) if sums and not first else []
    n_new, n_old = len(new), len(old)
    blocks = [list(unit[-1]) for unit in new + old]
    factors = [unit[-2] for unit in new + old]
    count, per = len(blocks), len(blocks[0])
    part_rows, wide = blocks[0][0].shape
    group, n_wide = normed[0].shape
    c_wide = cot[0].shape[1]
    rank = n_wide - c_wide
    width = c_wide - rank
    rows = 2 * group
    tile = group // 2
    tiles = rows // tile
    flat = [v for unit, factor in zip(blocks, factors) for v in unit + [factor]]
    old_flat = [v for unit in old for v in unit[:2]]
    n_sums = (4 if last else 2) if sums else 0

    def kernel(place_ref, core_ref, *refs):
        it = iter(refs)

        def take(n):
            return [next(it) for _ in range(n)]

        old_ref = take(2 * n_old)
        normed_hbm, cot_hbm = take(3), take(3)
        block_hbm = [take(per + 1) for _ in range(count)]
        before_hbm = take(len(before))
        sum_hbm = take(n_sums)
        act_ref, grad_ref, own_ref = (take(n_new) for _ in range(3))
        w_s, sem_w = take(2)
        if n_new:
            normed_s, cot_s, sem_x = take(3)
        if sums:
            acc_g, acc_o, sem_t, sem_out = take(4)
            fin_g, fin_o = (normed_s, cot_s) if last else (acc_g, acc_o)
        mine = core_ref[0]

        def fetch(k):
            slot = w_s.at[k % 2]
            return bring(block_hbm[k][:per], place_ref, slot, sem_w.at[k % 2]) + [
                pltpu.make_async_copy(
                    block_hbm[k][per], slot.at[pl.ds(width, 2 * rank)], sem_w.at[k % 2, places.shape[0]]
                )
            ]

        def load_x(t):
            copies = []
            for i, (src, dst) in enumerate(((normed_hbm, normed_s), (cot_hbm, cot_s))):
                if t < 2:
                    part, to = src[0].at[pl.ds(t * tile, tile)], t * tile
                else:
                    part = src[t - 1]
                    to = group + tile * (mine if t == 2 else 1 - mine)
                    to = pl.multiple_of(to, 16)
                copies.append(pltpu.make_async_copy(part, dst.at[pl.ds(to, tile)], sem_x.at[i, t]))
            return copies

        def load_t(t):
            r = pl.ds(t * tile, tile)
            return [
                pltpu.make_async_copy(src.at[r], dst.at[r], sem_t.at[i, t])
                for i, (src, dst) in enumerate(zip(before_hbm, (acc_g, acc_o)))
            ]

        def store_t(t, to):
            r = pl.ds(t * tile, tile)
            copies = []
            for i, src in enumerate((fin_g, fin_o)):
                dst = sum_hbm[2 * i + to].at[t // 2] if last else sum_hbm[i].at[r]
                copies.append(pltpu.make_async_copy(src.at[r], dst, sem_out.at[i, t]))
            return copies

        if n_new:
            for copy in load_x(0):
                copy.start()
        for copy in fetch(0):
            copy.start()
        if n_new:
            for copy in fetch(0):
                copy.wait()
            for t in range(1, tiles):
                for copy in load_x(t):
                    copy.start()
        if before:
            for t in range(tiles):
                for copy in load_t(t):
                    copy.start()
        for k in range(count):
            if k + 1 < count:
                for copy in fetch(k + 1):
                    copy.start()
            if k or not n_new:
                for copy in fetch(k):
                    copy.wait()
            slot = k % 2
            if k < n_new:
                act, grad = act_ref[k], grad_ref[k]
                for t in range(tiles):
                    r = pl.ds(t * tile, tile)
                    if k == 0 and t < 2:
                        for copy in load_x(t):
                            copy.wait()
                    if k == 0 and t == 2:
                        for copy in load_x(2) + load_x(3):
                            copy.wait()
                    x = normed_s[r, :]
                    gate = jnp.dot(x, w_s[slot, :, 0:WIDTH], preferred_element_type=F32)
                    up = jnp.dot(x, w_s[slot, :, WIDTH : 2 * WIDTH], preferred_element_type=F32)
                    back = jnp.dot(
                        cot_s[r, :],
                        w_s[slot, :c_wide, 2 * WIDTH : 3 * WIDTH],
                        preferred_element_type=F32,
                    )
                    sig = 1.0 / (1.0 + jnp.exp(-gate))
                    silu = gate * sig
                    act[r, :] = (silu * up).astype(BF)
                    grad[r, :WIDTH] = (back * up * (sig * (1.0 + gate * (1.0 - sig)))).astype(BF)
                    grad[r, WIDTH:] = (back * silu).astype(BF)
                low = normed_s[:, width:].T
                for part in range(2):
                    second = jnp.dot(
                        low[part * rank : (part + 1) * rank],
                        grad[:, part * WIDTH : (part + 1) * WIDTH],
                        preferred_element_type=F32,
                    ).astype(BF)
                    for at in range(0, WIDTH, rank):
                        to = part * WIDTH + at
                        own_ref[k][to : to + rank, :] = second[:, at : at + rank]
                own_ref[k][2 * WIDTH :, :] = jnp.dot(
                    act[...].T, cot_s[:, width:c_wide], preferred_element_type=F32
                ).astype(BF)
            else:
                act, grad = old_ref[2 * (k - n_new)], old_ref[2 * (k - n_new) + 1]
            if not sums:
                continue
            for t in range(tiles):
                r = pl.ds(t * tile, tile)
                if before and k == 0:
                    for copy in load_t(t):
                        copy.wait()
                for acc, fin, val, lo, hi, top in (
                    (acc_g, fin_g, grad, 0, 2 * WIDTH, n_wide),
                    (acc_o, fin_o, act, 2 * WIDTH, 3 * WIDTH, c_wide),
                ):
                    for at in range(0, top, 512):
                        n = slice(at, min(at + 512, top))
                        part = nt(val[r, :], w_s[slot, n, lo:hi])
                        if k or not first:
                            part = acc[r, n] + part
                        if k == count - 1:
                            fin[r, n] = part.astype(fin.dtype)
                        else:
                            acc[r, n] = part
                if k == count - 1 and last:
                    side = mine if t % 2 == 0 else 1 - mine
                    for to in range(2):

                        @pl.when(side == to)
                        def _():
                            for copy in store_t(t, to):
                                copy.start()

                elif k == count - 1:
                    for copy in store_t(t, 0):
                        copy.start()
        if sums:
            for t in range(tiles):
                for copy in store_t(t, 0):
                    copy.wait()

    scratch = [
        pltpu.VMEM((2, n_wide, wide), BF),
        pltpu.SemaphoreType.DMA((2, places.shape[0] + 1)),
    ]
    if n_new:
        scratch += [
            pltpu.VMEM((rows, n_wide), BF),
            pltpu.VMEM((rows, c_wide), BF),
            pltpu.SemaphoreType.DMA((2, tiles)),
        ]
    out_shape = []
    if sums:
        scratch += [
            pltpu.VMEM((rows, n_wide), F32),
            pltpu.VMEM((rows, c_wide), F32),
            pltpu.SemaphoreType.DMA((2, tiles)),
            pltpu.SemaphoreType.DMA((2, tiles)),
        ]
        for columns in (n_wide, c_wide):
            if last:
                out_shape += [jax.ShapeDtypeStruct((2, tile, columns), BF)] * 2
            else:
                out_shape += [jax.ShapeDtypeStruct((rows, columns), F32)]
    out_shape += [jax.ShapeDtypeStruct((rows, WIDTH), BF)] * n_new
    out_shape += [jax.ShapeDtypeStruct((rows, 2 * WIDTH), BF)] * n_new
    out_shape += [jax.ShapeDtypeStruct((3 * WIDTH, rank), BF)] * n_new
    n_hbm = 6 + len(flat)
    at = 2 + len(old_flat) + n_hbm
    out = pl.pallas_call(
        kernel,
        out_shape=out_shape,
        in_specs=[SMEM] * 2 + [VMEM] * len(old_flat) + [HBM] * (n_hbm + len(before)),
        out_specs=[HBM] * n_sums + [VMEM] * (3 * n_new),
        scratch_shapes=scratch,
        input_output_aliases={at: 0, at + 1: 1} if before and not last else {},
        compiler_params=pltpu.CompilerParams(vmem_limit_bytes=60 * 2**20),
        cost_estimate=pl.CostEstimate(
            flops=6 * (n_new + (count if sums else 0)) * rows * width * WIDTH,
            transcendentals=n_new * rows * WIDTH,
            bytes_accessed=4 * rows * width,
        ),
    )(places, core, *old_flat, *normed, *cot, *flat, *before)
    rest = out[n_sums:]
    return tuple(out[:n_sums]), list(zip(*(rest[i * n_new : (i + 1) * n_new] for i in range(3))))
def adapter_columns(ids_ref):
    sequences = ids_ref.shape[1]
    shape = (sequences * RANK, ADAPTER_COLS)
    row = lax.broadcasted_iota(jnp.int32, shape, 0)
    column = lax.broadcasted_iota(jnp.int32, shape, 1)
    start = jnp.zeros(shape, jnp.int32)
    for i in range(sequences):
        start = jnp.where(row // RANK == i, ids_ref[0, i] * RANK, start)
    return (column == start + row % RANK).astype(F32).astype(BF)


def pack(ids, factors, firsts):
    block = factors.shape[0] // BLOCKS
    sequences = ids.shape[1]
    lanes = BLOCKS * sequences * RANK

    def kernel(ids_ref, factor_ref, first_ref, factor_out, first_out, chosen_out):
        chosen = adapter_columns(ids_ref)
        chosen_out[...] = jnp.concatenate(
            [chosen[i * RANK : (i + 1) * RANK] for i in range(sequences)], axis=1
        )
        parts = [
            nt(factor_ref[i * block : (i + 1) * block, :], chosen) for i in range(BLOCKS)
        ]
        factor_out[...] = jnp.concatenate(parts, axis=1).astype(BF)
        parts = []
        for i in range(BLOCKS):
            q, s = i // 2, i % 2
            parts.append(
                nt(
                    first_ref[s * block : (s + 1) * block, q * ADAPTER_COLS : (q + 1) * ADAPTER_COLS],
                    chosen,
                )
            )
        first_out[...] = jnp.concatenate(parts, axis=1).astype(BF)

    return pl.pallas_call(
        kernel,
        out_shape=[jax.ShapeDtypeStruct((block, lanes), BF)] * 2
        + [jax.ShapeDtypeStruct((RANK, sequences * ADAPTER_COLS), BF)],
        in_specs=[SMEM, VMEM, VMEM],
        out_specs=[VMEM] * 3,
        compiler_params=pltpu.CompilerParams(vmem_limit_bytes=32 * 2**20),
        cost_estimate=pl.CostEstimate(flops=5_000_000_000, transcendentals=0, bytes_accessed=0),
    )(ids, factors, firsts)


def unpack(got):
    groups, share, lanes = got.shape
    share -= RANK
    each = lanes // BLOCKS
    sequences = each // RANK

    def kernel(got_ref, out_ref, total):
        total[...] = jnp.zeros_like(total)

        def one(g, _):
            packed = got_ref[g]
            chosen = jnp.concatenate(
                [
                    packed[share:, i * ADAPTER_COLS : (i + 1) * ADAPTER_COLS]
                    for i in range(sequences)
                ],
                axis=0,
            )
            for i in range(BLOCKS):
                total[i] += jnp.dot(
                    packed[:share, i * each : (i + 1) * each], chosen, preferred_element_type=F32
                )
            return 0

        lax.fori_loop(0, groups, one, 0)
        out_ref[...] = total[...].astype(BF)

    return pl.pallas_call(
        kernel,
        out_shape=jax.ShapeDtypeStruct((BLOCKS, share, ADAPTER_COLS), BF),
        in_specs=[VMEM],
        out_specs=VMEM,
        scratch_shapes=[pltpu.VMEM((BLOCKS, share, ADAPTER_COLS), F32)],
        compiler_params=pltpu.CompilerParams(vmem_limit_bytes=32 * 2**20),
        cost_estimate=pl.CostEstimate(flops=5_000_000_000, transcendentals=0, bytes_accessed=0),
    )(got)


def unit_results(at, parts, order):
    ring, share, cols = parts[0].shape
    units = len(order) * WIDTH

    def kernel(at_ref, *refs):
        gate_out, up_out, down_out, all_s = refs[8:]
        for i in range(8):
            core = at_ref[0] if i < 4 else 1 - at_ref[0]
            bit_y = at_ref[1] if i // 2 % 2 == 0 else 1 - at_ref[1]
            bit_x = at_ref[2] if i % 2 == 0 else 1 - at_ref[2]

            def one(r, _):
                place = lax.rem(at_ref[3] + ring - r, ring) * 2 + bit_y
                to = pl.multiple_of(place * share, 8)
                all_s[core * 2 + bit_x, pl.ds(to, share), :] = refs[i][r].astype(F32)
                return 0

            lax.fori_loop(0, ring, one, 0)
        for q in range(4):
            for i, j in enumerate(order):
                start = q * units + j * WIDTH
                row = i * 3 * WIDTH
                for at in range(0, WIDTH, cols):
                    to = slice(start + at, start + at + cols)
                    gate_out[:, to] = all_s[q, row + at : row + at + cols, :]
                    at += WIDTH
                    up_out[:, to] = all_s[q, row + at : row + at + cols, :]
                row += 2 * WIDTH
                down_out[start : start + WIDTH, :] = all_s[q, row : row + WIDTH, :]

    return pl.pallas_call(
        kernel,
        out_shape=[
            jax.ShapeDtypeStruct((cols, 4 * units), F32),
            jax.ShapeDtypeStruct((cols, 4 * units), F32),
            jax.ShapeDtypeStruct((4 * units, cols), F32),
        ],
        in_specs=[SMEM] + [VMEM] * 8,
        out_specs=[VMEM] * 3,
        scratch_shapes=[pltpu.VMEM((4, 3 * units, cols), F32)],
        compiler_params=pltpu.CompilerParams(vmem_limit_bytes=48 * 2**20),
        cost_estimate=pl.CostEstimate(flops=8_000_000_000, transcendentals=0, bytes_accessed=0),
    )(at, *parts)


def other_results(at, parts, share, second_cols):
    ring, rows, cols = parts[0].shape
    chips = 4 * ring
    late_rows = BLOCKS * 2 * share
    pair_rows = (rows - late_rows) // 2
    block = chips * share
    half = 2 * block
    query_cols, key_cols = second_cols

    def kernel(at_ref, *refs):
        part_refs, outs = refs[:8], refs[8:19]
        query_s, pair_s, output_s, down_s = refs[19:]
        (
            in_q, second_q, in_k, second_k, in_v, second_v, in_o, second_o, in_g, in_u, second_d,
        ) = outs
        homes = (query_s, pair_s, output_s, in_o, None)
        for i in range(8):
            core = at_ref[0] if i < 4 else 1 - at_ref[0]
            bit_y = at_ref[1] if i // 2 % 2 == 0 else 1 - at_ref[1]
            bit_x = at_ref[2] if i % 2 == 0 else 1 - at_ref[2]

            def one(r, _):
                chip = lax.rem(at_ref[3] + ring - r, ring) * 4 + bit_y * 2 + bit_x
                found = part_refs[i][r].astype(F32)
                for b, (home, s) in enumerate(
                    ((query_s, 0), (query_s, 1), (pair_s, 0), (output_s, 0), (output_s, 1), (in_o, 0), (in_o, 1))
                ):
                    size = block if home is pair_s else half
                    to = pl.multiple_of(core * size + s * block + chip * share, 8)
                    home[pl.ds(to, share), :] = found[2 * b * share : (2 * b + 1) * share]
                for b in range(BLOCKS):
                    home, s = (in_q, in_k, in_v, down_s)[b // 2], b % 2
                    to = pl.multiple_of(core * half + s * block + chip * share, 8)
                    home[pl.ds(to, share), :] = found[(2 * b + 1) * share : (2 * b + 2) * share]
                for k, home in enumerate((in_g, in_u)):
                    to = pl.multiple_of(core * half + chip * pair_rows, 8)
                    start = late_rows + k * pair_rows
                    home[pl.ds(to, pair_rows), :] = found[start : start + pair_rows]
                return 0

            lax.fori_loop(0, ring, one, 0)
        second_q[...] = query_s[...].T
        second_o[...] = output_s[...].T
        second_d[...] = down_s[...].T
        both = pair_s[...].T
        for out, start in ((second_k, 0), (second_v, key_cols)):
            out[...] = jnp.concatenate(
                [both[:, c * block + start : c * block + start + key_cols] for c in range(2)], axis=1
            )

    width = 2 * half

    def shape(*dims):
        return jax.ShapeDtypeStruct(dims, F32)

    return pl.pallas_call(
        kernel,
        out_shape=[
            shape(width, cols), shape(cols, 2 * query_cols), shape(width, cols),
            shape(cols, 2 * key_cols), shape(width, cols), shape(cols, 2 * key_cols),
            shape(width, cols), shape(cols, width), shape(width, cols), shape(width, cols),
            shape(cols, width),
        ],
        in_specs=[SMEM] + [VMEM] * 8,
        out_specs=[VMEM] * 11,
        scratch_shapes=[
            pltpu.VMEM((width, cols), F32),
            pltpu.VMEM((half, cols), F32),
            pltpu.VMEM((width, cols), F32),
            pltpu.VMEM((width, cols), F32),
        ],
        compiler_params=pltpu.CompilerParams(vmem_limit_bytes=48 * 2**20),
        cost_estimate=pl.CostEstimate(flops=8_000_000_000, transcendentals=0, bytes_accessed=0),
    )(at, *parts)


DP = ("ring", "second", "first")


def make_body(n):
    ring_size = n // 4
    perms = ring_and_swaps(n)

    def move(value, link):
        return lax.ppermute(value, DP, perms[link])

    def other_core(value):
        return lax.ppermute(value, "tensor", [(0, 1), (1, 0)])

    def take(value, start, size, axis=0):
        return lax.dynamic_slice_in_dim(value, start, size, axis)

    def body(
        hidden_in, adapter_ids, attn_gain, mlp_gain, w_query, w_key, w_value, w_output, w_gate,
        w_up, w_down, in_query, second_query, in_key, second_key, in_value, second_value,
        in_output, second_output, in_gate, second_gate, in_up, second_up, in_down, second_down,
        cotangent,
    ):
        num_rows, width = hidden_in.shape
        half_rows = num_rows // 2
        half_width = width // 2
        rank_cols = in_query.shape[1]
        units = w_gate.shape[1] // 2
        chunks = units // WIDTH
        shard = w_query.shape[0]

        ring_at, bit_y, bit_x = (lax.axis_index(name) for name in DP)
        core = lax.axis_index("tensor")
        core_at = core.astype(jnp.int32).reshape(1)
        bits = {"x": bit_x, "y": bit_y}

        def in_order(bit, value, received, axis=0):
            first = jnp.where(bit == 0, value, received)
            return jnp.concatenate([first, jnp.where(bit == 0, received, value)], axis=axis)

        def half_of(value):
            return take(value, core * half_rows, half_rows)

        def both_halves(value):
            return in_order(core, value, other_core(value))

        def cols_of_core(value):
            return take(value, core * half_width, half_width, 1)

        row_index = lax.iota(jnp.int32, num_rows)
        is_later = row_index >= PROMPT
        seq_of = jnp.where(is_later, 1 + (row_index - PROMPT) // CONT_LEN, 0)
        position = jnp.where(is_later, PROMPT + (row_index - PROMPT) % CONT_LEN, row_index)
        seq_ids = lax.iota(jnp.int32, adapter_ids.shape[1])
        row_adapter = jnp.sum(
            jnp.where(seq_of[:, None] == seq_ids[None, :], adapter_ids[0][None, :], 0), axis=1
        )
        select = (lax.iota(jnp.int32, rank_cols)[None, :] // RANK == row_adapter[:, None]).astype(F32)
        select_three = jnp.concatenate([select] * 3, axis=1)
        inv_freq = rope_base ** (-2.0 * lax.iota(F32, HEAD_DIM // 2) / HEAD_DIM)
        angles = inv_freq[:, None] * position.astype(F32)[None, :]
        cos_table, sin_table = jnp.cos(angles), jnp.sin(angles)
        attn_in = jnp.concatenate([in_query, in_key, in_value], axis=1)
        mlp_in = jnp.concatenate([in_gate, in_up], axis=1)
        attn_gain_f = attn_gain.astype(F32)
        mlp_gain_f = mlp_gain.astype(F32).reshape(1, width)
        two = jnp.array(adapter_scale, BF)

        unit_start = bit_x * units

        def half_units(start):
            return (
                take(w_gate, start, units, 1),
                take(w_up, start, units, 1),
                take(w_down, start, units, 0).T,
            )

        mine, others = half_units(unit_start), half_units(units - unit_start)

        def chunk_of(parts, j):
            return jnp.concatenate([p[:, j * WIDTH : (j + 1) * WIDTH] for p in parts], axis=1)

        factor_parts = (
            take(second_gate, unit_start, units, 1),
            take(second_up, unit_start, units, 1),
            take(in_down, unit_start, units, 0),
        )
        blank = jnp.zeros((rank_cols, WIDTH), BF)
        chunk_cols = 3 * WIDTH

        def factors_of(j):
            cols = slice(j * WIDTH, (j + 1) * WIDTH)
            gate, up, down = factor_parts
            upper = jnp.concatenate([gate[:, cols], blank, down[cols].T], axis=1)
            return jnp.concatenate(
                [upper, jnp.concatenate([blank, up[:, cols], blank], axis=1)], axis=0
            )

        grad_low_down = (
            adapter_scale * product_with_transpose(cotangent, second_down) * select
        ).astype(BF)
        cot_wide = jnp.concatenate([cotangent, grad_low_down], axis=1)

        held = {
            "A0.o": jnp.concatenate([w_query, w_key], axis=1),
            "A1.p0": jnp.concatenate([w_output.T, w_value], axis=1),
            "C.o": half_of(cot_wide),
        }
        groups = exchanges_of(chunks)
        for i, group in enumerate(groups):
            held[f"E{i}.o"] = jnp.concatenate([chunk_of(others, j) for j in group], axis=1)
        plan = plan_transfers(ring_size, chunks)
        steps, arrivals = schedule(plan, chunks)
        when = {name: s for s, names in arrivals.items() for name in names}
        last_step = len(steps) - 1

        def there(tag):
            return max(s for name, s in when.items() if name.split(".")[0] == tag)

        def pieces(tag):
            found, places = [], []
            for r in range(ring_size):
                ring = (ring_at - r + ring_size) % ring_size
                if tag[0] == "A":
                    for other in range(2):
                        found.append(held[f"{tag}.{'x' if other else 'b'}{r}"])
                        bit = 1 - bit_x if other else bit_x
                        places += [(ring * 2 + bit_y) * 2 + bit, (ring * 2 + 1 - bit_y) * 2 + bit]
                else:
                    for other in range(2):
                        name = f"{tag}.q{r}" if other else f"{tag}.p{r}" if r else tag
                        found.append(held[name])
                        pair = ring * 2 + (1 - bit_y if other else bit_y)
                        places += [pair * 2 + bit_x, pair * 2 + 1 - bit_x]
            places = jnp.stack(places).astype(jnp.int32)
            if shard % 16:
                whole = jnp.zeros((n, shard, found[0].shape[1]), BF)
                for i in range(n):
                    part = found[i // 2][(i % 2) * shard : (i % 2 + 1) * shard]
                    whole = lax.dynamic_update_slice(whole, part[None], (places[i], 0, 0))
                return [whole.reshape(n * shard, -1)], jnp.zeros((1,), jnp.int32)
            return found, places

        v = {}
        hidden_wide = hidden_in.astype(F32)
        normed_a = rms_norm(hidden_wide, attn_gain_f).astype(BF)
        low_attn = (matrix_product(normed_a, attn_in) * select_three).astype(BF)
        lows = [low_attn[:, i * rank_cols : (i + 1) * rank_cols] * two for i in range(3)]

        def start_attention():
            found, places = pieces("A0")
            v["query"], v["key"], v["a0"] = queries_and_keys(
                places, found, normed_a, lows[0], lows[1], second_query, second_key, cos_table,
                sin_table,
            )
            return [v["key"]]

        def finish_attention():
            found, places = pieces("A1")
            v["value"], v["attended"], v["lse"], branch, branch_low, v["a1"] = attention(
                places, found, normed_a, lows[2], second_value, v["query"], v["key"], in_output
            )
            v["branches"] = (branch, other_core(branch))
            v["branch_lows"] = (branch_low, other_core(branch_low))
            return [v["value"]]

        def start_feed_forward():
            v["middle"], v["normed"], v["low_output"] = after_attention(
                hidden_in, v["branches"], v["branch_lows"], select, second_output, mlp_gain_f, mlp_in
            )
            held["N.o"] = half_of(v["normed"])
            return [v["low_output"]]

        def meet_neighbour():
            v["normed_all"] = (v["normed"], held["N.x"], other_core(held["N.x"]))
            v["cot_all"] = (cot_wide, held["C.x"], other_core(held["C.x"]))
            return [v["normed_all"][2], v["cot_all"][2]]

        unit_out = {}

        def feed(new, old, totals, last, core_at=core_at):
            found = {j: pieces(f"M{j}") for j in new + old}
            sums, results = feed_forward(
                found[(new + old)[0]][1],
                core_at,
                v["normed_all"],
                v["cot_all"],
                [(factors_of(j), found[j][0]) for j in new],
                [unit_out[j][:2] + (factors_of(j), found[j][0]) for j in old],
                totals,
                last,
            )
            unit_out.update(zip(new, results))
            return sums

        def units_only(new):
            def run():
                feed(new, [], "none", False)
                return [unit_out[new[-1]][0]]

            return run

        order = sorted(range(chunks), key=lambda j: there(f"M{j}"))
        events = {}

        def at_step(s, run):
            events.setdefault(min(s, last_step), []).append(run)

        at_step(there("A0"), start_attention)
        at_step(there("A1"), finish_attention)
        at_step(there("A1") + NORMED_AFTER - 1, start_feed_forward)
        begin = there("N")
        at_step(begin, meet_neighbour)
        early, later, final = order[: chunks - 3], order[chunks - 3 : chunks - 1], order[-1]
        at = begin
        for i in range(0, len(early), 2):
            pair = early[i : i + 2]
            at = max([at] + [there(f"M{j}") for j in pair])
            at_step(at, units_only(pair))
            at += 1
        for j in later:
            at_step(max(at, there(f"M{j}")), units_only([j]))

        waits = []
        for s, step in enumerate(steps):
            sources = sorted({plan[name][1] for name in step})
            if s:
                arrived = [name for name in arrivals.get(s, []) if name not in sources]
                if sources and arrived + waits:
                    tied = tie([held[k] for k in sources], [held[k] for k in arrived] + waits)
                    held.update(zip(sources, tied))
                    waits = []
            for name in step:
                held[name] = move(held[plan[name][1]], plan[name][0])
            for name in arrivals.get(s + 1, []):
                if name.endswith(".e"):
                    for i, j in enumerate(groups[int(name[1:-2])]):
                        got = held[name][:, i * chunk_cols : (i + 1) * chunk_cols]
                        held[f"M{j}"] = jnp.concatenate([chunk_of(mine, j), got], axis=0)
                elif name == "A0.y":
                    held["A0.b0"] = jnp.concatenate([held["A0.o"], held[name]], axis=0)
                elif name.startswith("A1") and name[3] in "pq":
                    pair = [f"A1.{side}{name[4:]}" for side in "pq"]
                    if f"A1.b{name[4:]}" not in held and all(p in held for p in pair):
                        if max(when.get(p, 0) for p in pair) <= s + 1:
                            held[f"A1.b{name[4:]}"] = jnp.concatenate([held[p] for p in pair], axis=0)
            for run in events.get(s, []):
                waits += run()

        own = jnp.concatenate([unit_out[j][2] for j in order[:-1]], axis=0)
        totals = feed([final], early + later, None, True, tie([core_at], [own], 0)[0])
        grad_keep, grad_send, out_keep, out_send = totals

        def after(values, *others):
            return tie(list(values), list(others), 0)

        def total(parts):
            return jnp.sum(parts.astype(F32), axis=0).astype(BF)

        own = jnp.concatenate([own, unit_out[final][2]], axis=0)
        grad_got = other_core(grad_send)
        grad_out = (grad_keep[1].astype(F32) + grad_got[1].astype(F32)).astype(BF)
        grad_own = tie([grad_keep[0]], [grad_out])[0]
        own = after([own], grad_own)[0]
        grad_in_parts = (grad_own, grad_got[0], move(grad_out, "x"))
        out_send = after([out_send], grad_out)[0]
        out_got = other_core(out_send)
        out_out = (out_keep[1].astype(F32) + out_got[1].astype(F32)).astype(BF)
        got_units = lax.all_to_all(own.reshape(n // 2, -1, rank_cols), DP[:2], 0, 0)

        grad_middle, grad_branch, grad_low_mlp = after_feed_forward(
            core_at, grad_in_parts, v["middle"], cotangent, select, mlp_gain_f, mlp_in
        )
        out_in = move(after([out_out], grad_branch)[0], "x")
        grad_branch_other = other_core(grad_branch)
        grad_low_mlp = both_halves(grad_low_mlp)
        delta_mlp = transpose_then_product(
            cols_of_core(v["normed"][:, :width]), grad_low_mlp
        ).astype(BF)
        got_mlp = lax.all_to_all(delta_mlp.reshape(n, half_width // n, 2 * rank_cols), DP, 0, 0)

        units_sum = [total(got_units)]
        units_sum += [move(units_sum[0], f"z{r}") for r in range(1, ring_size)]
        back, back_low, factors = attention_back(
            core_at, (grad_branch, grad_branch_other), select, second_output, v["low_output"],
            v["attended"], in_output, v["a0"], v["a1"], v["query"], v["key"], v["value"], v["lse"],
            cos_table, sin_table, second_query, second_key, second_value, *lows,
        )
        back_low, out_in, got_mlp, *units_sum = after([back_low, out_in, got_mlp] + units_sum)
        back_low = back_low + other_core(back_low)
        grad_low_attn = (back_low * select_three).astype(BF)
        out_sum = out_keep[0].astype(F32) + out_got[0].astype(F32) + out_in.astype(F32)
        low_down = (out_sum[:, width:] * half_of(select)).astype(BF)
        firsts = jnp.concatenate(
            [
                transpose_then_product(cols_of_core(normed_a), grad_low_attn).astype(BF),
                (
                    adapter_scale
                    * transpose_then_product(cols_of_core(cotangent), both_halves(low_down))
                ).astype(BF),
            ],
            axis=1,
        )
        *packed, chosen = pack(adapter_ids, factors, firsts)
        share = packed[0].shape[0] // n
        packed = jnp.concatenate(
            [part.reshape(n, share, part.shape[1]) for part in packed]
            + [jnp.broadcast_to(chosen[None], (n,) + chosen.shape)],
            axis=1,
        )
        units_sum = jnp.stack(units_sum)
        got_late = lax.all_to_all(packed, DP, 0, 0)
        units_parts = [units_sum] + [move(units_sum, link) for link in ("x", "y", "xy")]
        got_late, *units_parts[1:] = after([got_late] + units_parts[1:])
        late = unpack(got_late)
        back, out_sum, grad_middle, hidden_half = after(
            [back, out_sum, grad_middle, half_of(hidden_in)], late
        )

        device = jnp.stack([core, bit_y, bit_x, ring_at]).astype(jnp.int32)
        gradient_second_gate, gradient_second_up, delta_in_down = unit_results(
            device, units_parts + [other_core(part) for part in units_parts], order
        )

        layer_output = both_halves(
            (
                half_of(v["middle"])
                + out_sum[:, :width]
                + adapter_scale * matrix_product(low_down, second_down)
            ).astype(BF)
        )
        back_half = half_of(back).astype(F32) + other_core(
            take(back, (1 - core) * half_rows, half_rows)
        ).astype(F32)
        grad_normed_a = back_half + product_with_transpose(half_of(grad_low_attn), attn_in)
        grad_in = both_halves(
            (grad_middle + rms_back(hidden_half.astype(F32), attn_gain_f, grad_normed_a)).astype(BF)
        )

        sums_mlp = total(got_mlp)
        sums = jnp.concatenate(
            [late.reshape(-1, rank_cols), sums_mlp[:, :rank_cols], sums_mlp[:, rank_cols:]],
            axis=0,
        )
        sums = jnp.stack([sums] + [move(sums, f"z{r}") for r in range(1, ring_size)], axis=0)
        parts = [sums] + [move(sums, link) for link in ("x", "y", "xy")]
        parts += [other_core(part) for part in parts]
        others = other_results(
            device,
            parts,
            share,
            (second_query.shape[1], second_key.shape[1]),
        )
        return (
            layer_output,
            grad_in,
            *others[:9],
            gradient_second_gate,
            others[9],
            gradient_second_up,
            delta_in_down,
            others[10],
        )

    return body


def solution(mesh):
    n, tensor = mesh.shape["dp"], mesh.shape["tensor"]
    split = jax.sharding.Mesh(mesh.devices.reshape(n // 4, 2, 2, tensor), DP + ("tensor",))
    return jax.shard_map(
        make_body(n),
        mesh=split,
        in_specs=(
            P(DP, None), P(DP, None), P(), P(), P(DP, "tensor"), P(DP, "tensor"), P(DP, "tensor"),
            P("tensor", DP), P(DP, "tensor"), P(DP, "tensor"), P("tensor", DP), P(),
            P(None, "tensor"), P(), P(None, "tensor"), P(), P(None, "tensor"), P("tensor", None),
            P(), P(), P(None, "tensor"), P(), P(None, "tensor"), P("tensor", None), P(), P(DP, None),
        ),
        out_specs=(P(DP, None), P(DP, None)) + (P(),) * 14,
        check_vma=False,
    )
```
